128 devices in a mesh: coarse: 8 (over z, core), fine: 16 (over x, y).
Axes of the slice: x: 4, y: 4, z: 4, core: 2. Of those that a mesh axis runs over, the one named last changes fastest.
Arguments:
- fine_features: bfloat16 [2048, 512, 128], P(('coarse', 'fine')), may hold values from -6 to 6
- occupancy: int32 [2048, 512], P(('coarse', 'fine')), may hold values 0 or 1
- parent: int32 [2048], P(('coarse', 'fine')), may hold values from 0 to 65535, as said below
- timestep: int32 [1], replicated, may hold values from 0 to 999
- coarse_features: bfloat16 [8, 64, 128, 512], P('coarse', 'fine'), may hold values from -6 to 6
- time_weight: bfloat16 [256, 1280], replicated, may hold values from -0.375 to 0.375
- conv_weight: bfloat16 [27, 512, 512], replicated, may hold values from -0.0546875 to 0.0546875
- up_weight: bfloat16 [512, 128], replicated, may hold values from -0.25 to 0.25
- inner_weight: bfloat16 [128, 128], replicated, may hold values from -0.5 to 0.5
- outer_weight: bfloat16 [128, 128], replicated, may hold values from -0.5 to 0.5
- coarse_cotangent: bfloat16 [8, 64, 128, 512], P('coarse', 'fine'), may hold values from -6 to 6
- fine_cotangent: bfloat16 [2048, 512, 128], P(('coarse', 'fine')), may hold values from -1.5 to 1.5
Outputs:
- grad_coarse: bfloat16 [8, 64, 128, 512], P('coarse', 'fine')
- grad_fine: bfloat16 [2048, 512, 128], P(('coarse', 'fine'))
The draws below stay inside these ranges and needn't reach their ends.
Inputs may be any that keep to these rules, and one draw needn't show every extreme that they name: A brick in rows [g * 256, (g + 1) * 256) has its parent among the cells with z in [g, (g + 1)), flat index (z * 64 + y) * 128 + x.
All inputs are finite; a program needn't handle non-finite values. No bound on the sum of `occupancy` on one device may be relied on, other than what follows from the above.
Results may differ from the reference program's by a relative error of at most 0.0065.
Values may be sent and summed in bfloat16 or wider, within the bound.
No kernel may reach another device: no remote copies, remote signals or barrier semaphores. Data moves between devices by JAX's collectives and lax.ppermute only.
A program may use at most 128 MiB of HBM per device.

```python
import math
import jax
import jax.numpy as jnp
from jax import lax

CC = 512
CF = 128
EMB = 256
VOX = 512
NX = 128
BRICK_DEV = 16
NZ = 8
NY = 64
SLAB = 8192
NCELLS = 65536
GROUP_BRICKS = 256
BRICKS = 2048


def draw_parent(key, part):
    key = jax.random.fold_in(key, 7)
    group_index = jnp.arange(BRICKS, dtype=jnp.int32) // GROUP_BRICKS
    within = jax.random.randint(key, (BRICKS,), 0, SLAB, dtype=jnp.int32)
    parents = group_index * SLAB + within
    parents = parents.at[0].set(0).at[BRICKS - 1].set(NCELLS - 1)
    return parents.astype(jnp.int32)


def set_ends(drawn, stream_key, low, top_value):
    index_at = [jax.random.randint(jax.random.fold_in(stream_key, axis), (), 0, length) for axis, length in enumerate(drawn.shape)]
    main_axis = drawn.shape.index(max(drawn.shape))
    next_to = index_at[:main_axis] + [(index_at[main_axis] + 1) % drawn.shape[main_axis]] + index_at[main_axis + 1:]
    return drawn.at[tuple(index_at)].set(low).at[tuple(next_to)].set(top_value)


def levels(stream_key, extent, shards, smallest, largest):
    loudness, own = 1.0, jax.random.fold_in(stream_key, 6)
    for dim, parts in shards:
        draws = jnp.exp(jax.random.uniform(jax.random.fold_in(own, dim), (parts,), jnp.float32, smallest / len(shards), largest / len(shards)))
        loudness = loudness * jnp.repeat(draws, extent[dim] // parts).reshape([-1 if axis == dim else 1 for axis in range(len(extent))])
    return loudness


def noise(stream_key, shape, scale, most, split=(), kind=jnp.bfloat16):
    entries = jax.random.normal(stream_key, shape, jnp.float32) * scale
    if len(split) > 0:
        entries = levels(stream_key, shape, split, -0.22, 0.18) * entries
    return jnp.clip(entries, min=-most, max=most).astype(kind)


def setup_inputs(seed: int = 0) -> dict:
    key_list = jax.random.split(jax.random.key(seed), 13)
    return {
        "fine_features": noise(key_list[0], (BRICKS, VOX, CF), 1.0, 6.0, ((0, 128),)),
        "occupancy": set_ends((jax.random.randint(key_list[1], (BRICKS, VOX), 0, 4) < 3).astype(jnp.int32), jax.random.fold_in(key_list[1], 1), 0, 1),
        "parent": draw_parent(jax.random.fold_in(key_list[12], 71), 0),
        "timestep": jax.random.randint(key_list[3], (1,), 0, 1000).astype(jnp.int32),
        "coarse_features": noise(key_list[4], (NZ, NY, NX, CC), 1.0, 6.0, ((0, 8), (1, 16))),
        "time_weight": noise(key_list[5], (EMB, 2 * CF + 2 * CC), EMB ** -0.5, 0.375),
        "conv_weight": noise(key_list[6], (27, CC, CC), (27 * CC) ** -0.5, 0.0546875),
        "up_weight": noise(key_list[7], (CC, CF), CC ** -0.5, 0.25),
        "inner_weight": noise(key_list[8], (CF, CF), CF ** -0.5, 0.5),
        "outer_weight": noise(key_list[9], (CF, CF), CF ** -0.5, 0.5),
        "coarse_cotangent": noise(key_list[10], (NZ, NY, NX, CC), 1.0, 6.0, ((0, 8), (1, 16))),
        "fine_cotangent": noise(key_list[11], (BRICKS, VOX, CF), 0.25, 1.5, ((0, 128),)),
    }


EPSILON = 1e-06

def silu_slope(values):
    sigmoid = jax.nn.sigmoid(values)
    return sigmoid * (1.0 + values * (1.0 - sigmoid))

def rms_scale(values):
    return lax.rsqrt(lax.optimization_barrier(jnp.mean(values * values, axis=-1, keepdims=True)) + EPSILON)

def modulation(timestep, time_weight, fine_width, coarse_width):
    half_width = time_weight.shape[0] // 2
    frequency = jnp.exp(-math.log(10000.0) * jnp.arange(half_width, dtype=jnp.float32) / half_width)
    angles = timestep.astype(jnp.float32)[0] * frequency
    embedded = jnp.concatenate([jnp.sin(angles), jnp.cos(angles)]).astype(jnp.bfloat16)
    modulated = jnp.dot(embedded[None, :], time_weight, preferred_element_type=jnp.float32)[0]
    scale_fine = modulated[:fine_width]
    shift_fine = modulated[fine_width:2 * fine_width]
    scale_coarse = modulated[2 * fine_width:2 * fine_width + coarse_width]
    shift_coarse = modulated[2 * fine_width + coarse_width:]
    return (scale_fine, shift_fine, scale_coarse, shift_coarse)

def fine_block(features, occupied, parent_rows, cotangent, inner_weight, outer_weight, scale_fine, shift_fine):
    bricks, voxels, width = features.shape
    fine_in = features.astype(jnp.float32) + parent_rows[:, None, :].astype(jnp.float32)
    fine_scale = rms_scale(fine_in)
    fine_normed = fine_in * fine_scale
    fine_pre = fine_normed * (1.0 + scale_fine) + shift_fine
    fine_act = jax.nn.silu(fine_pre).astype(jnp.bfloat16)
    inner_pre = jnp.dot(fine_act.reshape(-1, width), inner_weight, preferred_element_type=jnp.float32)
    masked = cotangent * occupied[:, :, None].astype(jnp.bfloat16)
    grad_hidden = jnp.dot(masked.reshape(-1, width), outer_weight.T, preferred_element_type=jnp.float32)
    grad_inner = (grad_hidden * silu_slope(inner_pre)).astype(jnp.bfloat16)
    grad_act = jnp.dot(grad_inner, inner_weight.T, preferred_element_type=jnp.float32)
    grad_act = grad_act.reshape(bricks, voxels, width)
    grad_norm = grad_act * silu_slope(fine_pre) * (1.0 + scale_fine)
    grad_in = masked.astype(jnp.float32) + fine_scale * (grad_norm - fine_normed * lax.optimization_barrier(jnp.mean(grad_norm * fine_normed, axis=-1, keepdims=True)))
    return (grad_in.astype(jnp.bfloat16), lax.optimization_barrier(jnp.sum(grad_in, axis=1)))

def corner_list():
    return [(layer_step, row_step, column_step) for layer_step in range(3) for row_step in range(3) for column_step in range(3)]

def reference(fine_features, occupancy, parent, timestep, coarse_features, time_weight, conv_weight, up_weight, inner_weight, outer_weight, coarse_cotangent, fine_cotangent):
    coarse_width, fine_width = up_weight.shape
    scale_fine, shift_fine, scale_coarse, shift_coarse = modulation(timestep, time_weight, fine_width, coarse_width)
    coarse_in = coarse_features.astype(jnp.float32)
    coarse_scale = rms_scale(coarse_in)
    coarse_normed = coarse_in * coarse_scale
    coarse_pre = coarse_normed * (1.0 + scale_coarse) + shift_coarse
    coarse_hidden = jax.nn.silu(coarse_pre).astype(jnp.bfloat16)
    padded = jnp.pad(coarse_hidden, ((1, 1), (1, 1), (1, 1), (0, 0)))
    conv_out = jnp.zeros((NZ * NY * NX, coarse_width), jnp.float32)
    for index, (layer_step, row_step, column_step) in enumerate(corner_list()):
        shifted = padded[layer_step:layer_step + NZ, row_step:row_step + NY, column_step:column_step + NX]
        conv_out = conv_out + jnp.dot(shifted.reshape(-1, coarse_width), conv_weight[index], preferred_element_type=jnp.float32)
    coarse_out = (coarse_in + conv_out.reshape(coarse_in.shape)).astype(jnp.bfloat16)
    lifted = jnp.dot(coarse_out.reshape(-1, coarse_width), up_weight, preferred_element_type=jnp.float32).astype(jnp.bfloat16)
    parent_rows = jnp.take(lifted, parent, axis=0)
    block_count = fine_features.shape[0] // BRICK_DEV

    def per_block(block_items):
        return fine_block(block_items[0], block_items[1], block_items[2], block_items[3], inner_weight, outer_weight, scale_fine, shift_fine)
    grads, sums = lax.map(per_block, (fine_features.reshape(block_count, BRICK_DEV, VOX, fine_width), occupancy.reshape(block_count, BRICK_DEV, VOX), parent_rows.reshape(block_count, BRICK_DEV, fine_width), fine_cotangent.reshape(block_count, BRICK_DEV, VOX, fine_width)))
    grad_fine = grads.reshape(fine_features.shape)
    brick_sums = sums.reshape(-1, fine_width)
    cell_sums = jax.ops.segment_sum(brick_sums, parent, num_segments=NCELLS).astype(jnp.bfloat16)
    grad_out = coarse_cotangent.astype(jnp.float32) + jnp.dot(cell_sums, up_weight.T, preferred_element_type=jnp.float32).reshape(coarse_in.shape)
    grad_padded = jnp.pad(grad_out.astype(jnp.bfloat16), ((1, 1), (1, 1), (1, 1), (0, 0)))
    grad_conv = jnp.zeros((NZ * NY * NX, coarse_width), jnp.float32)
    for index, (layer_step, row_step, column_step) in enumerate(corner_list()):
        shifted = grad_padded[layer_step:layer_step + NZ, row_step:row_step + NY, column_step:column_step + NX]
        grad_conv = grad_conv + jnp.dot(shifted.reshape(-1, coarse_width), conv_weight[26 - index].T, preferred_element_type=jnp.float32)
    grad_conv = grad_conv.reshape(coarse_in.shape)
    grad_cn = grad_conv * silu_slope(coarse_pre) * (1.0 + scale_coarse)
    grad_coarse = grad_out + coarse_scale * (grad_cn - coarse_normed * lax.optimization_barrier(jnp.mean(grad_cn * coarse_normed, axis=-1, keepdims=True)))
    return (grad_coarse.astype(jnp.bfloat16), grad_fine)
```

```python
import math

import jax
import jax.numpy as jnp
from jax import lax
from jax.experimental import pallas as pl
from jax.experimental.pallas import tpu as pltpu
from jax.sharding import PartitionSpec as P

EPSILON = 1e-06
MIB = 1024 * 1024
F32 = jnp.float32
BF16 = jnp.bfloat16
CHUNK = 64


def sigmoid(values):
    return 0.5 * jnp.tanh(0.5 * values) + 0.5


def silu_slope(values):
    gate = sigmoid(values)
    return gate * (1.0 + values * (1.0 - gate))


def rms_scale(values):
    return lax.rsqrt(jnp.mean(values * values, axis=-1, keepdims=True) + EPSILON)


def modulation(timestep, time_weight):
    half_width = time_weight.shape[0] // 2
    frequency = jnp.exp(-math.log(10000.0) * jnp.arange(half_width, dtype=F32) / half_width)
    angles = timestep.astype(F32)[0] * frequency
    embedded = jnp.concatenate([jnp.sin(angles), jnp.cos(angles)]).astype(BF16)
    return jnp.dot(embedded[None, :], time_weight, preferred_element_type=F32)


def shift_pairs(size):
    up = [(i, i + 1) for i in range(size - 1)]
    return up, [(j, i) for i, j in up]


def parent_conv_kernel(
    place, own, below, above, mod, info, conv_weight, up_weight, out, hidden, weights, sems
):
    cells, width = own.shape
    bricks = info.shape[0]
    taps = conv_weight.shape[0]

    def load(tap):
        return pltpu.make_async_copy(conv_weight.at[tap], weights.at[tap], sems.at[tap])

    for tap in range(taps):
        load(tap).start()
    scale = 1.0 + mod[0:1, 256:768]
    shift = mod[0:1, 768:1280]
    for layer, source in ((1, own), (0, below), (2, above)):
        values = source[...].astype(F32)
        pre = values * rms_scale(values) * scale + shift
        act = pre * sigmoid(pre)
        if layer != 1:
            act = jnp.where(place[1 + layer // 2] > 0, act, 0.0)
        hidden[layer] = act.astype(BF16)

    first_row = place[0]
    spots = info[...]
    spots_t = spots.astype(F32).T
    row_t = spots_t[0:1, :].astype(jnp.int32) - first_row
    near_t = jnp.where((row_t >= -1) & (row_t <= 4), 1.0, 0.0)
    row_c = spots[:, 0:1].astype(F32).astype(jnp.int32) - first_row
    near_c = jnp.where((row_c >= -1) & (row_c <= 4), 1.0, 0.0)
    brick_i = lax.broadcasted_iota(jnp.int32, (bricks, bricks), 0)
    brick_j = lax.broadcasted_iota(jnp.int32, (bricks, bricks), 1)
    place_t = jnp.dot(
        jnp.broadcast_to(near_t, (16, bricks)).astype(BF16),
        jnp.where(brick_i < brick_j, 1.0, 0.0).astype(BF16),
        preferred_element_type=F32,
    )[0:1].astype(jnp.int32)
    place_c = jnp.dot(
        jnp.where(brick_j < brick_i, 1.0, 0.0).astype(BF16),
        jnp.broadcast_to(near_c, (bricks, 128)).astype(BF16),
        preferred_element_type=F32,
    )[:, 0:CHUNK].astype(jnp.int32)
    near_count = jnp.sum(near_t).astype(jnp.int32)

    def one_chunk(chunk, first):
        begin = chunk * CHUNK
        slot = lax.broadcasted_iota(jnp.int32, (CHUNK, bricks), 0) + begin
        pick = jnp.where((slot == place_t) & (near_t > 0), 1.0, 0.0).astype(BF16)
        found = jnp.dot(pick, spots, preferred_element_type=F32)
        row = found[:, 0:1].astype(jnp.int32) - first_row
        column = found[:, 64:65].astype(jnp.int32)
        lane = lax.broadcasted_iota(jnp.int32, (CHUNK, cells), 1)
        onehots = []
        for row_step in (-1, 0, 1):
            for column_step in (-1, 0, 1):
                y, x = row + row_step, column + column_step
                inside = (y >= 0) & (y < 4) & (x >= 0) & (x < 128)
                cell = jnp.where(inside, y * 128 + x, -1)
                onehots.append(jnp.where(lane == cell, 1.0, 0.0).astype(BF16))
        onehot = jnp.concatenate(onehots, axis=0)
        total = jnp.dot(onehots[4], own[...], preferred_element_type=F32)
        for layer in range(3):
            gathered = jnp.dot(onehot, hidden[layer], preferred_element_type=F32).astype(BF16)
            for corner in range(9):
                tap = 9 * layer + corner
                if first:
                    load(tap).wait()
                total += jnp.dot(
                    gathered[corner * CHUNK : (corner + 1) * CHUNK],
                    weights[tap],
                    preferred_element_type=F32,
                )
        lifted = jnp.dot(total.astype(BF16), up_weight[...], preferred_element_type=F32)
        high = lifted.astype(BF16)
        low = (lifted - high.astype(F32)).astype(BF16)
        slot_c = lax.broadcasted_iota(jnp.int32, (bricks, CHUNK), 1) + begin
        spread = jnp.where((slot_c == place_c) & (near_c > 0), 1.0, 0.0).astype(BF16)
        return jnp.dot(spread, high, preferred_element_type=F32) + jnp.dot(
            spread, low, preferred_element_type=F32
        )

    out[...] = one_chunk(0, True)

    @pl.loop(1, (near_count + CHUNK - 1) // CHUNK)
    def _(chunk):
        out[...] += one_chunk(chunk, False)


def parent_conv(place, own, below, above, mod, info, conv_weight, up_weight):
    cells, width = own.shape
    taps = conv_weight.shape[0]
    vmem = pl.BlockSpec(memory_space=pltpu.VMEM)
    return pl.pallas_call(
        parent_conv_kernel,
        out_shape=jax.ShapeDtypeStruct((info.shape[0], up_weight.shape[1]), F32),
        in_specs=[pl.BlockSpec(memory_space=pltpu.SMEM)] + [vmem] * 5 + [pl.BlockSpec(memory_space=pl.ANY), vmem],
        out_specs=vmem,
        scratch_shapes=[
            pltpu.VMEM((3, cells, width), BF16),
            pltpu.VMEM((taps, width, width), BF16),
            pltpu.SemaphoreType.DMA((taps,)),
        ],
        compiler_params=pltpu.CompilerParams(vmem_limit_bytes=40 * MIB),
        cost_estimate=pl.CostEstimate(flops=2 * 128 * 27 * 512 * 512, bytes_accessed=16 * MIB, transcendentals=0),
        name="parent_conv",
    )(place, own, below, above, mod, info, conv_weight, up_weight)


def fine_kernel(features, masked_in, parts, mod, inner_weight, outer_weight, grads, sums):
    step = pl.program_id(0)
    scale = 1.0 + mod[0:1, 0:128]
    shift = mod[0:1, 128:256]
    for item in range(features.shape[0]):
        brick = step * features.shape[0] + item
        lifted = jnp.sum(parts[:, pl.ds(brick, 1), :], axis=0).astype(BF16).astype(F32)
        fine_in = features[item].astype(F32) + lifted
        fine_scale = rms_scale(fine_in)
        normed = fine_in * fine_scale
        pre = normed * scale + shift
        gate = sigmoid(pre)
        act = pre * gate
        slope = gate + act * (1.0 - gate)
        inner_pre = jnp.dot(act.astype(BF16), inner_weight[...], preferred_element_type=F32)
        masked = masked_in[item]
        grad_hidden = lax.dot_general(
            masked, outer_weight[...], (((1,), (1,)), ((), ())), preferred_element_type=F32
        )
        grad_inner = (grad_hidden * silu_slope(inner_pre)).astype(BF16)
        grad_act = lax.dot_general(
            grad_inner, inner_weight[...], (((1,), (1,)), ((), ())), preferred_element_type=F32
        )
        grad_norm = grad_act * slope * scale
        inner = jnp.mean(grad_norm * normed, axis=-1, keepdims=True)
        grad_in = masked.astype(F32) + fine_scale * (grad_norm - normed * inner)
        grads[item] = grad_in.astype(BF16)
        sums[pl.ds(brick, 1), :] = jnp.sum(grad_in, axis=0, keepdims=True)


def fine_block(features, masked, parts, mod, inner_weight, outer_weight):
    bricks, voxels, width = features.shape
    per_step = 2
    block = pl.BlockSpec((per_step, voxels, width), lambda i: (i, 0, 0))

    def whole(array):
        return pl.BlockSpec(array.shape, lambda i: (0,) * array.ndim)

    return pl.pallas_call(
        fine_kernel,
        grid=(bricks // per_step,),
        out_shape=(
            jax.ShapeDtypeStruct(features.shape, BF16),
            jax.ShapeDtypeStruct((bricks, width), F32),
        ),
        in_specs=[block, block, whole(parts), whole(mod), whole(inner_weight), whole(outer_weight)],
        out_specs=(block, pl.BlockSpec((bricks, width), lambda i: (0, 0))),
        compiler_params=pltpu.CompilerParams(vmem_limit_bytes=32 * MIB),
        cost_estimate=pl.CostEstimate(flops=10**9, bytes_accessed=6 * MIB, transcendentals=2**21),
        name="fine_block",
    )(features, masked, parts, mod, inner_weight, outer_weight)


def coarse_grad_kernel(
    place, features, own, below, above, row_before, row_after, mod, packs, conv_weight, up_weight,
    out, grad, center, total, weights, sems,
):
    cells, width = own.shape
    taps = conv_weight.shape[0]

    def load(part):
        return pltpu.make_async_copy(
            conv_weight.at[pl.ds(3 * part, 3)], weights.at[part], sems.at[part]
        )

    for part in range(taps // 3):
        load(part).start()
    first_row = place[0]
    halo_cells = 6 * 128
    for layer, source in ((1, own), (0, below), (2, above)):
        sums = packs[:, layer, 0:16, :].reshape(256, 128)
        spots_t = packs[:, layer, 16:32, :].reshape(256, 128).astype(F32).T
        row = spots_t[0:1, :].astype(jnp.int32) - first_row + 1
        column = spots_t[64:65, :].astype(jnp.int32)
        cell = row * 128 + column
        onehot = jnp.where(
            lax.broadcasted_iota(jnp.int32, (halo_cells, 256), 0) == cell, 1.0, 0.0
        ).astype(BF16)
        cell_sums = jnp.dot(onehot, sums, preferred_element_type=F32).astype(BF16)
        lift = lax.dot_general(
            cell_sums, up_weight[...], (((1,), (1,)), ((), ())), preferred_element_type=F32
        )
        middle = lift[128:640] + source[...].astype(F32)
        if layer == 1:
            center[...] = middle
        grad[layer, 0:128] = (lift[0:128] + row_before[layer].astype(F32)).astype(BF16)
        grad[layer, 128:640] = middle.astype(BF16)
        grad[layer, 640:768] = (lift[640:768] + row_after[layer].astype(F32)).astype(BF16)

    for layer_step in range(3):
        for row_step in range(3):
            part = 3 * layer_step + row_step
            load(part).wait()
            begin = (2 - row_step) * 128
            block = grad[2 - layer_step, begin : begin + cells]
            for column_step in range(3):
                piece = lax.dot_general(
                    block,
                    weights[part, column_step],
                    (((1,), (1,)), ((), ())),
                    preferred_element_type=F32,
                )
                if part == 0:
                    total[column_step] = piece
                else:
                    total[column_step] += piece
    column = lax.broadcasted_iota(jnp.int32, (cells, 1), 0) % 128
    left = jnp.where(column == 127, 0.0, pltpu.roll(total[0], cells - 1, 0))
    right = jnp.where(column == 0, 0.0, pltpu.roll(total[2], 1, 0))
    grad_conv = total[1] + left + right
    scale = 1.0 + mod[0:1, 256:768]
    shift = mod[0:1, 768:1280]
    values = features[...].astype(F32)
    coarse_scale = rms_scale(values)
    normed = values * coarse_scale
    grad_cn = grad_conv * silu_slope(normed * scale + shift) * scale
    inner = jnp.mean(grad_cn * normed, axis=-1, keepdims=True)
    out[...] = (center[...] + coarse_scale * (grad_cn - normed * inner)).astype(BF16)


def coarse_grad(place, features, own, below, above, row_before, row_after, mod, packs, conv_weight, up_weight):
    cells, width = own.shape
    taps = conv_weight.shape[0]
    vmem = pl.BlockSpec(memory_space=pltpu.VMEM)
    return pl.pallas_call(
        coarse_grad_kernel,
        out_shape=jax.ShapeDtypeStruct((cells, width), BF16),
        in_specs=[pl.BlockSpec(memory_space=pltpu.SMEM)] + [vmem] * 8 + [pl.BlockSpec(memory_space=pl.ANY), vmem],
        out_specs=vmem,
        scratch_shapes=[
            pltpu.VMEM((3, 6 * 128, width), BF16),
            pltpu.VMEM((cells, width), F32),
            pltpu.VMEM((3, cells, width), F32),
            pltpu.VMEM((taps // 3, 3, width, width), BF16),
            pltpu.SemaphoreType.DMA((taps // 3,)),
        ],
        compiler_params=pltpu.CompilerParams(vmem_limit_bytes=48 * MIB),
        cost_estimate=pl.CostEstimate(flops=2 * 512 * 27 * 512 * 512, bytes_accessed=18 * MIB, transcendentals=0),
        name="coarse_grad",
    )(place, features, own, below, above, row_before, row_after, mod, packs, conv_weight, up_weight)


def per_device(
    fine_features,
    occupancy,
    parent,
    timestep,
    coarse_features,
    time_weight,
    conv_weight,
    up_weight,
    inner_weight,
    outer_weight,
    coarse_cotangent,
    fine_cotangent,
):
    layer_count, row_count, column_count, width = coarse_features.shape
    fine_width = up_weight.shape[1]
    bricks = parent.shape[0]
    fine_size, coarse_size = lax.axis_size("fine"), lax.axis_size("coarse")
    coarse_index, fine_index = lax.axis_index("coarse"), lax.axis_index("fine")
    cells = layer_count * row_count * column_count
    up, down = shift_pairs(coarse_size)
    row_up, row_down = shift_pairs(fine_size)

    local = parent - coarse_index * (cells * fine_size)
    row, column = local // column_count, local % column_count
    lane = jnp.arange(128)[None, :]
    spots = jnp.where(lane < 64, row[:, None], column[:, None]).astype(BF16)
    place = jnp.stack(
        [fine_index * row_count, (coarse_index > 0).astype(jnp.int32), (coarse_index < coarse_size - 1).astype(jnp.int32)]
    ).astype(jnp.int32)

    features = coarse_features.reshape(cells, width)
    cotangent = coarse_cotangent.reshape(cells, width)
    features_below = lax.ppermute(features, "coarse", up)
    features_above = lax.ppermute(features, "coarse", down)
    all_spots = lax.all_to_all(
        jnp.broadcast_to(spots[None], (fine_size, bricks, 128)), "fine", 0, 0, tiled=True
    ).reshape(fine_size * bricks, 128)
    cot_below = lax.ppermute(cotangent, "coarse", up)
    cot_above = lax.ppermute(cotangent, "coarse", down)
    mod = modulation(timestep, time_weight)
    masked = fine_cotangent * occupancy[:, :, None].astype(BF16)

    partial_rows = parent_conv(
        place, features, features_below, features_above, mod, all_spots, conv_weight, up_weight
    )
    parts = lax.all_to_all(
        partial_rows.reshape(fine_size, bricks, fine_width), "fine", 0, 0, tiled=True
    )
    three = jnp.stack([cot_below, cotangent, cot_above])
    row_before = lax.ppermute(three[:, cells - column_count :], "fine", row_up)
    row_after = lax.ppermute(three[:, :column_count], "fine", row_down)

    grad_fine, sums = fine_block(fine_features, masked, parts, mod, inner_weight, outer_weight)
    pack = jnp.concatenate([sums.astype(BF16), spots])
    pack_below = lax.ppermute(pack, "coarse", up)
    pack_above = lax.ppermute(pack, "coarse", down)
    packs = jnp.stack([pack_below, pack, pack_above])
    packs = lax.all_to_all(
        jnp.broadcast_to(packs[None], (fine_size,) + packs.shape), "fine", 0, 0, tiled=True
    )
    grad_coarse = coarse_grad(
        place, features, cotangent, cot_below, cot_above, row_before, row_after, mod, packs, conv_weight, up_weight
    )
    return (grad_coarse.reshape(coarse_features.shape), grad_fine)


def solution(mesh):
    in_specs = (
        P(("coarse", "fine"), None, None),
        P(("coarse", "fine"), None),
        P(("coarse", "fine")),
        P(),
        P("coarse", "fine", None, None),
        P(),
        P(),
        P(),
        P(),
        P(),
        P("coarse", "fine", None, None),
        P(("coarse", "fine"), None, None),
    )
    out_specs = (P("coarse", "fine", None, None), P(("coarse", "fine"), None, None))
    return jax.shard_map(
        per_device, mesh=mesh, in_specs=in_specs, out_specs=out_specs, check_vma=False
    )
```

```python
import math

import jax
import jax.numpy as jnp
from jax import lax
from jax.experimental import pallas as pl
from jax.experimental.pallas import tpu as pltpu
from jax.sharding import PartitionSpec as P

EPSILON = 1e-06
MIB = 1024 * 1024
F32 = jnp.float32
BF16 = jnp.bfloat16
CHUNK = 64


def sigmoid(values):
    return 0.5 * jnp.tanh(0.5 * values) + 0.5


def silu_slope(values):
    gate = sigmoid(values)
    return gate * (1.0 + values * (1.0 - gate))


def rms_scale(values):
    return lax.rsqrt(jnp.mean(values * values, axis=-1, keepdims=True) + EPSILON)


def modulation(timestep, time_weight):
    half_width = time_weight.shape[0] // 2
    frequency = jnp.exp(-math.log(10000.0) * jnp.arange(half_width, dtype=F32) / half_width)
    angles = timestep.astype(F32)[0] * frequency
    embedded = jnp.concatenate([jnp.sin(angles), jnp.cos(angles)]).astype(BF16)
    return jnp.dot(embedded[None, :], time_weight, preferred_element_type=F32)


def shift_pairs(size):
    up = [(i, i + 1) for i in range(size - 1)]
    return up, [(j, i) for i, j in up]


def prepare_kernel(place, own, below, above, mod, conv_weight, hidden, weights, sems):
    taps = conv_weight.shape[0]
    parts = sems.shape[0]
    size = taps // parts
    copies = [
        pltpu.make_async_copy(
            conv_weight.at[pl.ds(size * part, size)], weights.at[pl.ds(size * part, size)], sems.at[part]
        )
        for part in range(parts)
    ]
    for copy in copies:
        copy.start()
    scale = 1.0 + mod[0:1, 256:768]
    shift = mod[0:1, 768:1280]
    for layer, source in ((1, own), (0, below), (2, above)):
        values = source[...].astype(F32)
        pre = values * rms_scale(values) * scale + shift
        act = pre * sigmoid(pre)
        if layer != 1:
            act = jnp.where(place[1 + layer // 2] > 0, act, 0.0)
        hidden[layer] = act.astype(BF16)
    for copy in copies:
        copy.wait()


def prepare(place, own, below, above, mod, conv_weight):
    vmem = pl.BlockSpec(memory_space=pltpu.VMEM)
    return pl.pallas_call(
        prepare_kernel,
        out_shape=(
            jax.ShapeDtypeStruct((3,) + own.shape, BF16),
            jax.ShapeDtypeStruct(conv_weight.shape, BF16),
        ),
        in_specs=[pl.BlockSpec(memory_space=pltpu.SMEM)] + [vmem] * 4 + [pl.BlockSpec(memory_space=pl.ANY)],
        out_specs=(vmem, vmem),
        scratch_shapes=[pltpu.SemaphoreType.DMA((9,))],
        compiler_params=pltpu.CompilerParams(vmem_limit_bytes=28 * MIB),
        cost_estimate=pl.CostEstimate(flops=2**24, bytes_accessed=16 * MIB, transcendentals=2**20),
        name="prepare",
    )(place, own, below, above, mod, conv_weight)


def near_slots(spots, first_row):
    bricks = spots.shape[0]
    spots_t = spots.astype(F32).T
    row_t = spots_t[0:1, :].astype(jnp.int32) - first_row
    near_t = (row_t >= -1) & (row_t <= 4)
    brick_i = lax.broadcasted_iota(jnp.int32, (bricks, bricks), 0)
    brick_j = lax.broadcasted_iota(jnp.int32, (bricks, bricks), 1)
    place_t = jnp.dot(
        jnp.broadcast_to(jnp.where(near_t, 1.0, 0.0), (16, bricks)).astype(BF16),
        jnp.where(brick_i < brick_j, 1.0, 0.0).astype(BF16),
        preferred_element_type=F32,
    )[0:1].astype(jnp.int32)
    count = jnp.sum(jnp.where(near_t, 1.0, 0.0)).astype(jnp.int32)
    return jnp.where(near_t, place_t, -1), count


def tap_cells(pick, spots, first_row, cells):
    found = jnp.dot(pick, spots, preferred_element_type=F32)
    row = found[:, 0:1].astype(jnp.int32) - first_row
    column = found[:, 64:65].astype(jnp.int32)
    lane = lax.broadcasted_iota(jnp.int32, (pick.shape[0], cells), 1)
    onehots = []
    for row_step in (-1, 0, 1):
        for column_step in (-1, 0, 1):
            y, x = row + row_step, column + column_step
            inside = (y >= 0) & (y < 4) & (x >= 0) & (x < 128)
            cell = jnp.where(inside, y * 128 + x, -1)
            onehots.append(jnp.where(lane == cell, 1.0, 0.0).astype(BF16))
    return onehots


def parent_conv_kernel(place, own, hidden, info, weights, up_weight, out):
    cells, width = own.shape
    bricks = info.shape[0]
    first_row = place[0]
    spots = info[...]
    slots, near_count = near_slots(spots, first_row)

    def one_chunk(chunk):
        slot = lax.broadcasted_iota(jnp.int32, (CHUNK, bricks), 0) + chunk * CHUNK
        pick = jnp.where(slot == slots, 1.0, 0.0).astype(BF16)
        onehots = tap_cells(pick, spots, first_row, cells)
        onehot = jnp.concatenate(onehots, axis=0)
        total = jnp.dot(onehots[4], own[...], preferred_element_type=F32)
        for layer in range(3):
            gathered = jnp.dot(onehot, hidden[layer], preferred_element_type=F32).astype(BF16)
            for corner in range(9):
                total += jnp.dot(
                    gathered[corner * CHUNK : (corner + 1) * CHUNK],
                    weights[9 * layer + corner],
                    preferred_element_type=F32,
                )
        lifted = jnp.dot(total.astype(BF16), up_weight[...], preferred_element_type=F32)
        high = lifted.astype(BF16)
        low = (lifted - high.astype(F32)).astype(BF16)
        across = (((0,), (0,)), ((), ()))
        return lax.dot_general(pick, high, across, preferred_element_type=F32) + lax.dot_general(
            pick, low, across, preferred_element_type=F32
        )

    out[...] = one_chunk(0)

    @pl.loop(1, (near_count + CHUNK - 1) // CHUNK)
    def _(chunk):
        out[...] += one_chunk(chunk)


def parent_conv(place, own, hidden, info, weights, up_weight):
    vmem = pl.BlockSpec(memory_space=pltpu.VMEM)
    return pl.pallas_call(
        parent_conv_kernel,
        out_shape=jax.ShapeDtypeStruct((info.shape[0], up_weight.shape[1]), F32),
        in_specs=[pl.BlockSpec(memory_space=pltpu.SMEM)] + [vmem] * 5,
        out_specs=vmem,
        compiler_params=pltpu.CompilerParams(vmem_limit_bytes=16 * MIB),
        cost_estimate=pl.CostEstimate(flops=2 * 128 * 27 * 512 * 512, bytes_accessed=16 * MIB, transcendentals=0),
        name="parent_conv",
    )(place, own, hidden, info, weights, up_weight)


def fine_kernel(features, cotangent, occupied, parts, mod, inner_weight, outer_weight, grads, sums, spread):
    step = pl.program_id(0)

    @pl.when(step == 0)
    def _():
        spread[...] = occupied[...].astype(F32).T.astype(BF16)

    scale = 1.0 + mod[0:1, 0:128]
    shift = mod[0:1, 128:256]
    bricks = occupied.shape[0]
    for item in range(features.shape[0]):
        brick = step * features.shape[0] + item
        mask = jnp.dot(
            spread[...],
            jnp.where(lax.broadcasted_iota(jnp.int32, (bricks, 128), 0) == brick, 1.0, 0.0).astype(BF16),
            preferred_element_type=F32,
        )
        lifted = jnp.sum(parts[:, pl.ds(brick, 1), :], axis=0).astype(BF16).astype(F32)
        fine_in = features[item].astype(F32) + lifted
        fine_scale = rms_scale(fine_in)
        normed = fine_in * fine_scale
        pre = normed * scale + shift
        gate = sigmoid(pre)
        act = pre * gate
        slope = gate + act * (1.0 - gate)
        inner_pre = jnp.dot(act.astype(BF16), inner_weight[...], preferred_element_type=F32)
        masked = cotangent[item].astype(F32) * mask
        grad_hidden = lax.dot_general(
            masked.astype(BF16), outer_weight[...], (((1,), (1,)), ((), ())), preferred_element_type=F32
        )
        grad_inner = (grad_hidden * silu_slope(inner_pre)).astype(BF16)
        grad_act = lax.dot_general(
            grad_inner, inner_weight[...], (((1,), (1,)), ((), ())), preferred_element_type=F32
        )
        grad_norm = grad_act * slope * scale
        inner = jnp.mean(grad_norm * normed, axis=-1, keepdims=True)
        grad_in = masked + fine_scale * (grad_norm - normed * inner)
        grads[item] = grad_in.astype(BF16)
        sums[pl.ds(brick, 1), :] = jnp.sum(grad_in, axis=0, keepdims=True)


def fine_block(features, cotangent, occupied, parts, mod, inner_weight, outer_weight):
    bricks, voxels, width = features.shape
    per_step = 2
    block = pl.BlockSpec((per_step, voxels, width), lambda i: (i, 0, 0))

    def whole(array):
        return pl.BlockSpec(array.shape, lambda i: (0,) * array.ndim)

    return pl.pallas_call(
        fine_kernel,
        grid=(bricks // per_step,),
        out_shape=(
            jax.ShapeDtypeStruct(features.shape, BF16),
            jax.ShapeDtypeStruct((bricks, width), F32),
        ),
        in_specs=[block, block, whole(occupied), whole(parts), whole(mod), whole(inner_weight), whole(outer_weight)],
        out_specs=(block, pl.BlockSpec((bricks, width), lambda i: (0, 0))),
        scratch_shapes=[pltpu.VMEM((voxels, bricks), BF16)],
        compiler_params=pltpu.CompilerParams(vmem_limit_bytes=20 * MIB),
        cost_estimate=pl.CostEstimate(flops=10**9, bytes_accessed=6 * MIB, transcendentals=2**21),
        name="fine_block",
    )(features, cotangent, occupied, parts, mod, inner_weight, outer_weight)


def cotangent_conv_kernel(own, below, above, row_before, row_after, weights, out, grad, total):
    cells, width = own.shape
    for layer, source in ((1, own), (0, below), (2, above)):
        grad[layer, 0:128] = row_before[layer]
        grad[layer, 128:640] = source[...]
        grad[layer, 640:768] = row_after[layer]
    for layer_step in range(3):
        for row_step in range(3):
            part = 3 * layer_step + row_step
            begin = (2 - row_step) * 128
            block = grad[2 - layer_step, begin : begin + cells]
            for column_step in range(3):
                piece = lax.dot_general(
                    block,
                    weights[3 * part + column_step],
                    (((1,), (1,)), ((), ())),
                    preferred_element_type=F32,
                )
                if part == 0:
                    total[column_step] = piece
                else:
                    total[column_step] += piece
    column = lax.broadcasted_iota(jnp.int32, (cells, 1), 0) % 128
    left = jnp.where(column == 127, 0.0, pltpu.roll(total[0], cells - 1, 0))
    right = jnp.where(column == 0, 0.0, pltpu.roll(total[2], 1, 0))
    out[...] = total[1] + left + right


def cotangent_conv(own, below, above, row_before, row_after, weights):
    cells, width = own.shape
    vmem = pl.BlockSpec(memory_space=pltpu.VMEM)
    return pl.pallas_call(
        cotangent_conv_kernel,
        out_shape=jax.ShapeDtypeStruct((cells, width), F32),
        in_specs=[vmem] * 6,
        out_specs=vmem,
        scratch_shapes=[
            pltpu.VMEM((3, 6 * 128, width), BF16),
            pltpu.VMEM((3, cells, width), F32),
        ],
        compiler_params=pltpu.CompilerParams(vmem_limit_bytes=24 * MIB),
        cost_estimate=pl.CostEstimate(flops=2 * 512 * 27 * 512 * 512, bytes_accessed=18 * MIB, transcendentals=0),
        name="cotangent_conv",
    )(own, below, above, row_before, row_after, weights)


def coarse_grad_kernel(
    place, features, own, conv, mod, packs, packs_below, packs_above, weights, up_weight, out, total, center
):
    cells, width = own.shape
    first_row = place[0]
    across = (((0,), (0,)), ((), ()))
    total[...] = conv[...]
    center[...] = own[...].astype(F32)
    for layer, pack in ((1, packs), (0, packs_below), (2, packs_above)):
        sums = pack[:, 0:16, :].reshape(256, 128)
        spots = pack[:, 16:32, :].reshape(256, 128)
        slots, near_count = near_slots(spots, first_row)

        def one_chunk(chunk, layer=layer, sums=sums, spots=spots, slots=slots):
            slot = lax.broadcasted_iota(jnp.int32, (CHUNK, 256), 0) + chunk * CHUNK
            pick = jnp.where(slot == slots, 1.0, 0.0).astype(BF16)
            onehots = tap_cells(pick, spots, first_row, cells)
            rows = jnp.dot(pick, sums, preferred_element_type=F32).astype(BF16)
            lift = lax.dot_general(
                rows, up_weight[...], (((1,), (1,)), ((), ())), preferred_element_type=F32
            )
            high = lift.astype(BF16)
            if layer == 1:
                low = (lift - high.astype(F32)).astype(BF16)
                center[...] += lax.dot_general(
                    jnp.concatenate([onehots[4], onehots[4]], axis=0),
                    jnp.concatenate([high, low], axis=0),
                    across,
                    preferred_element_type=F32,
                )
            spread = [
                lax.dot_general(
                    high,
                    weights[9 * (2 - layer) + corner],
                    (((1,), (1,)), ((), ())),
                    preferred_element_type=F32,
                ).astype(BF16)
                for corner in range(9)
            ]
            total[...] += lax.dot_general(
                jnp.concatenate(onehots, axis=0),
                jnp.concatenate(spread, axis=0),
                across,
                preferred_element_type=F32,
            )

        one_chunk(0)
        pl.loop(1, (near_count + CHUNK - 1) // CHUNK)(one_chunk)

    scale = 1.0 + mod[0:1, 256:768]
    shift = mod[0:1, 768:1280]
    values = features[...].astype(F32)
    coarse_scale = rms_scale(values)
    normed = values * coarse_scale
    grad_cn = total[...] * silu_slope(normed * scale + shift) * scale
    inner = jnp.mean(grad_cn * normed, axis=-1, keepdims=True)
    out[...] = (center[...] + coarse_scale * (grad_cn - normed * inner)).astype(BF16)


def coarse_grad(place, features, own, conv, mod, packs, packs_below, packs_above, weights, up_weight):
    cells, width = own.shape
    vmem = pl.BlockSpec(memory_space=pltpu.VMEM)
    return pl.pallas_call(
        coarse_grad_kernel,
        out_shape=jax.ShapeDtypeStruct((cells, width), BF16),
        in_specs=[pl.BlockSpec(memory_space=pltpu.SMEM)] + [vmem] * 9,
        out_specs=vmem,
        scratch_shapes=[pltpu.VMEM((cells, width), F32), pltpu.VMEM((cells, width), F32)],
        compiler_params=pltpu.CompilerParams(vmem_limit_bytes=20 * MIB),
        cost_estimate=pl.CostEstimate(flops=2 * 256 * 27 * 512 * 512, bytes_accessed=18 * MIB, transcendentals=0),
        name="coarse_grad",
    )(place, features, own, conv, mod, packs, packs_below, packs_above, weights, up_weight)


def per_device(
    fine_features,
    occupancy,
    parent,
    timestep,
    coarse_features,
    time_weight,
    conv_weight,
    up_weight,
    inner_weight,
    outer_weight,
    coarse_cotangent,
    fine_cotangent,
):
    layer_count, row_count, column_count, width = coarse_features.shape
    fine_width = up_weight.shape[1]
    bricks = parent.shape[0]
    fine_size, coarse_size = lax.axis_size("fine"), lax.axis_size("coarse")
    coarse_index, fine_index = lax.axis_index("coarse"), lax.axis_index("fine")
    cells = layer_count * row_count * column_count
    up, down = shift_pairs(coarse_size)
    row_up, row_down = shift_pairs(fine_size)

    local = parent - coarse_index * (cells * fine_size)
    row, column = local // column_count, local % column_count
    lane = jnp.arange(128)[None, :]
    spots = jnp.where(lane < 64, row[:, None], column[:, None]).astype(BF16)
    place = jnp.stack(
        [fine_index * row_count, (coarse_index > 0).astype(jnp.int32), (coarse_index < coarse_size - 1).astype(jnp.int32)]
    ).astype(jnp.int32)

    features = coarse_features.reshape(cells, width)
    cotangent = coarse_cotangent.reshape(cells, width)
    features_below = lax.ppermute(features, "coarse", up)
    features_above = lax.ppermute(features, "coarse", down)
    all_spots = lax.all_to_all(
        jnp.broadcast_to(spots[None], (fine_size, bricks, 128)), "fine", 0, 0, tiled=True
    ).reshape(fine_size * bricks, 128)
    cot_below = lax.ppermute(cotangent, "coarse", up)
    cot_above = lax.ppermute(cotangent, "coarse", down)
    mod = modulation(timestep, time_weight)

    hidden, weights = prepare(place, features, features_below, features_above, mod, conv_weight)
    partial_rows = parent_conv(place, features, hidden, all_spots, weights, up_weight)
    parts = lax.all_to_all(
        partial_rows.reshape(fine_size, bricks, fine_width), "fine", 0, 0, tiled=True
    )
    three = jnp.stack([cot_below, cotangent, cot_above])
    row_before = lax.ppermute(three[:, cells - column_count :], "fine", row_up)
    row_after = lax.ppermute(three[:, :column_count], "fine", row_down)

    grad_fine, sums = fine_block(
        fine_features, fine_cotangent, occupancy, parts, mod, inner_weight, outer_weight
    )
    pack = jnp.concatenate([sums.astype(BF16), spots])
    packs = lax.all_to_all(
        jnp.broadcast_to(pack[None], (fine_size,) + pack.shape), "fine", 0, 0, tiled=True
    )
    conv = cotangent_conv(cotangent, cot_below, cot_above, row_before, row_after, weights)
    packs_below = lax.ppermute(packs, "coarse", up)
    packs_above = lax.ppermute(packs, "coarse", down)
    grad_coarse = coarse_grad(
        place, features, cotangent, conv, mod, packs, packs_below, packs_above, weights, up_weight
    )
    return (grad_coarse.reshape(coarse_features.shape), grad_fine)


def solution(mesh):
    in_specs = (
        P(("coarse", "fine"), None, None),
        P(("coarse", "fine"), None),
        P(("coarse", "fine")),
        P(),
        P("coarse", "fine", None, None),
        P(),
        P(),
        P(),
        P(),
        P(),
        P("coarse", "fine", None, None),
        P(("coarse", "fine"), None, None),
    )
    out_specs = (P("coarse", "fine", None, None), P(("coarse", "fine"), None, None))
    return jax.shard_map(
        per_device, mesh=mesh, in_specs=in_specs, out_specs=out_specs, check_vma=False
    )
```

```python
import math

import jax
import jax.numpy as jnp
from jax import lax
from jax.experimental import pallas as pl
from jax.experimental.pallas import tpu as pltpu
from jax.sharding import PartitionSpec as P

EPSILON = 1e-06
MIB = 1024 * 1024
F32 = jnp.float32
BF16 = jnp.bfloat16
CHUNK = 64
VMEM = pl.BlockSpec(memory_space=pltpu.VMEM)
SMEM = pl.BlockSpec(memory_space=pltpu.SMEM)
HBM = pl.BlockSpec(memory_space=pltpu.HBM)


def start_copies(pairs, sems):
    copies = [pltpu.make_async_copy(src, dst, sems.at[i]) for i, (src, dst) in enumerate(pairs)]
    for copy in copies:
        copy.start()
    return copies


def sigmoid(values):
    return 0.5 * jnp.tanh(0.5 * values) + 0.5


def silu_slope(values):
    gate = sigmoid(values)
    return gate * (1.0 + values * (1.0 - gate))


def rms_scale(values):
    return lax.rsqrt(jnp.mean(values * values, axis=-1, keepdims=True) + EPSILON)


def modulation(timestep, time_weight):
    half_width = time_weight.shape[0] // 2
    frequency = jnp.exp(-math.log(10000.0) * jnp.arange(half_width, dtype=F32) / half_width)
    angles = timestep.astype(F32)[0] * frequency
    embedded = jnp.concatenate([jnp.sin(angles), jnp.cos(angles)]).astype(BF16)
    return jnp.dot(embedded[None, :], time_weight, preferred_element_type=F32)


def shift_pairs(size):
    up = [(i, i + 1) for i in range(size - 1)]
    return up, [(j, i) for i, j in up]


def near_slots(spots, first_row, valid=True):
    bricks = spots.shape[0]
    spots_t = spots.astype(F32).T
    row_t = spots_t[0:1, :].astype(jnp.int32) - first_row
    near_t = (row_t >= -1) & (row_t <= 4) & valid
    brick_i = lax.broadcasted_iota(jnp.int32, (bricks, bricks), 0)
    brick_j = lax.broadcasted_iota(jnp.int32, (bricks, bricks), 1)
    place_t = jnp.dot(
        jnp.broadcast_to(jnp.where(near_t, 1.0, 0.0), (16, bricks)).astype(BF16),
        jnp.where(brick_i < brick_j, 1.0, 0.0).astype(BF16),
        preferred_element_type=F32,
    )[0:1].astype(jnp.int32)
    count = jnp.sum(jnp.where(near_t, 1.0, 0.0)).astype(jnp.int32)
    return jnp.where(near_t, place_t, -1), count


def tap_cells(pick, spots, first_row, cells):
    found = jnp.dot(pick, spots, preferred_element_type=F32)
    row = found[:, 0:1].astype(jnp.int32) - first_row
    column = found[:, 64:65].astype(jnp.int32)
    lane = lax.broadcasted_iota(jnp.int32, (pick.shape[0], cells), 1)
    onehots = []
    for row_step in (-1, 0, 1):
        for column_step in (-1, 0, 1):
            y, x = row + row_step, column + column_step
            inside = (y >= 0) & (y < 4) & (x >= 0) & (x < 128)
            cell = jnp.where(inside, y * 128 + x, -1)
            onehots.append(jnp.where(lane == cell, 1.0, 0.0).astype(BF16))
    return onehots


def parent_conv_kernel(
    place, own_hbm, below_hbm, above_hbm, mod, info, conv_weight, up_hbm,
    out, cells_in, hidden, weights, up_weight, sems, tap_sems,
):
    cells, width = own_hbm.shape
    bricks = info.shape[0]
    taps = conv_weight.shape[0]
    sources = (below_hbm, own_hbm, above_hbm)
    copies = start_copies(
        [(source, cells_in.at[layer]) for layer, source in enumerate(sources)] + [(up_hbm, up_weight)], sems
    )
    loads = start_copies([(conv_weight.at[tap], weights.at[tap]) for tap in range(taps)], tap_sems)
    first_row = place[0]
    spots = info[...]
    slots, near_count = near_slots(spots, first_row)
    scale = 1.0 + mod[0:1, 256:768]
    shift = mod[0:1, 768:1280]
    for layer in range(3):
        copies[layer].wait()
        values = cells_in[layer].astype(F32)
        pre = values * rms_scale(values) * scale + shift
        act = pre * sigmoid(pre)
        if layer != 1:
            act = jnp.where(place[1 + layer // 2] > 0, act, 0.0)
        hidden[layer] = act.astype(BF16)
    copies[3].wait()

    def one_chunk(chunk, first=False):
        slot = lax.broadcasted_iota(jnp.int32, (CHUNK, bricks), 0) + chunk * CHUNK
        pick = jnp.where(slot == slots, 1.0, 0.0).astype(BF16)
        onehots = tap_cells(pick, spots, first_row, cells)
        onehot = jnp.concatenate(onehots, axis=0)
        total = jnp.dot(onehots[4], cells_in[1], preferred_element_type=F32)
        for layer in range(3):
            gathered = jnp.dot(onehot, hidden[layer], preferred_element_type=F32).astype(BF16)
            for corner in range(9):
                tap = 9 * layer + corner
                if first:
                    loads[tap].wait()
                total += jnp.dot(
                    gathered[corner * CHUNK : (corner + 1) * CHUNK],
                    weights[tap],
                    preferred_element_type=F32,
                )
        lifted = jnp.dot(total.astype(BF16), up_weight[...], preferred_element_type=F32)
        high = lifted.astype(BF16)
        low = (lifted - high.astype(F32)).astype(BF16)
        across = (((0,), (0,)), ((), ()))
        return lax.dot_general(pick, high, across, preferred_element_type=F32) + lax.dot_general(
            pick, low, across, preferred_element_type=F32
        )

    out[...] = one_chunk(0, True)

    @pl.loop(1, (near_count + CHUNK - 1) // CHUNK)
    def _(chunk):
        out[...] += one_chunk(chunk)


def parent_conv(place, own, below, above, mod, info, conv_weight, up_weight):
    taps = conv_weight.shape[0]
    return pl.pallas_call(
        parent_conv_kernel,
        out_shape=jax.ShapeDtypeStruct((info.shape[0], up_weight.shape[1]), F32),
        in_specs=[SMEM, HBM, HBM, HBM, VMEM, VMEM, HBM, HBM],
        out_specs=VMEM,
        scratch_shapes=[
            pltpu.VMEM((3,) + own.shape, BF16),
            pltpu.VMEM((3,) + own.shape, BF16),
            pltpu.VMEM(conv_weight.shape, BF16),
            pltpu.VMEM(up_weight.shape, BF16),
            pltpu.SemaphoreType.DMA((4,)),
            pltpu.SemaphoreType.DMA((taps,)),
        ],
        compiler_params=pltpu.CompilerParams(vmem_limit_bytes=50 * MIB),
        cost_estimate=pl.CostEstimate(flops=2 * 128 * 27 * 512 * 512, bytes_accessed=16 * MIB, transcendentals=0),
        name="parent_conv",
    )(place, own, below, above, mod, info, conv_weight, up_weight)


def fine_kernel(
    features_hbm, cotangent_hbm, occupied_hbm, parts, spots, mod, inner_hbm, outer_hbm, grads_hbm, pack,
    features, cotangent, grads, occupied, inner_weight, outer_weight, sums, sems, in_sems, out_sems,
):
    bricks = features.shape[0]

    def fetch(brick):
        return (
            pltpu.make_async_copy(features_hbm.at[brick], features.at[brick], in_sems.at[0, brick]),
            pltpu.make_async_copy(cotangent_hbm.at[brick], cotangent.at[brick], in_sems.at[1, brick]),
        )

    def flush(brick):
        return pltpu.make_async_copy(grads.at[brick], grads_hbm.at[brick], out_sems.at[brick])

    copies = start_copies(
        [(occupied_hbm, occupied), (inner_hbm, inner_weight), (outer_hbm, outer_weight)], sems
    )
    for brick in range(bricks):
        for copy in fetch(brick):
            copy.start()
    scale = 1.0 + mod[0:1, 0:128]
    shift = mod[0:1, 128:256]
    for copy in copies:
        copy.wait()
    spread = occupied[...].astype(F32).T.astype(BF16)

    @pl.loop(0, bricks // 2)
    def _(step):
        for item in range(2):
            brick = step * 2 + item
            for copy in fetch(brick):
                copy.wait()
            mask = jnp.dot(
                spread,
                jnp.where(lax.broadcasted_iota(jnp.int32, (bricks, 128), 0) == brick, 1.0, 0.0).astype(BF16),
                preferred_element_type=F32,
            )
            lifted = jnp.sum(parts[:, pl.ds(brick, 1), :], axis=0).astype(BF16).astype(F32)
            fine_in = features[brick].astype(F32) + lifted
            fine_scale = rms_scale(fine_in)
            normed = fine_in * fine_scale
            pre = normed * scale + shift
            gate = sigmoid(pre)
            act = pre * gate
            slope = gate + act * (1.0 - gate)
            inner_pre = jnp.dot(act.astype(BF16), inner_weight[...], preferred_element_type=F32)
            masked = cotangent[brick].astype(F32) * mask
            grad_hidden = lax.dot_general(
                masked.astype(BF16), outer_weight[...], (((1,), (1,)), ((), ())), preferred_element_type=F32
            )
            grad_inner = (grad_hidden * silu_slope(inner_pre)).astype(BF16)
            grad_act = lax.dot_general(
                grad_inner, inner_weight[...], (((1,), (1,)), ((), ())), preferred_element_type=F32
            )
            grad_norm = grad_act * slope * scale
            inner = jnp.mean(grad_norm * normed, axis=-1, keepdims=True)
            grad_in = masked + fine_scale * (grad_norm - normed * inner)
            grads[brick] = grad_in.astype(BF16)
            flush(brick).start()
            sums[pl.ds(brick, 1), :] = jnp.sum(grad_in, axis=0, keepdims=True)

    total = sums[...].astype(BF16)
    for target in range(pack.shape[0]):
        pack[target, 0:bricks] = total
        pack[target, bricks : 2 * bricks] = spots[...]
    for brick in range(bricks):
        flush(brick).wait()


def fine_block(features, cotangent, occupied, parts, spots, mod, inner_weight, outer_weight):
    bricks, voxels, width = features.shape
    return pl.pallas_call(
        fine_kernel,
        out_shape=(
            jax.ShapeDtypeStruct(features.shape, BF16),
            jax.ShapeDtypeStruct((parts.shape[0], 2 * bricks, width), BF16),
        ),
        in_specs=[HBM, HBM, HBM, VMEM, VMEM, VMEM, HBM, HBM],
        out_specs=(HBM, VMEM),
        scratch_shapes=[
            pltpu.VMEM(features.shape, BF16),
            pltpu.VMEM(features.shape, BF16),
            pltpu.VMEM(features.shape, BF16),
            pltpu.VMEM(occupied.shape, jnp.int32),
            pltpu.VMEM(inner_weight.shape, BF16),
            pltpu.VMEM(outer_weight.shape, BF16),
            pltpu.VMEM((bricks, width), F32),
            pltpu.SemaphoreType.DMA((3,)),
            pltpu.SemaphoreType.DMA((2, bricks)),
            pltpu.SemaphoreType.DMA((bricks,)),
        ],
        compiler_params=pltpu.CompilerParams(vmem_limit_bytes=60 * MIB),
        cost_estimate=pl.CostEstimate(flops=3 * 10**10, bytes_accessed=6 * MIB, transcendentals=2**21),
        name="fine_block",
    )(features, cotangent, occupied, parts, spots, mod, inner_weight, outer_weight)


def edge_rows_kernel(own, below, above, first, last, sems):
    cells = own.shape[0]
    pairs = []
    for layer, source in enumerate((below, own, above)):
        pairs.append((source.at[pl.ds(0, 128)], first.at[layer]))
        pairs.append((source.at[pl.ds(cells - 128, 128)], last.at[layer]))
    for copy in start_copies(pairs, sems):
        copy.wait()


def edge_rows(own, below, above):
    shape = jax.ShapeDtypeStruct((3, 128, own.shape[1]), BF16)
    return pl.pallas_call(
        edge_rows_kernel,
        out_shape=(shape, shape),
        in_specs=[HBM] * 3,
        out_specs=(HBM, HBM),
        scratch_shapes=[pltpu.SemaphoreType.DMA((6,))],
        cost_estimate=pl.CostEstimate(flops=0, bytes_accessed=2 * MIB, transcendentals=0),
        name="edge_rows",
    )(own, below, above)


def cell_lift(pack, up_weight, first_row):
    spots_t = pack[:, 16:32, :].reshape(256, 128).astype(F32).T
    row = spots_t[0:1, :].astype(jnp.int32) - first_row + 1
    column = spots_t[64:65, :].astype(jnp.int32)
    onehot = jnp.where(
        lax.broadcasted_iota(jnp.int32, (6 * 128, 256), 0) == row * 128 + column, 1.0, 0.0
    ).astype(BF16)
    cell_sums = jnp.dot(onehot, pack[:, 0:16, :].reshape(256, 128), preferred_element_type=F32).astype(BF16)
    return lax.dot_general(cell_sums, up_weight, (((1,), (1,)), ((), ())), preferred_element_type=F32)


def add_taps(grad, weights, loads, layer_step, slot, total, fresh):
    for row_step in range(3):
        loads[row_step].wait()
        begin = (2 - row_step) * 128
        block = grad[begin : begin + 512]
        for column_step in range(3):
            piece = lax.dot_general(
                block, weights[slot + row_step, column_step], (((1,), (1,)), ((), ())), preferred_element_type=F32
            )
            if fresh and row_step == 0:
                total[column_step] = piece
            else:
                total[column_step] += piece


def join_columns(total):
    column = lax.broadcasted_iota(jnp.int32, (512, 1), 0) % 128
    left = jnp.where(column == 127, 0.0, pltpu.roll(total[0], 511, 0))
    right = jnp.where(column == 0, 0.0, pltpu.roll(total[2], 1, 0))
    return total[1] + left + right


def own_layer_kernel(
    place, own_hbm, row_before, row_after, pack, conv_weight, up_hbm,
    conv, center, cot, grad, weights, up_weight, total, sems, tap_sems,
):
    copies = start_copies(
        [
            (up_hbm, up_weight),
            (own_hbm, cot.at[pl.ds(128, 512)]),
            (row_before.at[1], cot.at[pl.ds(0, 128)]),
            (row_after.at[1], cot.at[pl.ds(640, 128)]),
        ],
        sems,
    )
    loads = start_copies(
        [(conv_weight.at[pl.ds(9 + 3 * part, 3)], weights.at[part]) for part in range(3)], tap_sems
    )
    for copy in copies:
        copy.wait()
    whole = cell_lift(pack, up_weight[...], place[0]) + cot[...].astype(F32)
    center[...] = whole[128:640]
    grad[...] = whole.astype(BF16)
    add_taps(grad, weights, loads, 1, 0, total, True)
    conv[...] = join_columns(total)


def own_layer(place, own, row_before, row_after, pack, conv_weight, up_weight):
    cells, width = own.shape
    shape = jax.ShapeDtypeStruct((cells, width), F32)
    return pl.pallas_call(
        own_layer_kernel,
        out_shape=(shape, shape),
        in_specs=[SMEM, HBM, HBM, HBM, VMEM, HBM, HBM],
        out_specs=(VMEM, VMEM),
        scratch_shapes=[
            pltpu.VMEM((6 * 128, width), BF16),
            pltpu.VMEM((6 * 128, width), BF16),
            pltpu.VMEM((3, 3, width, width), BF16),
            pltpu.VMEM(up_weight.shape, BF16),
            pltpu.VMEM((3, cells, width), F32),
            pltpu.SemaphoreType.DMA((4,)),
            pltpu.SemaphoreType.DMA((3,)),
        ],
        compiler_params=pltpu.CompilerParams(vmem_limit_bytes=50 * MIB),
        cost_estimate=pl.CostEstimate(flops=2 * 512 * 9 * 512 * 512, bytes_accessed=6 * MIB, transcendentals=0),
        name="own_layer",
    )(place, own, row_before, row_after, pack, conv_weight, up_weight)


def coarse_grad_kernel(
    place, features_hbm, below_hbm, above_hbm, row_before, row_after, conv_hbm, center_hbm, mod,
    pack_below, pack_above, conv_weight, up_hbm,
    out, cot, grad, weights, up_weight, total, features, conv, center, sems, tap_sems, late_sems,
):
    sources = ((0, below_hbm), (2, above_hbm))
    pairs = [(up_hbm, up_weight)]
    for slot, (layer, source) in enumerate(sources):
        pairs.append((source, cot.at[slot, pl.ds(128, 512)]))
        pairs.append((row_before.at[layer], cot.at[slot, pl.ds(0, 128)]))
        pairs.append((row_after.at[layer], cot.at[slot, pl.ds(640, 128)]))
    copies = start_copies(pairs, sems)
    loads = start_copies(
        [
            (conv_weight.at[pl.ds(9 * (2 - layer) + 3 * part, 3)], weights.at[3 * slot + part])
            for slot, (layer, source) in enumerate(sources)
            for part in range(3)
        ],
        tap_sems,
    )
    late = start_copies([(features_hbm, features), (conv_hbm, conv), (center_hbm, center)], late_sems)
    copies[0].wait()
    for slot, pack in ((0, pack_below), (1, pack_above)):
        for copy in copies[1 + 3 * slot : 4 + 3 * slot]:
            copy.wait()
        lift = cell_lift(pack, up_weight[...], place[0])
        grad[slot] = (lift + cot[slot].astype(F32)).astype(BF16)
        add_taps(
            grad.at[slot], weights, loads[3 * slot : 3 * slot + 3], 2 - 2 * slot, 3 * slot, total, slot == 0
        )
    for copy in late:
        copy.wait()
    grad_conv = conv[...] + join_columns(total)
    scale = 1.0 + mod[0:1, 256:768]
    shift = mod[0:1, 768:1280]
    values = features[...].astype(F32)
    coarse_scale = rms_scale(values)
    normed = values * coarse_scale
    grad_cn = grad_conv * silu_slope(normed * scale + shift) * scale
    inner = jnp.mean(grad_cn * normed, axis=-1, keepdims=True)
    out[...] = (center[...] + coarse_scale * (grad_cn - normed * inner)).astype(BF16)


def coarse_grad(
    place, features, below, above, row_before, row_after, conv, center, mod, pack_below, pack_above, conv_weight, up_weight
):
    cells, width = features.shape
    return pl.pallas_call(
        coarse_grad_kernel,
        out_shape=jax.ShapeDtypeStruct((cells, width), BF16),
        in_specs=[SMEM] + [HBM] * 7 + [VMEM] * 3 + [HBM] * 2,
        out_specs=VMEM,
        scratch_shapes=[
            pltpu.VMEM((2, 6 * 128, width), BF16),
            pltpu.VMEM((2, 6 * 128, width), BF16),
            pltpu.VMEM((6, 3, width, width), BF16),
            pltpu.VMEM(up_weight.shape, BF16),
            pltpu.VMEM((3, cells, width), F32),
            pltpu.VMEM((cells, width), BF16),
            pltpu.VMEM((cells, width), F32),
            pltpu.VMEM((cells, width), F32),
            pltpu.SemaphoreType.DMA((7,)),
            pltpu.SemaphoreType.DMA((6,)),
            pltpu.SemaphoreType.DMA((3,)),
        ],
        compiler_params=pltpu.CompilerParams(vmem_limit_bytes=50 * MIB),
        cost_estimate=pl.CostEstimate(flops=2 * 512 * 18 * 512 * 512, bytes_accessed=16 * MIB, transcendentals=0),
        name="coarse_grad",
    )(place, features, below, above, row_before, row_after, conv, center, mod, pack_below, pack_above, conv_weight, up_weight)


def per_device(
    fine_features,
    occupancy,
    parent,
    timestep,
    coarse_features,
    time_weight,
    conv_weight,
    up_weight,
    inner_weight,
    outer_weight,
    coarse_cotangent,
    fine_cotangent,
):
    layer_count, row_count, column_count, width = coarse_features.shape
    fine_width = up_weight.shape[1]
    bricks = parent.shape[0]
    fine_size, coarse_size = lax.axis_size("fine"), lax.axis_size("coarse")
    coarse_index, fine_index = lax.axis_index("coarse"), lax.axis_index("fine")
    cells = layer_count * row_count * column_count
    up, down = shift_pairs(coarse_size)
    row_up, row_down = shift_pairs(fine_size)

    local = parent - coarse_index * (cells * fine_size)
    row, column = local // column_count, local % column_count
    lane = jnp.arange(128)[None, :]
    spots = jnp.where(lane < 64, row[:, None], column[:, None]).astype(BF16)
    place = jnp.stack(
        [fine_index * row_count, (coarse_index > 0).astype(jnp.int32), (coarse_index < coarse_size - 1).astype(jnp.int32)]
    ).astype(jnp.int32)

    features = coarse_features.reshape(cells, width)
    cotangent = coarse_cotangent.reshape(cells, width)
    spots_out = jnp.broadcast_to(spots[None], (fine_size, bricks, 128))
    sent_features, _ = lax.optimization_barrier((features, spots_out))
    all_spots = lax.all_to_all(spots_out, "fine", 0, 0, tiled=True).reshape(fine_size * bricks, 128)
    features_below = lax.ppermute(sent_features, "coarse", up)
    features_above = lax.ppermute(sent_features, "coarse", down)
    sent_cotangent, _ = lax.optimization_barrier((cotangent, all_spots))
    cot_below = lax.ppermute(sent_cotangent, "coarse", up)
    cot_above = lax.ppermute(sent_cotangent, "coarse", down)
    mod = modulation(timestep, time_weight)

    partial_rows = parent_conv(
        place, features, features_below, features_above, mod, all_spots, conv_weight, up_weight
    )
    parts = lax.all_to_all(
        partial_rows.reshape(fine_size, bricks, fine_width), "fine", 0, 0, tiled=True
    )
    edge_cotangent, _ = lax.optimization_barrier((cotangent, partial_rows))
    first_rows, last_rows = edge_rows(edge_cotangent, cot_below, cot_above)
    row_before = lax.ppermute(last_rows, "fine", row_up)
    row_after = lax.ppermute(first_rows, "fine", row_down)

    grad_fine, pack = fine_block(
        fine_features, fine_cotangent, occupancy, parts, spots, mod, inner_weight, outer_weight
    )
    packs = lax.all_to_all(pack, "fine", 0, 0, tiled=True)
    packs_below = lax.ppermute(packs, "coarse", up)
    packs_above = lax.ppermute(packs, "coarse", down)
    conv, center = own_layer(place, cotangent, row_before, row_after, packs, conv_weight, up_weight)
    grad_coarse = coarse_grad(
        place, features, cot_below, cot_above, row_before, row_after, conv, center, mod,
        packs_below, packs_above, conv_weight, up_weight
    )
    return (grad_coarse.reshape(coarse_features.shape), grad_fine)


def solution(mesh):
    in_specs = (
        P(("coarse", "fine"), None, None),
        P(("coarse", "fine"), None),
        P(("coarse", "fine")),
        P(),
        P("coarse", "fine", None, None),
        P(),
        P(),
        P(),
        P(),
        P(),
        P("coarse", "fine", None, None),
        P(("coarse", "fine"), None, None),
    )
    out_specs = (P("coarse", "fine", None, None), P(("coarse", "fine"), None, None))
    return jax.shard_map(
        per_device, mesh=mesh, in_specs=in_specs, out_specs=out_specs, check_vma=False
    )
```

```python
import math

import jax
import jax.numpy as jnp
from jax import lax
from jax.experimental import pallas as pl
from jax.experimental.pallas import tpu as pltpu
from jax.sharding import PartitionSpec as P

EPSILON = 1e-06
MIB = 1024 * 1024
F32 = jnp.float32
BF16 = jnp.bfloat16
CHUNK = 64
VMEM = pl.BlockSpec(memory_space=pltpu.VMEM)
SMEM = pl.BlockSpec(memory_space=pltpu.SMEM)
HBM = pl.BlockSpec(memory_space=pltpu.HBM)


def start_copies(pairs, sems):
    copies = [pltpu.make_async_copy(src, dst, sems.at[i]) for i, (src, dst) in enumerate(pairs)]
    for copy in copies:
        copy.start()
    return copies


def sigmoid(values):
    return 0.5 * jnp.tanh(0.5 * values) + 0.5


def silu_slope(values):
    gate = sigmoid(values)
    return gate * (1.0 + values * (1.0 - gate))


def rms_scale(values):
    return lax.rsqrt(jnp.mean(values * values, axis=-1, keepdims=True) + EPSILON)


def modulation(timestep, time_weight):
    half_width = time_weight.shape[0] // 2
    frequency = jnp.exp(-math.log(10000.0) * jnp.arange(half_width, dtype=F32) / half_width)
    angles = timestep.astype(F32)[0] * frequency
    embedded = jnp.concatenate([jnp.sin(angles), jnp.cos(angles)]).astype(BF16)
    return jnp.dot(embedded[None, :], time_weight, preferred_element_type=F32)


def shift_pairs(size):
    up = [(i, i + 1) for i in range(size - 1)]
    return up, [(j, i) for i, j in up]


def near_slots(spots, first_row, valid=True):
    bricks = spots.shape[0]
    spots_t = spots.astype(F32).T
    row_t = spots_t[0:1, :].astype(jnp.int32) - first_row
    near_t = (row_t >= -1) & (row_t <= 4) & valid
    brick_i = lax.broadcasted_iota(jnp.int32, (bricks, bricks), 0)
    brick_j = lax.broadcasted_iota(jnp.int32, (bricks, bricks), 1)
    place_t = jnp.dot(
        jnp.broadcast_to(jnp.where(near_t, 1.0, 0.0), (16, bricks)).astype(BF16),
        jnp.where(brick_i < brick_j, 1.0, 0.0).astype(BF16),
        preferred_element_type=F32,
    )[0:1].astype(jnp.int32)
    count = jnp.sum(jnp.where(near_t, 1.0, 0.0)).astype(jnp.int32)
    return jnp.where(near_t, place_t, -1), count


def tap_cells(pick, spots, first_row, cells):
    found = jnp.dot(pick, spots, preferred_element_type=F32)
    row = found[:, 0:1].astype(jnp.int32) - first_row
    column = found[:, 64:65].astype(jnp.int32)
    lane = lax.broadcasted_iota(jnp.int32, (pick.shape[0], cells), 1)
    onehots = []
    for row_step in (-1, 0, 1):
        for column_step in (-1, 0, 1):
            y, x = row + row_step, column + column_step
            inside = (y >= 0) & (y < 4) & (x >= 0) & (x < 128)
            cell = jnp.where(inside, y * 128 + x, -1)
            onehots.append(jnp.where(lane == cell, 1.0, 0.0).astype(BF16))
    return onehots


def parent_conv_kernel(
    place, own_hbm, below_hbm, above_hbm, mod, info, conv_weight, up_hbm,
    out, cells_in, hidden, weights, up_weight, sems, tap_sems,
):
    cells, width = own_hbm.shape
    bricks = info.shape[0]
    taps = conv_weight.shape[0]
    sources = (below_hbm, own_hbm, above_hbm)
    copies = start_copies(
        [(source, cells_in.at[layer]) for layer, source in enumerate(sources)] + [(up_hbm, up_weight)], sems
    )
    loads = start_copies([(conv_weight.at[tap], weights.at[tap]) for tap in range(taps)], tap_sems)
    first_row = place[0]
    spots = info[...]
    slots, near_count = near_slots(spots, first_row)
    scale = 1.0 + mod[0:1, 256:768]
    shift = mod[0:1, 768:1280]
    for layer in range(3):
        copies[layer].wait()
        values = cells_in[layer].astype(F32)
        pre = values * rms_scale(values) * scale + shift
        act = pre * sigmoid(pre)
        if layer != 1:
            act = jnp.where(place[1 + layer // 2] > 0, act, 0.0)
        hidden[layer] = act.astype(BF16)
    copies[3].wait()

    def one_chunk(chunk, first=False):
        slot = lax.broadcasted_iota(jnp.int32, (CHUNK, bricks), 0) + chunk * CHUNK
        pick = jnp.where(slot == slots, 1.0, 0.0).astype(BF16)
        onehots = tap_cells(pick, spots, first_row, cells)
        onehot = jnp.concatenate(onehots, axis=0)
        total = jnp.dot(onehots[4], cells_in[1], preferred_element_type=F32)
        for layer in range(3):
            gathered = jnp.dot(onehot, hidden[layer], preferred_element_type=F32).astype(BF16)
            for corner in range(9):
                tap = 9 * layer + corner
                if first:
                    loads[tap].wait()
                total += jnp.dot(
                    gathered[corner * CHUNK : (corner + 1) * CHUNK],
                    weights[tap],
                    preferred_element_type=F32,
                )
        lifted = jnp.dot(total.astype(BF16), up_weight[...], preferred_element_type=F32)
        high = lifted.astype(BF16)
        low = (lifted - high.astype(F32)).astype(BF16)
        across = (((0,), (0,)), ((), ()))
        return lax.dot_general(pick, high, across, preferred_element_type=F32) + lax.dot_general(
            pick, low, across, preferred_element_type=F32
        )

    out[...] = one_chunk(0, True)

    @pl.loop(1, (near_count + CHUNK - 1) // CHUNK)
    def _(chunk):
        out[...] += one_chunk(chunk)


def parent_conv(place, own, below, above, mod, info, conv_weight, up_weight):
    taps = conv_weight.shape[0]
    return pl.pallas_call(
        parent_conv_kernel,
        out_shape=jax.ShapeDtypeStruct((info.shape[0], up_weight.shape[1]), F32),
        in_specs=[SMEM] + [pl.BlockSpec(memory_space=pl.ANY)] * 3 + [VMEM, VMEM] + [pl.BlockSpec(memory_space=pl.ANY)] * 2,
        out_specs=VMEM,
        scratch_shapes=[
            pltpu.VMEM((3,) + own.shape, BF16),
            pltpu.VMEM((3,) + own.shape, BF16),
            pltpu.VMEM(conv_weight.shape, BF16),
            pltpu.VMEM(up_weight.shape, BF16),
            pltpu.SemaphoreType.DMA((4,)),
            pltpu.SemaphoreType.DMA((taps,)),
        ],
        compiler_params=pltpu.CompilerParams(vmem_limit_bytes=50 * MIB),
        cost_estimate=pl.CostEstimate(flops=2 * 128 * 27 * 512 * 512, bytes_accessed=16 * MIB, transcendentals=0),
        name="parent_conv",
    )(place, own, below, above, mod, info, conv_weight, up_weight)


def fine_kernel(
    features, cotangent, occupied, parts, spots, mod, inner_weight, outer_weight, grads, pack, spread, sums
):
    step = pl.program_id(0)
    bricks = occupied.shape[0]

    @pl.when(step == 0)
    def _():
        spread[...] = occupied[...].astype(F32).T.astype(BF16)

    scale = 1.0 + mod[0:1, 0:128]
    shift = mod[0:1, 128:256]
    for item in range(features.shape[0]):
        brick = step * features.shape[0] + item
        mask = jnp.dot(
            spread[...],
            jnp.where(lax.broadcasted_iota(jnp.int32, (bricks, 128), 0) == brick, 1.0, 0.0).astype(BF16),
            preferred_element_type=F32,
        )
        lifted = jnp.sum(parts[:, pl.ds(brick, 1), :], axis=0).astype(BF16).astype(F32)
        fine_in = features[item].astype(F32) + lifted
        fine_scale = rms_scale(fine_in)
        normed = fine_in * fine_scale
        pre = normed * scale + shift
        gate = sigmoid(pre)
        act = pre * gate
        slope = gate + act * (1.0 - gate)
        inner_pre = jnp.dot(act.astype(BF16), inner_weight[...], preferred_element_type=F32)
        masked = cotangent[item].astype(F32) * mask
        grad_hidden = lax.dot_general(
            masked.astype(BF16), outer_weight[...], (((1,), (1,)), ((), ())), preferred_element_type=F32
        )
        grad_inner = (grad_hidden * silu_slope(inner_pre)).astype(BF16)
        grad_act = lax.dot_general(
            grad_inner, inner_weight[...], (((1,), (1,)), ((), ())), preferred_element_type=F32
        )
        grad_norm = grad_act * slope * scale
        inner = jnp.mean(grad_norm * normed, axis=-1, keepdims=True)
        grad_in = masked + fine_scale * (grad_norm - normed * inner)
        grads[item] = grad_in.astype(BF16)
        sums[pl.ds(brick, 1), :] = jnp.sum(grad_in, axis=0, keepdims=True)

    @pl.when(step == pl.num_programs(0) - 1)
    def _():
        total = sums[...].astype(BF16)
        for target in range(pack.shape[0]):
            pack[target, 0:bricks] = total
            pack[target, bricks : 2 * bricks] = spots[...]


def fine_block(features, cotangent, occupied, parts, spots, mod, inner_weight, outer_weight):
    bricks, voxels, width = features.shape
    per_step = 2
    block = pl.BlockSpec((per_step, voxels, width), lambda i: (i, 0, 0))

    def whole(shape):
        return pl.BlockSpec(shape, lambda i: (0,) * len(shape))

    pack_shape = (parts.shape[0], 2 * bricks, width)
    fixed = (occupied, parts, spots, mod, inner_weight, outer_weight)
    return pl.pallas_call(
        fine_kernel,
        grid=(bricks // per_step,),
        out_shape=(
            jax.ShapeDtypeStruct(features.shape, BF16),
            jax.ShapeDtypeStruct(pack_shape, BF16),
        ),
        in_specs=[block, block] + [whole(array.shape) for array in fixed],
        out_specs=(block, whole(pack_shape)),
        scratch_shapes=[pltpu.VMEM((voxels, bricks), BF16), pltpu.VMEM((bricks, width), F32)],
        compiler_params=pltpu.CompilerParams(vmem_limit_bytes=58 * MIB),
        cost_estimate=pl.CostEstimate(flops=3 * 10**10, bytes_accessed=6 * MIB, transcendentals=2**21),
        name="fine_block",
    )(features, cotangent, *fixed)


def edge_rows_kernel(own, below, above, first, last, sems):
    cells = own.shape[0]
    pairs = []
    for layer, source in enumerate((below, own, above)):
        pairs.append((source.at[pl.ds(0, 128)], first.at[layer]))
        pairs.append((source.at[pl.ds(cells - 128, 128)], last.at[layer]))
    for copy in start_copies(pairs, sems):
        copy.wait()


def edge_rows(own, below, above):
    shape = jax.ShapeDtypeStruct((3, 128, own.shape[1]), BF16)
    return pl.pallas_call(
        edge_rows_kernel,
        out_shape=(shape, shape),
        in_specs=[pl.BlockSpec(memory_space=pl.ANY)] * 3,
        out_specs=(VMEM, VMEM),
        scratch_shapes=[pltpu.SemaphoreType.DMA((6,))],
        cost_estimate=pl.CostEstimate(flops=0, bytes_accessed=2 * MIB, transcendentals=0),
        name="edge_rows",
    )(own, below, above)


def cell_lift(pack, up_weight, first_row):
    spots_t = pack[:, 16:32, :].reshape(256, 128).astype(F32).T
    row = spots_t[0:1, :].astype(jnp.int32) - first_row + 1
    column = spots_t[64:65, :].astype(jnp.int32)
    onehot = jnp.where(
        lax.broadcasted_iota(jnp.int32, (6 * 128, 256), 0) == row * 128 + column, 1.0, 0.0
    ).astype(BF16)
    cell_sums = jnp.dot(onehot, pack[:, 0:16, :].reshape(256, 128), preferred_element_type=F32).astype(BF16)
    return lax.dot_general(cell_sums, up_weight, (((1,), (1,)), ((), ())), preferred_element_type=F32)


def own_lift_kernel(place, packs, up_hbm, lift, up_weight, sems):
    (copy,) = start_copies([(up_hbm, up_weight)], sems)
    copy.wait()
    lift[...] = cell_lift(packs, up_weight[...], place[0])


def own_lift(place, packs, up_weight):
    width = up_weight.shape[0]
    return pl.pallas_call(
        own_lift_kernel,
        out_shape=jax.ShapeDtypeStruct((6 * 128, width), F32),
        in_specs=[SMEM, VMEM, pl.BlockSpec(memory_space=pl.ANY)],
        out_specs=VMEM,
        scratch_shapes=[pltpu.VMEM(up_weight.shape, BF16), pltpu.SemaphoreType.DMA((1,))],
        compiler_params=pltpu.CompilerParams(vmem_limit_bytes=40 * MIB),
        cost_estimate=pl.CostEstimate(flops=3 * 10**10, bytes_accessed=2 * MIB, transcendentals=0),
        name="own_lift",
    )(place, packs, up_weight)


def coarse_grad_kernel(
    place, features_hbm, own_hbm, below_hbm, above_hbm, row_before, row_after, mod, lift_hbm, packs_below, packs_above,
    conv_weight, up_hbm,
    out, cot, grad, lift, center, total, weights, up_weight, features, sems, tap_sems,
):
    cells, width = own_hbm.shape
    taps = conv_weight.shape[0]
    order = (1, 0, 2)
    sources = (below_hbm, own_hbm, above_hbm)
    pairs = [(lift_hbm, lift)]
    for layer in order:
        pairs.append((sources[layer], cot.at[layer, pl.ds(128, cells)]))
        pairs.append((row_before.at[layer], cot.at[layer, pl.ds(0, 128)]))
        pairs.append((row_after.at[layer], cot.at[layer, pl.ds(640, 128)]))
    pairs += [(up_hbm, up_weight), (features_hbm, features)]
    copies = start_copies(pairs, sems)
    loads = start_copies(
        [
            (conv_weight.at[pl.ds(9 * (2 - layer) + 3 * row_step, 3)], weights.at[3 * slot + row_step])
            for slot, layer in enumerate(order)
            for row_step in range(3)
        ],
        tap_sems,
    )
    for slot, layer in enumerate(order):
        for copy in copies[1 + 3 * slot : 4 + 3 * slot]:
            copy.wait()
        if layer == 1:
            copies[0].wait()
            whole = lift[...] + cot[layer].astype(F32)
            center[...] = whole[128:640]
            copies[10].wait()
        else:
            pack = packs_below if layer == 0 else packs_above
            whole = cell_lift(pack, up_weight[...], place[0]) + cot[layer].astype(F32)
        grad[layer] = whole.astype(BF16)
        for row_step in range(3):
            loads[3 * slot + row_step].wait()
            begin = (2 - row_step) * 128
            block = grad[layer, begin : begin + cells]
            for column_step in range(3):
                piece = lax.dot_general(
                    block,
                    weights[3 * slot + row_step, column_step],
                    (((1,), (1,)), ((), ())),
                    preferred_element_type=F32,
                )
                if slot == 0 and row_step == 0:
                    total[column_step] = piece
                else:
                    total[column_step] += piece
    copies[11].wait()
    column = lax.broadcasted_iota(jnp.int32, (cells, 1), 0) % 128
    left = jnp.where(column == 127, 0.0, pltpu.roll(total[0], cells - 1, 0))
    right = jnp.where(column == 0, 0.0, pltpu.roll(total[2], 1, 0))
    grad_conv = total[1] + left + right
    scale = 1.0 + mod[0:1, 256:768]
    shift = mod[0:1, 768:1280]
    values = features[...].astype(F32)
    coarse_scale = rms_scale(values)
    normed = values * coarse_scale
    grad_cn = grad_conv * silu_slope(normed * scale + shift) * scale
    inner = jnp.mean(grad_cn * normed, axis=-1, keepdims=True)
    out[...] = (center[...] + coarse_scale * (grad_cn - normed * inner)).astype(BF16)


def coarse_grad(
    place, features, own, below, above, row_before, row_after, mod, lift, packs_below, packs_above, conv_weight, up_weight
):
    cells, width = features.shape
    taps = conv_weight.shape[0]
    anywhere = pl.BlockSpec(memory_space=pl.ANY)
    return pl.pallas_call(
        coarse_grad_kernel,
        out_shape=jax.ShapeDtypeStruct((cells, width), BF16),
        in_specs=[SMEM] + [anywhere] * 6 + [VMEM, anywhere, VMEM, VMEM] + [anywhere] * 2,
        out_specs=VMEM,
        scratch_shapes=[
            pltpu.VMEM((3, 6 * 128, width), BF16),
            pltpu.VMEM((3, 6 * 128, width), BF16),
            pltpu.VMEM((6 * 128, width), F32),
            pltpu.VMEM((cells, width), F32),
            pltpu.VMEM((3, cells, width), F32),
            pltpu.VMEM((taps // 3, 3, width, width), BF16),
            pltpu.VMEM(up_weight.shape, BF16),
            pltpu.VMEM((cells, width), BF16),
            pltpu.SemaphoreType.DMA((12,)),
            pltpu.SemaphoreType.DMA((taps // 3,)),
        ],
        compiler_params=pltpu.CompilerParams(vmem_limit_bytes=52 * MIB),
        cost_estimate=pl.CostEstimate(flops=2 * 512 * 27 * 512 * 512, bytes_accessed=18 * MIB, transcendentals=0),
        name="coarse_grad",
    )(place, features, own, below, above, row_before, row_after, mod, lift, packs_below, packs_above, conv_weight, up_weight)


def per_device(
    fine_features,
    occupancy,
    parent,
    timestep,
    coarse_features,
    time_weight,
    conv_weight,
    up_weight,
    inner_weight,
    outer_weight,
    coarse_cotangent,
    fine_cotangent,
):
    layer_count, row_count, column_count, width = coarse_features.shape
    fine_width = up_weight.shape[1]
    bricks = parent.shape[0]
    fine_size, coarse_size = lax.axis_size("fine"), lax.axis_size("coarse")
    coarse_index, fine_index = lax.axis_index("coarse"), lax.axis_index("fine")
    cells = layer_count * row_count * column_count
    up, down = shift_pairs(coarse_size)
    row_up, row_down = shift_pairs(fine_size)

    local = parent - coarse_index * (cells * fine_size)
    row, column = local // column_count, local % column_count
    lane = jnp.arange(128)[None, :]
    spots = jnp.where(lane < 64, row[:, None], column[:, None]).astype(BF16)
    place = jnp.stack(
        [fine_index * row_count, (coarse_index > 0).astype(jnp.int32), (coarse_index < coarse_size - 1).astype(jnp.int32)]
    ).astype(jnp.int32)

    features = coarse_features.reshape(cells, width)
    cotangent = coarse_cotangent.reshape(cells, width)
    spots_out = jnp.broadcast_to(spots[None], (fine_size, bricks, 128))
    sent_features, _ = lax.optimization_barrier((features, spots_out))
    all_spots = lax.all_to_all(spots_out, "fine", 0, 0, tiled=True).reshape(fine_size * bricks, 128)
    features_below = lax.ppermute(sent_features, "coarse", up)
    features_above = lax.ppermute(sent_features, "coarse", down)
    mod = modulation(timestep, time_weight)

    partial_rows = parent_conv(
        place, features, features_below, features_above, mod, all_spots, conv_weight, up_weight
    )
    parts = lax.all_to_all(
        partial_rows.reshape(fine_size, bricks, fine_width), "fine", 0, 0, tiled=True
    )
    sent_cotangent, _ = lax.optimization_barrier((cotangent, partial_rows))
    cot_below = lax.ppermute(sent_cotangent, "coarse", up)
    cot_above = lax.ppermute(sent_cotangent, "coarse", down)

    grad_fine, pack = fine_block(
        fine_features, fine_cotangent, occupancy, parts, spots, mod, inner_weight, outer_weight
    )
    packs = lax.all_to_all(pack, "fine", 0, 0, tiled=True)
    edge_cotangent, _ = lax.optimization_barrier((cotangent, pack))
    first_rows, last_rows = edge_rows(edge_cotangent, cot_below, cot_above)
    row_before = lax.ppermute(last_rows, "fine", row_up)
    row_after = lax.ppermute(first_rows, "fine", row_down)
    sent_packs, _ = lax.optimization_barrier((packs, first_rows))
    packs_below = lax.ppermute(sent_packs, "coarse", up)
    packs_above = lax.ppermute(sent_packs, "coarse", down)
    lift = own_lift(place, packs, up_weight)
    grad_coarse = coarse_grad(
        place, features, cotangent, cot_below, cot_above, row_before, row_after, mod,
        lift, packs_below, packs_above, conv_weight, up_weight
    )
    return (grad_coarse.reshape(coarse_features.shape), grad_fine)


def solution(mesh):
    in_specs = (
        P(("coarse", "fine"), None, None),
        P(("coarse", "fine"), None),
        P(("coarse", "fine")),
        P(),
        P("coarse", "fine", None, None),
        P(),
        P(),
        P(),
        P(),
        P(),
        P("coarse", "fine", None, None),
        P(("coarse", "fine"), None, None),
    )
    out_specs = (P("coarse", "fine", None, None), P(("coarse", "fine"), None, None))
    return jax.shard_map(
        per_device, mesh=mesh, in_specs=in_specs, out_specs=out_specs, check_vma=False
    )
```

```python
import math

import jax
import jax.numpy as jnp
from jax import lax
from jax.experimental import pallas as pl
from jax.experimental.pallas import tpu as pltpu
from jax.sharding import PartitionSpec as P

EPSILON = 1e-06
MIB = 1024 * 1024
F32 = jnp.float32
BF16 = jnp.bfloat16
CHUNK = 64
VMEM = pl.BlockSpec(memory_space=pltpu.VMEM)
SMEM = pl.BlockSpec(memory_space=pltpu.SMEM)
HBM = pl.BlockSpec(memory_space=pltpu.HBM)


def start_copies(pairs, sems):
    copies = [pltpu.make_async_copy(src, dst, sems.at[i]) for i, (src, dst) in enumerate(pairs)]
    for copy in copies:
        copy.start()
    return copies


def sigmoid(values):
    return 0.5 * jnp.tanh(0.5 * values) + 0.5


def silu_slope(values):
    gate = sigmoid(values)
    return gate * (1.0 + values * (1.0 - gate))


def rms_scale(values):
    return lax.rsqrt(jnp.mean(values * values, axis=-1, keepdims=True) + EPSILON)


def modulation(timestep, time_weight):
    half_width = time_weight.shape[0] // 2
    frequency = jnp.exp(-math.log(10000.0) * jnp.arange(half_width, dtype=F32) / half_width)
    angles = timestep.astype(F32)[0] * frequency
    embedded = jnp.concatenate([jnp.sin(angles), jnp.cos(angles)]).astype(BF16)
    return jnp.dot(embedded[None, :], time_weight, preferred_element_type=F32)


def shift_pairs(size):
    up = [(i, i + 1) for i in range(size - 1)]
    return up, [(j, i) for i, j in up]


def near_slots(spots, first_row, valid=True):
    bricks = spots.shape[0]
    spots_t = spots.astype(F32).T
    row_t = spots_t[0:1, :].astype(jnp.int32) - first_row
    near_t = (row_t >= -1) & (row_t <= 4) & valid
    brick_i = lax.broadcasted_iota(jnp.int32, (bricks, bricks), 0)
    brick_j = lax.broadcasted_iota(jnp.int32, (bricks, bricks), 1)
    place_t = jnp.dot(
        jnp.broadcast_to(jnp.where(near_t, 1.0, 0.0), (16, bricks)).astype(BF16),
        jnp.where(brick_i < brick_j, 1.0, 0.0).astype(BF16),
        preferred_element_type=F32,
    )[0:1].astype(jnp.int32)
    count = jnp.sum(jnp.where(near_t, 1.0, 0.0)).astype(jnp.int32)
    return jnp.where(near_t, place_t, -1), count


def tap_cells(pick, spots, first_row, cells):
    found = jnp.dot(pick, spots, preferred_element_type=F32)
    row = found[:, 0:1].astype(jnp.int32) - first_row
    column = found[:, 64:65].astype(jnp.int32)
    lane = lax.broadcasted_iota(jnp.int32, (pick.shape[0], cells), 1)
    onehots = []
    for row_step in (-1, 0, 1):
        for column_step in (-1, 0, 1):
            y, x = row + row_step, column + column_step
            inside = (y >= 0) & (y < 4) & (x >= 0) & (x < 128)
            cell = jnp.where(inside, y * 128 + x, -1)
            onehots.append(jnp.where(lane == cell, 1.0, 0.0).astype(BF16))
    return onehots


def weight_loads(conv_weight, weights, sems, order):
    copies = {}
    for layer in order:
        for part in (3 * layer, 3 * layer + 1, 3 * layer + 2):
            copies[part] = pltpu.make_async_copy(
                conv_weight.at[pl.ds(3 * part, 3)], weights.at[pl.ds(3 * part, 3)], sems.at[part]
            )
            copies[part].start()
    return copies


def hide(values, mod):
    values = values.astype(F32)
    pre = values * rms_scale(values) * (1.0 + mod[0:1, 256:768]) + mod[0:1, 768:1280]
    return pre * sigmoid(pre)


def parent_conv_kernel(
    place, own, below, above, mod, info, conv_weight, up_weight, out, hidden, weights, sems
):
    cells, width = own.shape
    loads = weight_loads(conv_weight, weights, sems, (1, 0, 2))
    bricks = info.shape[0]
    first_row = place[0]
    spots = info[...]
    slots, near_count = near_slots(spots, first_row)
    hidden[1] = hide(own[...], mod).astype(BF16)
    for layer, source in ((0, below), (2, above)):
        hidden[layer] = jnp.where(place[1 + layer // 2] > 0, hide(source[...], mod), 0.0).astype(BF16)

    def one_chunk(chunk, first=False):
        slot = lax.broadcasted_iota(jnp.int32, (CHUNK, bricks), 0) + chunk * CHUNK
        pick = jnp.where(slot == slots, 1.0, 0.0).astype(BF16)
        onehots = tap_cells(pick, spots, first_row, cells)
        onehot = jnp.concatenate(onehots, axis=0)
        total = jnp.dot(onehots[4], own[...], preferred_element_type=F32)
        for layer in (1, 0, 2):
            gathered = jnp.dot(onehot, hidden[layer], preferred_element_type=F32).astype(BF16)
            for corner in range(9):
                if first and corner % 3 == 0:
                    loads[3 * layer + corner // 3].wait()
                total += jnp.dot(
                    gathered[corner * CHUNK : (corner + 1) * CHUNK],
                    weights[9 * layer + corner],
                    preferred_element_type=F32,
                )
        lifted = jnp.dot(total.astype(BF16), up_weight[...], preferred_element_type=F32)
        high = lifted.astype(BF16)
        low = (lifted - high.astype(F32)).astype(BF16)
        across = (((0,), (0,)), ((), ()))
        return lax.dot_general(pick, high, across, preferred_element_type=F32) + lax.dot_general(
            pick, low, across, preferred_element_type=F32
        )

    out[...] = one_chunk(0, True)

    @pl.loop(1, (near_count + CHUNK - 1) // CHUNK)
    def _(chunk):
        out[...] += one_chunk(chunk)


def parent_conv(place, own, below, above, mod, info, conv_weight, up_weight):
    return pl.pallas_call(
        parent_conv_kernel,
        out_shape=jax.ShapeDtypeStruct((info.shape[0], up_weight.shape[1]), F32),
        in_specs=[SMEM] + [VMEM] * 5 + [pl.BlockSpec(memory_space=pl.ANY), VMEM],
        out_specs=VMEM,
        scratch_shapes=[
            pltpu.VMEM((3,) + own.shape, BF16),
            pltpu.VMEM(conv_weight.shape, BF16),
            pltpu.SemaphoreType.DMA((9,)),
        ],
        compiler_params=pltpu.CompilerParams(vmem_limit_bytes=41 * MIB),
        cost_estimate=pl.CostEstimate(flops=2 * 128 * 27 * 512 * 512, bytes_accessed=16 * MIB, transcendentals=0),
        name="parent_conv",
    )(place, own, below, above, mod, info, conv_weight, up_weight)


def fine_kernel(
    features, cotangent, occupied, parts, spots, mod, inner_weight, outer_weight,
    grads, pack, spread, sums, inner_pair, outer_pair,
):
    step = pl.program_id(0)
    bricks = occupied.shape[0]

    @pl.when(step == 0)
    def _():
        spread[...] = occupied[...].astype(F32).T.astype(BF16)
        for pair, weight in ((inner_pair, inner_weight), (outer_pair, outer_weight)):
            pair[...] = jnp.zeros((256, 256), BF16)
            pair[0:128, 0:128] = weight[...]
            pair[128:256, 128:256] = weight[...]

    def beside(left, right):
        return jnp.concatenate([left, right], axis=1)

    def mean(values):
        rows = values.shape[0]
        return beside(
            jnp.broadcast_to(jnp.mean(values[:, 0:128], -1, keepdims=True), (rows, 128)),
            jnp.broadcast_to(jnp.mean(values[:, 128:256], -1, keepdims=True), (rows, 128)),
        )

    scale = 1.0 + beside(mod[0:1, 0:128], mod[0:1, 0:128])
    shift = beside(mod[0:1, 128:256], mod[0:1, 128:256])
    transposed = (((1,), (1,)), ((), ()))
    side = lax.broadcasted_iota(jnp.int32, (bricks, 256), 1) // 128
    for item in range(0, features.shape[0], 2):
        brick = step * features.shape[0] + item
        pick = jnp.where(lax.broadcasted_iota(jnp.int32, (bricks, 256), 0) == brick + side, 1.0, 0.0).astype(BF16)
        mask = jnp.dot(spread[...], pick, preferred_element_type=F32)
        lifted = beside(
            jnp.sum(parts[:, pl.ds(brick, 1), :], axis=0), jnp.sum(parts[:, pl.ds(brick + 1, 1), :], axis=0)
        ).astype(BF16).astype(F32)
        fine_in = beside(features[item], features[item + 1]).astype(F32) + lifted
        fine_scale = lax.rsqrt(mean(fine_in * fine_in) + EPSILON)
        normed = fine_in * fine_scale
        pre = normed * scale + shift
        gate = sigmoid(pre)
        act = pre * gate
        slope = gate + act * (1.0 - gate)
        inner_pre = jnp.dot(act.astype(BF16), inner_pair[...], preferred_element_type=F32)
        masked = beside(cotangent[item], cotangent[item + 1]).astype(F32) * mask
        grad_hidden = lax.dot_general(masked.astype(BF16), outer_pair[...], transposed, preferred_element_type=F32)
        grad_inner = (grad_hidden * silu_slope(inner_pre)).astype(BF16)
        grad_act = lax.dot_general(grad_inner, inner_pair[...], transposed, preferred_element_type=F32)
        grad_norm = grad_act * slope * scale
        grad_in = masked + fine_scale * (grad_norm - normed * mean(grad_norm * normed))
        rounded = grad_in.astype(BF16)
        grads[item] = rounded[:, 0:128]
        grads[item + 1] = rounded[:, 128:256]
        total = jnp.sum(grad_in, axis=0, keepdims=True)
        sums[pl.ds(brick, 1), :] = total[:, 0:128]
        sums[pl.ds(brick + 1, 1), :] = total[:, 128:256]

    @pl.when(step == pl.num_programs(0) - 1)
    def _():
        total = sums[...].astype(BF16)
        for target in range(pack.shape[0]):
            pack[target, 0:bricks] = total
            pack[target, bricks : 2 * bricks] = spots[...]


def fine_block(features, cotangent, occupied, parts, spots, mod, inner_weight, outer_weight):
    bricks, voxels, width = features.shape
    per_step = 4
    block = pl.BlockSpec((per_step, voxels, width), lambda i: (i, 0, 0))

    def whole(shape):
        return pl.BlockSpec(shape, lambda i: (0,) * len(shape))

    pack_shape = (parts.shape[0], 2 * bricks, width)
    fixed = (occupied, parts, spots, mod, inner_weight, outer_weight)
    return pl.pallas_call(
        fine_kernel,
        grid=(bricks // per_step,),
        out_shape=(
            jax.ShapeDtypeStruct(features.shape, BF16),
            jax.ShapeDtypeStruct(pack_shape, BF16),
        ),
        in_specs=[block, block] + [whole(array.shape) for array in fixed],
        out_specs=(block, whole(pack_shape)),
        scratch_shapes=[
            pltpu.VMEM((voxels, bricks), BF16),
            pltpu.VMEM((bricks, width), F32),
            pltpu.VMEM((256, 256), BF16),
            pltpu.VMEM((256, 256), BF16),
        ],
        compiler_params=pltpu.CompilerParams(vmem_limit_bytes=58 * MIB),
        cost_estimate=pl.CostEstimate(flops=3 * 10**10, bytes_accessed=6 * MIB, transcendentals=2**21),
        name="fine_block",
    )(features, cotangent, *fixed)


def edge_rows_kernel(own, below, above, first, last, sems):
    cells = own.shape[0]
    pairs = []
    for layer, source in enumerate((below, own, above)):
        pairs.append((source.at[pl.ds(0, 128)], first.at[layer]))
        pairs.append((source.at[pl.ds(cells - 128, 128)], last.at[layer]))
    for copy in start_copies(pairs, sems):
        copy.wait()


def edge_rows(own, below, above):
    shape = jax.ShapeDtypeStruct((3, 128, own.shape[1]), BF16)
    return pl.pallas_call(
        edge_rows_kernel,
        out_shape=(shape, shape),
        in_specs=[pl.BlockSpec(memory_space=pl.ANY)] * 3,
        out_specs=(VMEM, VMEM),
        scratch_shapes=[pltpu.SemaphoreType.DMA((6,))],
        cost_estimate=pl.CostEstimate(flops=0, bytes_accessed=2 * MIB, transcendentals=0),
        name="edge_rows",
    )(own, below, above)


def cell_lift(pack, up_weight, first_row):
    spots_t = pack[:, 16:32, :].reshape(256, 128).astype(F32).T
    row = spots_t[0:1, :].astype(jnp.int32) - first_row + 1
    column = spots_t[64:65, :].astype(jnp.int32)
    onehot = jnp.where(
        lax.broadcasted_iota(jnp.int32, (6 * 128, 256), 0) == row * 128 + column, 1.0, 0.0
    ).astype(BF16)
    cell_sums = jnp.dot(onehot, pack[:, 0:16, :].reshape(256, 128), preferred_element_type=F32).astype(BF16)
    return lax.dot_general(cell_sums, up_weight, (((1,), (1,)), ((), ())), preferred_element_type=F32)


def own_lift_kernel(place, packs, up_hbm, lift, up_weight, sems):
    (copy,) = start_copies([(up_hbm, up_weight)], sems)
    copy.wait()
    lift[...] = cell_lift(packs, up_weight[...], place[0])


def own_lift(place, packs, up_weight):
    width = up_weight.shape[0]
    return pl.pallas_call(
        own_lift_kernel,
        out_shape=jax.ShapeDtypeStruct((6 * 128, width), F32),
        in_specs=[SMEM, VMEM, pl.BlockSpec(memory_space=pl.ANY)],
        out_specs=VMEM,
        scratch_shapes=[pltpu.VMEM(up_weight.shape, BF16), pltpu.SemaphoreType.DMA((1,))],
        compiler_params=pltpu.CompilerParams(vmem_limit_bytes=40 * MIB),
        cost_estimate=pl.CostEstimate(flops=10**8, bytes_accessed=2 * MIB, transcendentals=0),
        name="own_lift",
    )(place, packs, up_weight)


def coarse_grad_kernel(
    place, features, own, below, above, row_before, row_after, mod, lift, packs_below, packs_above, conv_weight,
    up_weight, out, grad, center, total, weights, sems,
):
    cells, width = own.shape
    loads = weight_loads(conv_weight, weights, sems, (1, 2, 0))
    first = True
    for layer, source in ((1, own), (0, below), (2, above)):
        if layer == 1:
            added = lift[...]
        else:
            added = cell_lift(packs_below if layer == 0 else packs_above, up_weight[...], place[0])
        middle = added[128:640] + source[...].astype(F32)
        if layer == 1:
            center[...] = middle
        grad[layer, 0:128] = (added[0:128] + row_before[layer].astype(F32)).astype(BF16)
        grad[layer, 128:640] = middle.astype(BF16)
        grad[layer, 640:768] = (added[640:768] + row_after[layer].astype(F32)).astype(BF16)
        for row_step in range(3):
            loads[3 * (2 - layer) + row_step].wait()
            begin = (2 - row_step) * 128
            block = grad[layer, begin : begin + cells]
            for column_step in range(3):
                piece = lax.dot_general(
                    block,
                    weights[9 * (2 - layer) + 3 * row_step + column_step],
                    (((1,), (1,)), ((), ())),
                    preferred_element_type=F32,
                )
                if first and row_step == 0:
                    total[column_step] = piece
                else:
                    total[column_step] += piece
        first = False
    column = lax.broadcasted_iota(jnp.int32, (cells, 1), 0) % 128
    left = jnp.where(column == 127, 0.0, pltpu.roll(total[0], cells - 1, 0))
    right = jnp.where(column == 0, 0.0, pltpu.roll(total[2], 1, 0))
    grad_conv = total[1] + left + right
    scale = 1.0 + mod[0:1, 256:768]
    shift = mod[0:1, 768:1280]
    values = features[...].astype(F32)
    coarse_scale = rms_scale(values)
    normed = values * coarse_scale
    grad_cn = grad_conv * silu_slope(normed * scale + shift) * scale
    inner = jnp.mean(grad_cn * normed, axis=-1, keepdims=True)
    out[...] = (center[...] + coarse_scale * (grad_cn - normed * inner)).astype(BF16)


def coarse_grad(
    place, features, own, below, above, row_before, row_after, mod, lift, packs_below, packs_above, conv_weight, up_weight
):
    cells, width = features.shape
    return pl.pallas_call(
        coarse_grad_kernel,
        out_shape=jax.ShapeDtypeStruct((cells, width), BF16),
        in_specs=[SMEM] + [VMEM] * 10 + [pl.BlockSpec(memory_space=pl.ANY), VMEM],
        out_specs=VMEM,
        scratch_shapes=[
            pltpu.VMEM((3, 6 * 128, width), BF16),
            pltpu.VMEM((cells, width), F32),
            pltpu.VMEM((3, cells, width), F32),
            pltpu.VMEM(conv_weight.shape, BF16),
            pltpu.SemaphoreType.DMA((9,)),
        ],
        compiler_params=pltpu.CompilerParams(vmem_limit_bytes=48 * MIB),
        cost_estimate=pl.CostEstimate(flops=2 * 512 * 27 * 512 * 512, bytes_accessed=18 * MIB, transcendentals=0),
        name="coarse_grad",
    )(place, features, own, below, above, row_before, row_after, mod, lift, packs_below, packs_above, conv_weight, up_weight)


def per_device(
    fine_features,
    occupancy,
    parent,
    timestep,
    coarse_features,
    time_weight,
    conv_weight,
    up_weight,
    inner_weight,
    outer_weight,
    coarse_cotangent,
    fine_cotangent,
):
    layer_count, row_count, column_count, width = coarse_features.shape
    fine_width = up_weight.shape[1]
    bricks = parent.shape[0]
    fine_size, coarse_size = lax.axis_size("fine"), lax.axis_size("coarse")
    coarse_index, fine_index = lax.axis_index("coarse"), lax.axis_index("fine")
    cells = layer_count * row_count * column_count
    up, down = shift_pairs(coarse_size)
    row_up, row_down = shift_pairs(fine_size)

    local = parent - coarse_index * (cells * fine_size)
    row, column = local // column_count, local % column_count
    lane = jnp.arange(128)[None, :]
    spots = jnp.where(lane < 64, row[:, None], column[:, None]).astype(BF16)
    place = jnp.stack(
        [fine_index * row_count, (coarse_index > 0).astype(jnp.int32), (coarse_index < coarse_size - 1).astype(jnp.int32)]
    ).astype(jnp.int32)

    features = coarse_features.reshape(cells, width)
    cotangent = coarse_cotangent.reshape(cells, width)
    spots_out = jnp.broadcast_to(spots[None], (fine_size, bricks, 128))
    all_spots = lax.all_to_all(spots_out, "fine", 0, 0, tiled=True).reshape(fine_size * bricks, 128)
    features_below = lax.ppermute(features, "coarse", up)
    features_above = lax.ppermute(features, "coarse", down)
    sent_cotangent, _ = lax.optimization_barrier((cotangent, all_spots))
    cot_below = lax.ppermute(sent_cotangent, "coarse", up)
    cot_above = lax.ppermute(sent_cotangent, "coarse", down)
    mod = modulation(timestep, time_weight)

    partial_rows = parent_conv(
        place, features, features_below, features_above, mod, all_spots, conv_weight, up_weight
    )
    parts = lax.all_to_all(
        partial_rows.reshape(fine_size, bricks, fine_width), "fine", 0, 0, tiled=True
    )
    edge_cotangent, _ = lax.optimization_barrier((cotangent, partial_rows))
    first_rows, last_rows = edge_rows(edge_cotangent, cot_below, cot_above)
    row_before = lax.ppermute(last_rows, "fine", row_up)
    row_after = lax.ppermute(first_rows, "fine", row_down)

    parts, _ = lax.optimization_barrier((parts, first_rows))
    grad_fine, pack = fine_block(
        fine_features, fine_cotangent, occupancy, parts, spots, mod, inner_weight, outer_weight
    )
    packs = lax.all_to_all(pack, "fine", 0, 0, tiled=True)
    packs_below = lax.ppermute(packs, "coarse", up)
    packs_above = lax.ppermute(packs, "coarse", down)
    lift = own_lift(place, packs, up_weight)
    grad_coarse = coarse_grad(
        place, features, cotangent, cot_below, cot_above, row_before, row_after, mod,
        lift, packs_below, packs_above, conv_weight, up_weight
    )
    return (grad_coarse.reshape(coarse_features.shape), grad_fine)


def solution(mesh):
    in_specs = (
        P(("coarse", "fine"), None, None),
        P(("coarse", "fine"), None),
        P(("coarse", "fine")),
        P(),
        P("coarse", "fine", None, None),
        P(),
        P(),
        P(),
        P(),
        P(),
        P("coarse", "fine", None, None),
        P(("coarse", "fine"), None, None),
    )
    out_specs = (P("coarse", "fine", None, None), P(("coarse", "fine"), None, None))
    return jax.shard_map(
        per_device, mesh=mesh, in_specs=in_specs, out_specs=out_specs, check_vma=False
    )
```

```python
import math

import jax
import jax.numpy as jnp
from jax import lax
from jax.experimental import pallas as pl
from jax.experimental.pallas import tpu as pltpu
from jax.sharding import PartitionSpec as P

EPSILON = 1e-06
MIB = 1024 * 1024
F32 = jnp.float32
BF16 = jnp.bfloat16
CHUNK = 64
VMEM = pl.BlockSpec(memory_space=pltpu.VMEM)
SMEM = pl.BlockSpec(memory_space=pltpu.SMEM)
HBM = pl.BlockSpec(memory_space=pltpu.HBM)


def start_copies(pairs, sems):
    copies = [pltpu.make_async_copy(src, dst, sems.at[i]) for i, (src, dst) in enumerate(pairs)]
    for copy in copies:
        copy.start()
    return copies


def sigmoid(values):
    return 0.5 * jnp.tanh(0.5 * values) + 0.5


def silu_slope(values):
    gate = sigmoid(values)
    return gate * (1.0 + values * (1.0 - gate))


def rms_scale(values):
    return lax.rsqrt(jnp.mean(values * values, axis=-1, keepdims=True) + EPSILON)


def modulation(timestep, time_weight):
    half_width = time_weight.shape[0] // 2
    frequency = jnp.exp(-math.log(10000.0) * jnp.arange(half_width, dtype=F32) / half_width)
    angles = timestep.astype(F32)[0] * frequency
    embedded = jnp.concatenate([jnp.sin(angles), jnp.cos(angles)]).astype(BF16)
    return jnp.dot(embedded[None, :], time_weight, preferred_element_type=F32)


def shift_pairs(size):
    up = [(i, i + 1) for i in range(size - 1)]
    return up, [(j, i) for i, j in up]


def near_slots(spots, first_row, valid=True):
    bricks = spots.shape[0]
    spots_t = spots.astype(F32).T
    row_t = spots_t[0:1, :].astype(jnp.int32) - first_row
    near_t = (row_t >= -1) & (row_t <= 4) & valid
    brick_i = lax.broadcasted_iota(jnp.int32, (bricks, bricks), 0)
    brick_j = lax.broadcasted_iota(jnp.int32, (bricks, bricks), 1)
    place_t = jnp.dot(
        jnp.broadcast_to(jnp.where(near_t, 1.0, 0.0), (16, bricks)).astype(BF16),
        jnp.where(brick_i < brick_j, 1.0, 0.0).astype(BF16),
        preferred_element_type=F32,
    )[0:1].astype(jnp.int32)
    count = jnp.sum(jnp.where(near_t, 1.0, 0.0)).astype(jnp.int32)
    return jnp.where(near_t, place_t, -1), count


def tap_cells(pick, spots, first_row, cells):
    found = jnp.dot(pick, spots, preferred_element_type=F32)
    row = found[:, 0:1].astype(jnp.int32) - first_row
    column = found[:, 64:65].astype(jnp.int32)
    lane = lax.broadcasted_iota(jnp.int32, (pick.shape[0], cells), 1)
    onehots = []
    for row_step in (-1, 0, 1):
        for column_step in (-1, 0, 1):
            y, x = row + row_step, column + column_step
            inside = (y >= 0) & (y < 4) & (x >= 0) & (x < 128)
            cell = jnp.where(inside, y * 128 + x, -1)
            onehots.append(jnp.where(lane == cell, 1.0, 0.0).astype(BF16))
    return onehots


def weight_loads(conv_weight, weights, sems, order):
    copies = {}
    for layer in order:
        for part in (3 * layer, 3 * layer + 1, 3 * layer + 2):
            copies[part] = pltpu.make_async_copy(
                conv_weight.at[pl.ds(3 * part, 3)], weights.at[pl.ds(3 * part, 3)], sems.at[part]
            )
            copies[part].start()
    return copies


def parent_conv_kernel(
    place, own_hbm, below_hbm, above_hbm, mod, info, conv_weight, up_hbm,
    out, cells_in, hidden, weights, up_weight, sems, tap_sems,
):
    cells, width = own_hbm.shape
    bricks = info.shape[0]
    taps = conv_weight.shape[0]
    sources = (below_hbm, own_hbm, above_hbm)
    copies = start_copies(
        [(source, cells_in.at[layer]) for layer, source in enumerate(sources)] + [(up_hbm, up_weight)], sems
    )
    loads = start_copies([(conv_weight.at[tap], weights.at[tap]) for tap in range(taps)], tap_sems)
    first_row = place[0]
    spots = info[...]
    slots, near_count = near_slots(spots, first_row)
    scale = 1.0 + mod[0:1, 256:768]
    shift = mod[0:1, 768:1280]
    for layer in range(3):
        copies[layer].wait()
        values = cells_in[layer].astype(F32)
        pre = values * rms_scale(values) * scale + shift
        act = pre * sigmoid(pre)
        if layer != 1:
            act = jnp.where(place[1 + layer // 2] > 0, act, 0.0)
        hidden[layer] = act.astype(BF16)
    copies[3].wait()

    def one_chunk(chunk, first=False):
        slot = lax.broadcasted_iota(jnp.int32, (CHUNK, bricks), 0) + chunk * CHUNK
        pick = jnp.where(slot == slots, 1.0, 0.0).astype(BF16)
        onehots = tap_cells(pick, spots, first_row, cells)
        onehot = jnp.concatenate(onehots, axis=0)
        total = jnp.dot(onehots[4], cells_in[1], preferred_element_type=F32)
        for layer in range(3):
            gathered = jnp.dot(onehot, hidden[layer], preferred_element_type=F32).astype(BF16)
            for corner in range(9):
                tap = 9 * layer + corner
                if first:
                    loads[tap].wait()
                total += jnp.dot(
                    gathered[corner * CHUNK : (corner + 1) * CHUNK],
                    weights[tap],
                    preferred_element_type=F32,
                )
        lifted = jnp.dot(total.astype(BF16), up_weight[...], preferred_element_type=F32)
        high = lifted.astype(BF16)
        low = (lifted - high.astype(F32)).astype(BF16)
        across = (((0,), (0,)), ((), ()))
        return lax.dot_general(pick, high, across, preferred_element_type=F32) + lax.dot_general(
            pick, low, across, preferred_element_type=F32
        )

    out[...] = one_chunk(0, True)

    @pl.loop(1, (near_count + CHUNK - 1) // CHUNK)
    def _(chunk):
        out[...] += one_chunk(chunk)


def parent_conv(place, own, below, above, mod, info, conv_weight, up_weight):
    taps = conv_weight.shape[0]
    return pl.pallas_call(
        parent_conv_kernel,
        out_shape=jax.ShapeDtypeStruct((info.shape[0], up_weight.shape[1]), F32),
        in_specs=[SMEM] + [pl.BlockSpec(memory_space=pl.ANY)] * 3 + [VMEM, VMEM] + [pl.BlockSpec(memory_space=pl.ANY)] * 2,
        out_specs=VMEM,
        scratch_shapes=[
            pltpu.VMEM((3,) + own.shape, BF16),
            pltpu.VMEM((3,) + own.shape, BF16),
            pltpu.VMEM(conv_weight.shape, BF16),
            pltpu.VMEM(up_weight.shape, BF16),
            pltpu.SemaphoreType.DMA((4,)),
            pltpu.SemaphoreType.DMA((taps,)),
        ],
        compiler_params=pltpu.CompilerParams(vmem_limit_bytes=62 * MIB),
        cost_estimate=pl.CostEstimate(flops=2 * 128 * 27 * 512 * 512, bytes_accessed=16 * MIB, transcendentals=0),
        name="parent_conv",
    )(place, own, below, above, mod, info, conv_weight, up_weight)


def fine_kernel(
    features, cotangent, occupied, parts, spots, mod, inner_weight, outer_weight,
    grads, pack, spread, sums, inner_pair, outer_pair,
):
    step = pl.program_id(0)
    bricks = occupied.shape[0]

    @pl.when(step == 0)
    def _():
        spread[...] = occupied[...].astype(F32).T.astype(BF16)
        for pair, weight in ((inner_pair, inner_weight), (outer_pair, outer_weight)):
            pair[...] = jnp.zeros((256, 256), BF16)
            pair[0:128, 0:128] = weight[...]
            pair[128:256, 128:256] = weight[...]

    def beside(left, right):
        return jnp.concatenate([left, right], axis=1)

    def mean(values):
        rows = values.shape[0]
        return beside(
            jnp.broadcast_to(jnp.mean(values[:, 0:128], -1, keepdims=True), (rows, 128)),
            jnp.broadcast_to(jnp.mean(values[:, 128:256], -1, keepdims=True), (rows, 128)),
        )

    scale = 1.0 + beside(mod[0:1, 0:128], mod[0:1, 0:128])
    shift = beside(mod[0:1, 128:256], mod[0:1, 128:256])
    transposed = (((1,), (1,)), ((), ()))
    side = lax.broadcasted_iota(jnp.int32, (bricks, 256), 1) // 128
    for item in range(0, features.shape[0], 2):
        brick = step * features.shape[0] + item
        pick = jnp.where(lax.broadcasted_iota(jnp.int32, (bricks, 256), 0) == brick + side, 1.0, 0.0).astype(BF16)
        mask = jnp.dot(spread[...], pick, preferred_element_type=F32)
        lifted = beside(
            jnp.sum(parts[:, pl.ds(brick, 1), :], axis=0), jnp.sum(parts[:, pl.ds(brick + 1, 1), :], axis=0)
        ).astype(BF16).astype(F32)
        fine_in = beside(features[item], features[item + 1]).astype(F32) + lifted
        fine_scale = lax.rsqrt(mean(fine_in * fine_in) + EPSILON)
        normed = fine_in * fine_scale
        pre = normed * scale + shift
        gate = sigmoid(pre)
        act = pre * gate
        slope = gate + act * (1.0 - gate)
        inner_pre = jnp.dot(act.astype(BF16), inner_pair[...], preferred_element_type=F32)
        masked = beside(cotangent[item], cotangent[item + 1]).astype(F32) * mask
        grad_hidden = lax.dot_general(masked.astype(BF16), outer_pair[...], transposed, preferred_element_type=F32)
        grad_inner = (grad_hidden * silu_slope(inner_pre)).astype(BF16)
        grad_act = lax.dot_general(grad_inner, inner_pair[...], transposed, preferred_element_type=F32)
        grad_norm = grad_act * slope * scale
        grad_in = masked + fine_scale * (grad_norm - normed * mean(grad_norm * normed))
        rounded = grad_in.astype(BF16)
        grads[item] = rounded[:, 0:128]
        grads[item + 1] = rounded[:, 128:256]
        total = jnp.sum(grad_in, axis=0, keepdims=True)
        sums[pl.ds(brick, 1), :] = total[:, 0:128]
        sums[pl.ds(brick + 1, 1), :] = total[:, 128:256]

    @pl.when(step == pl.num_programs(0) - 1)
    def _():
        total = sums[...].astype(BF16)
        for target in range(pack.shape[0]):
            pack[target, 0:bricks] = total
            pack[target, bricks : 2 * bricks] = spots[...]


def fine_block(features, cotangent, occupied, parts, spots, mod, inner_weight, outer_weight):
    bricks, voxels, width = features.shape
    per_step = 4
    block = pl.BlockSpec((per_step, voxels, width), lambda i: (i, 0, 0))

    def whole(shape):
        return pl.BlockSpec(shape, lambda i: (0,) * len(shape))

    pack_shape = (parts.shape[0], 2 * bricks, width)
    fixed = (occupied, parts, spots, mod, inner_weight, outer_weight)
    return pl.pallas_call(
        fine_kernel,
        grid=(bricks // per_step,),
        out_shape=(
            jax.ShapeDtypeStruct(features.shape, BF16),
            jax.ShapeDtypeStruct(pack_shape, BF16),
        ),
        in_specs=[block, block] + [whole(array.shape) for array in fixed],
        out_specs=(block, whole(pack_shape)),
        scratch_shapes=[
            pltpu.VMEM((voxels, bricks), BF16),
            pltpu.VMEM((bricks, width), F32),
            pltpu.VMEM((256, 256), BF16),
            pltpu.VMEM((256, 256), BF16),
        ],
        compiler_params=pltpu.CompilerParams(vmem_limit_bytes=57 * MIB),
        cost_estimate=pl.CostEstimate(flops=3 * 10**10, bytes_accessed=6 * MIB, transcendentals=2**21),
        name="fine_block",
    )(features, cotangent, *fixed)


def edge_rows_kernel(own, below, above, first, last, sems):
    cells = own.shape[0]
    pairs = []
    for layer, source in enumerate((below, own, above)):
        pairs.append((source.at[pl.ds(0, 128)], first.at[layer]))
        pairs.append((source.at[pl.ds(cells - 128, 128)], last.at[layer]))
    for copy in start_copies(pairs, sems):
        copy.wait()


def edge_rows(own, below, above):
    shape = jax.ShapeDtypeStruct((3, 128, own.shape[1]), BF16)
    return pl.pallas_call(
        edge_rows_kernel,
        out_shape=(shape, shape),
        in_specs=[pl.BlockSpec(memory_space=pl.ANY)] * 3,
        out_specs=(VMEM, VMEM),
        scratch_shapes=[pltpu.SemaphoreType.DMA((6,))],
        cost_estimate=pl.CostEstimate(flops=0, bytes_accessed=2 * MIB, transcendentals=0),
        name="edge_rows",
    )(own, below, above)


def cell_lift(pack, up_weight, first_row):
    spots_t = pack[:, 16:32, :].reshape(256, 128).astype(F32).T
    row = spots_t[0:1, :].astype(jnp.int32) - first_row + 1
    column = spots_t[64:65, :].astype(jnp.int32)
    onehot = jnp.where(
        lax.broadcasted_iota(jnp.int32, (6 * 128, 256), 0) == row * 128 + column, 1.0, 0.0
    ).astype(BF16)
    cell_sums = jnp.dot(onehot, pack[:, 0:16, :].reshape(256, 128), preferred_element_type=F32).astype(BF16)
    return lax.dot_general(cell_sums, up_weight, (((1,), (1,)), ((), ())), preferred_element_type=F32)


def own_lift_kernel(place, packs, up_hbm, lift, up_weight, sems):
    (copy,) = start_copies([(up_hbm, up_weight)], sems)
    copy.wait()
    lift[...] = cell_lift(packs, up_weight[...], place[0])


def own_lift(place, packs, up_weight):
    width = up_weight.shape[0]
    return pl.pallas_call(
        own_lift_kernel,
        out_shape=jax.ShapeDtypeStruct((6 * 128, width), F32),
        in_specs=[SMEM, VMEM, pl.BlockSpec(memory_space=pl.ANY)],
        out_specs=VMEM,
        scratch_shapes=[pltpu.VMEM(up_weight.shape, BF16), pltpu.SemaphoreType.DMA((1,))],
        compiler_params=pltpu.CompilerParams(vmem_limit_bytes=40 * MIB),
        cost_estimate=pl.CostEstimate(flops=3 * 10**10, bytes_accessed=2 * MIB, transcendentals=0),
        name="own_lift",
    )(place, packs, up_weight)


def coarse_grad_kernel(
    place, features, own, below, above, row_before, row_after, mod, lift, packs_below, packs_above, conv_weight,
    up_weight, out, grad, center, total, weights, sems,
):
    cells, width = own.shape
    loads = weight_loads(conv_weight, weights, sems, (1, 2, 0))
    first = True
    for layer, source in ((1, own), (0, below), (2, above)):
        if layer == 1:
            added = lift[...]
        else:
            added = cell_lift(packs_below if layer == 0 else packs_above, up_weight[...], place[0])
        middle = added[128:640] + source[...].astype(F32)
        if layer == 1:
            center[...] = middle
        grad[layer, 0:128] = (added[0:128] + row_before[layer].astype(F32)).astype(BF16)
        grad[layer, 128:640] = middle.astype(BF16)
        grad[layer, 640:768] = (added[640:768] + row_after[layer].astype(F32)).astype(BF16)
        for row_step in range(3):
            loads[3 * (2 - layer) + row_step].wait()
            begin = (2 - row_step) * 128
            block = grad[layer, begin : begin + cells]
            for column_step in range(3):
                piece = lax.dot_general(
                    block,
                    weights[9 * (2 - layer) + 3 * row_step + column_step],
                    (((1,), (1,)), ((), ())),
                    preferred_element_type=F32,
                )
                if first and row_step == 0:
                    total[column_step] = piece
                else:
                    total[column_step] += piece
        first = False
    column = lax.broadcasted_iota(jnp.int32, (cells, 1), 0) % 128
    left = jnp.where(column == 127, 0.0, pltpu.roll(total[0], cells - 1, 0))
    right = jnp.where(column == 0, 0.0, pltpu.roll(total[2], 1, 0))
    grad_conv = total[1] + left + right
    scale = 1.0 + mod[0:1, 256:768]
    shift = mod[0:1, 768:1280]
    values = features[...].astype(F32)
    coarse_scale = rms_scale(values)
    normed = values * coarse_scale
    grad_cn = grad_conv * silu_slope(normed * scale + shift) * scale
    inner = jnp.mean(grad_cn * normed, axis=-1, keepdims=True)
    out[...] = (center[...] + coarse_scale * (grad_cn - normed * inner)).astype(BF16)


def coarse_grad(
    place, features, own, below, above, row_before, row_after, mod, lift, packs_below, packs_above, conv_weight, up_weight
):
    cells, width = features.shape
    return pl.pallas_call(
        coarse_grad_kernel,
        out_shape=jax.ShapeDtypeStruct((cells, width), BF16),
        in_specs=[SMEM] + [VMEM] * 10 + [pl.BlockSpec(memory_space=pl.ANY), VMEM],
        out_specs=VMEM,
        scratch_shapes=[
            pltpu.VMEM((3, 6 * 128, width), BF16),
            pltpu.VMEM((cells, width), F32),
            pltpu.VMEM((3, cells, width), F32),
            pltpu.VMEM(conv_weight.shape, BF16),
            pltpu.SemaphoreType.DMA((9,)),
        ],
        compiler_params=pltpu.CompilerParams(vmem_limit_bytes=48 * MIB),
        cost_estimate=pl.CostEstimate(flops=2 * 512 * 27 * 512 * 512, bytes_accessed=18 * MIB, transcendentals=0),
        name="coarse_grad",
    )(place, features, own, below, above, row_before, row_after, mod, lift, packs_below, packs_above, conv_weight, up_weight)


def per_device(
    fine_features,
    occupancy,
    parent,
    timestep,
    coarse_features,
    time_weight,
    conv_weight,
    up_weight,
    inner_weight,
    outer_weight,
    coarse_cotangent,
    fine_cotangent,
):
    layer_count, row_count, column_count, width = coarse_features.shape
    fine_width = up_weight.shape[1]
    bricks = parent.shape[0]
    fine_size, coarse_size = lax.axis_size("fine"), lax.axis_size("coarse")
    coarse_index, fine_index = lax.axis_index("coarse"), lax.axis_index("fine")
    cells = layer_count * row_count * column_count
    up, down = shift_pairs(coarse_size)
    row_up, row_down = shift_pairs(fine_size)

    local = parent - coarse_index * (cells * fine_size)
    row, column = local // column_count, local % column_count
    lane = jnp.arange(128)[None, :]
    spots = jnp.where(lane < 64, row[:, None], column[:, None]).astype(BF16)
    place = jnp.stack(
        [fine_index * row_count, (coarse_index > 0).astype(jnp.int32), (coarse_index < coarse_size - 1).astype(jnp.int32)]
    ).astype(jnp.int32)

    features = coarse_features.reshape(cells, width)
    cotangent = coarse_cotangent.reshape(cells, width)
    spots_out = jnp.broadcast_to(spots[None], (fine_size, bricks, 128))
    all_spots = lax.all_to_all(spots_out, "fine", 0, 0, tiled=True).reshape(fine_size * bricks, 128)
    sent_features, _ = lax.optimization_barrier((features, spots_out))
    features_below = lax.ppermute(sent_features, "coarse", up)
    features_above = lax.ppermute(sent_features, "coarse", down)
    sent_cotangent, _ = lax.optimization_barrier((cotangent, all_spots))
    cot_below = lax.ppermute(sent_cotangent, "coarse", up)
    cot_above = lax.ppermute(sent_cotangent, "coarse", down)
    mod = modulation(timestep, time_weight)

    partial_rows = parent_conv(
        place, features, features_below, features_above, mod, all_spots, conv_weight, up_weight
    )
    parts = lax.all_to_all(
        partial_rows.reshape(fine_size, bricks, fine_width), "fine", 0, 0, tiled=True
    )
    edge_cotangent, _ = lax.optimization_barrier((cotangent, partial_rows))
    first_rows, last_rows = edge_rows(edge_cotangent, cot_below, cot_above)
    row_before = lax.ppermute(last_rows, "fine", row_up)
    row_after = lax.ppermute(first_rows, "fine", row_down)

    parts, _ = lax.optimization_barrier((parts, first_rows))
    grad_fine, pack = fine_block(
        fine_features, fine_cotangent, occupancy, parts, spots, mod, inner_weight, outer_weight
    )
    packs = lax.all_to_all(pack, "fine", 0, 0, tiled=True)
    packs_below = lax.ppermute(packs, "coarse", up)
    packs_above = lax.ppermute(packs, "coarse", down)
    lift = own_lift(place, packs, up_weight)
    grad_coarse = coarse_grad(
        place, features, cotangent, cot_below, cot_above, row_before, row_after, mod,
        lift, packs_below, packs_above, conv_weight, up_weight
    )
    return (grad_coarse.reshape(coarse_features.shape), grad_fine)


def solution(mesh):
    in_specs = (
        P(("coarse", "fine"), None, None),
        P(("coarse", "fine"), None),
        P(("coarse", "fine")),
        P(),
        P("coarse", "fine", None, None),
        P(),
        P(),
        P(),
        P(),
        P(),
        P("coarse", "fine", None, None),
        P(("coarse", "fine"), None, None),
    )
    out_specs = (P("coarse", "fine", None, None), P(("coarse", "fine"), None, None))
    return jax.shard_map(
        per_device, mesh=mesh, in_specs=in_specs, out_specs=out_specs, check_vma=False
    )
```

```python
import math

import jax
import jax.numpy as jnp
from jax import lax
from jax.experimental import pallas as pl
from jax.experimental.pallas import tpu as pltpu
from jax.sharding import PartitionSpec as P

EPSILON = 1e-06
MIB = 1024 * 1024
F32 = jnp.float32
BF16 = jnp.bfloat16
CHUNK = 64
VMEM = pl.BlockSpec(memory_space=pltpu.VMEM)
SMEM = pl.BlockSpec(memory_space=pltpu.SMEM)
HBM = pl.BlockSpec(memory_space=pltpu.HBM)


def start_copies(pairs, sems):
    copies = [pltpu.make_async_copy(src, dst, sems.at[i]) for i, (src, dst) in enumerate(pairs)]
    for copy in copies:
        copy.start()
    return copies


def sigmoid(values):
    return 0.5 * jnp.tanh(0.5 * values) + 0.5


def silu_slope(values):
    gate = sigmoid(values)
    return gate * (1.0 + values * (1.0 - gate))


def rms_scale(values):
    return lax.rsqrt(jnp.mean(values * values, axis=-1, keepdims=True) + EPSILON)


def modulation(timestep, time_weight):
    half_width = time_weight.shape[0] // 2
    frequency = jnp.exp(-math.log(10000.0) * jnp.arange(half_width, dtype=F32) / half_width)
    angles = timestep.astype(F32)[0] * frequency
    embedded = jnp.concatenate([jnp.sin(angles), jnp.cos(angles)]).astype(BF16)
    return jnp.dot(embedded[None, :], time_weight, preferred_element_type=F32)


def shift_pairs(size):
    up = [(i, i + 1) for i in range(size - 1)]
    return up, [(j, i) for i, j in up]


def near_slots(spots, first_row, valid=True):
    bricks = spots.shape[0]
    spots_t = spots.astype(F32).T
    row_t = spots_t[0:1, :].astype(jnp.int32) - first_row
    near_t = (row_t >= -1) & (row_t <= 4) & valid
    brick_i = lax.broadcasted_iota(jnp.int32, (bricks, bricks), 0)
    brick_j = lax.broadcasted_iota(jnp.int32, (bricks, bricks), 1)
    place_t = jnp.dot(
        jnp.broadcast_to(jnp.where(near_t, 1.0, 0.0), (16, bricks)).astype(BF16),
        jnp.where(brick_i < brick_j, 1.0, 0.0).astype(BF16),
        preferred_element_type=F32,
    )[0:1].astype(jnp.int32)
    count = jnp.sum(jnp.where(near_t, 1.0, 0.0)).astype(jnp.int32)
    return jnp.where(near_t, place_t, -1), count


def tap_cells(pick, spots, first_row, cells):
    found = jnp.dot(pick, spots, preferred_element_type=F32)
    row = found[:, 0:1].astype(jnp.int32) - first_row
    column = found[:, 64:65].astype(jnp.int32)
    lane = lax.broadcasted_iota(jnp.int32, (pick.shape[0], cells), 1)
    onehots = []
    for row_step in (-1, 0, 1):
        for column_step in (-1, 0, 1):
            y, x = row + row_step, column + column_step
            inside = (y >= 0) & (y < 4) & (x >= 0) & (x < 128)
            cell = jnp.where(inside, y * 128 + x, -1)
            onehots.append(jnp.where(lane == cell, 1.0, 0.0).astype(BF16))
    return onehots


def weight_loads(conv_weight, weights, sems, order):
    copies = {}
    for layer in order:
        for part in (3 * layer, 3 * layer + 1, 3 * layer + 2):
            copies[part] = pltpu.make_async_copy(
                conv_weight.at[pl.ds(3 * part, 3)], weights.at[pl.ds(3 * part, 3)], sems.at[part]
            )
            copies[part].start()
    return copies


def parent_conv_kernel(
    place, own_hbm, below_hbm, above_hbm, mod, info, conv_weight, up_hbm,
    out, cells_in, hidden, weights, up_weight, sems, tap_sems,
):
    cells, width = own_hbm.shape
    bricks = info.shape[0]
    taps = conv_weight.shape[0]
    sources = (below_hbm, own_hbm, above_hbm)
    copies = start_copies(
        [(source, cells_in.at[layer]) for layer, source in enumerate(sources)] + [(up_hbm, up_weight)], sems
    )
    for copy in copies:
        copy.wait()
    loads = start_copies(
        [(conv_weight.at[pl.ds(3 * part, 3)], weights.at[pl.ds(3 * part, 3)]) for part in range(taps // 3)], tap_sems
    )
    first_row = place[0]
    spots = info[...]
    slots, near_count = near_slots(spots, first_row)
    scale = 1.0 + mod[0:1, 256:768]
    shift = mod[0:1, 768:1280]
    for layer in range(3):
        values = cells_in[layer].astype(F32)
        pre = values * rms_scale(values) * scale + shift
        act = pre * sigmoid(pre)
        if layer != 1:
            act = jnp.where(place[1 + layer // 2] > 0, act, 0.0)
        hidden[layer] = act.astype(BF16)

    def one_chunk(chunk, first=False):
        slot = lax.broadcasted_iota(jnp.int32, (CHUNK, bricks), 0) + chunk * CHUNK
        pick = jnp.where(slot == slots, 1.0, 0.0).astype(BF16)
        onehots = tap_cells(pick, spots, first_row, cells)
        onehot = jnp.concatenate(onehots, axis=0)
        total = jnp.dot(onehots[4], cells_in[1], preferred_element_type=F32)
        for layer in range(3):
            gathered = jnp.dot(onehot, hidden[layer], preferred_element_type=F32).astype(BF16)
            for corner in range(9):
                tap = 9 * layer + corner
                if first and tap % 3 == 0:
                    loads[tap // 3].wait()
                total += jnp.dot(
                    gathered[corner * CHUNK : (corner + 1) * CHUNK],
                    weights[tap],
                    preferred_element_type=F32,
                )
        lifted = jnp.dot(total.astype(BF16), up_weight[...], preferred_element_type=F32)
        high = lifted.astype(BF16)
        low = (lifted - high.astype(F32)).astype(BF16)
        across = (((0,), (0,)), ((), ()))
        return lax.dot_general(pick, high, across, preferred_element_type=F32) + lax.dot_general(
            pick, low, across, preferred_element_type=F32
        )

    out[...] = one_chunk(0, True)

    @pl.loop(1, (near_count + CHUNK - 1) // CHUNK)
    def _(chunk):
        out[...] += one_chunk(chunk)


def parent_conv(place, own, below, above, mod, info, conv_weight, up_weight):
    taps = conv_weight.shape[0]
    return pl.pallas_call(
        parent_conv_kernel,
        out_shape=jax.ShapeDtypeStruct((info.shape[0], up_weight.shape[1]), F32),
        in_specs=[SMEM] + [pl.BlockSpec(memory_space=pl.ANY)] * 3 + [VMEM, VMEM] + [pl.BlockSpec(memory_space=pl.ANY)] * 2,
        out_specs=VMEM,
        scratch_shapes=[
            pltpu.VMEM((3,) + own.shape, BF16),
            pltpu.VMEM((3,) + own.shape, BF16),
            pltpu.VMEM(conv_weight.shape, BF16),
            pltpu.VMEM(up_weight.shape, BF16),
            pltpu.SemaphoreType.DMA((4,)),
            pltpu.SemaphoreType.DMA((taps // 3,)),
        ],
        compiler_params=pltpu.CompilerParams(vmem_limit_bytes=62 * MIB),
        cost_estimate=pl.CostEstimate(flops=2 * 128 * 27 * 512 * 512, bytes_accessed=16 * MIB, transcendentals=0),
        name="parent_conv",
    )(place, own, below, above, mod, info, conv_weight, up_weight)


def fine_kernel(
    features, cotangent, occupied, parts, spots, mod, inner_weight, outer_weight,
    grads, pack, spread, sums, inner_pair, outer_pair,
):
    step = pl.program_id(0)
    bricks = occupied.shape[0]

    @pl.when(step == 0)
    def _():
        spread[...] = occupied[...].astype(F32).T.astype(BF16)
        for pair, weight in ((inner_pair, inner_weight), (outer_pair, outer_weight)):
            pair[...] = jnp.zeros((256, 256), BF16)
            pair[0:128, 0:128] = weight[...]
            pair[128:256, 128:256] = weight[...]

    def beside(left, right):
        return jnp.concatenate([left, right], axis=1)

    def mean(values):
        rows = values.shape[0]
        return beside(
            jnp.broadcast_to(jnp.mean(values[:, 0:128], -1, keepdims=True), (rows, 128)),
            jnp.broadcast_to(jnp.mean(values[:, 128:256], -1, keepdims=True), (rows, 128)),
        )

    scale = 1.0 + beside(mod[0:1, 0:128], mod[0:1, 0:128])
    shift = beside(mod[0:1, 128:256], mod[0:1, 128:256])
    transposed = (((1,), (1,)), ((), ()))
    side = lax.broadcasted_iota(jnp.int32, (bricks, 256), 1) // 128
    for item in range(0, features.shape[0], 2):
        brick = step * features.shape[0] + item
        pick = jnp.where(lax.broadcasted_iota(jnp.int32, (bricks, 256), 0) == brick + side, 1.0, 0.0).astype(BF16)
        mask = jnp.dot(spread[...], pick, preferred_element_type=F32)
        lifted = beside(
            jnp.sum(parts[:, pl.ds(brick, 1), :], axis=0), jnp.sum(parts[:, pl.ds(brick + 1, 1), :], axis=0)
        ).astype(BF16).astype(F32)
        fine_in = beside(features[item], features[item + 1]).astype(F32) + lifted
        fine_scale = lax.rsqrt(mean(fine_in * fine_in) + EPSILON)
        normed = fine_in * fine_scale
        pre = normed * scale + shift
        gate = sigmoid(pre)
        act = pre * gate
        slope = gate + act * (1.0 - gate)
        inner_pre = jnp.dot(act.astype(BF16), inner_pair[...], preferred_element_type=F32)
        masked = beside(cotangent[item], cotangent[item + 1]).astype(F32) * mask
        grad_hidden = lax.dot_general(masked.astype(BF16), outer_pair[...], transposed, preferred_element_type=F32)
        grad_inner = (grad_hidden * silu_slope(inner_pre)).astype(BF16)
        grad_act = lax.dot_general(grad_inner, inner_pair[...], transposed, preferred_element_type=F32)
        grad_norm = grad_act * slope * scale
        grad_in = masked + fine_scale * (grad_norm - normed * mean(grad_norm * normed))
        rounded = grad_in.astype(BF16)
        grads[item] = rounded[:, 0:128]
        grads[item + 1] = rounded[:, 128:256]
        total = jnp.sum(grad_in, axis=0, keepdims=True)
        sums[pl.ds(brick, 1), :] = total[:, 0:128]
        sums[pl.ds(brick + 1, 1), :] = total[:, 128:256]

    @pl.when(step == pl.num_programs(0) - 1)
    def _():
        total = sums[...].astype(BF16)
        for target in range(pack.shape[0]):
            pack[target, 0:bricks] = total
            pack[target, bricks : 2 * bricks] = spots[...]


def fine_block(features, cotangent, occupied, parts, spots, mod, inner_weight, outer_weight):
    bricks, voxels, width = features.shape
    per_step = 4
    block = pl.BlockSpec((per_step, voxels, width), lambda i: (i, 0, 0))

    def whole(shape):
        return pl.BlockSpec(shape, lambda i: (0,) * len(shape))

    pack_shape = (parts.shape[0], 2 * bricks, width)
    fixed = (occupied, parts, spots, mod, inner_weight, outer_weight)
    return pl.pallas_call(
        fine_kernel,
        grid=(bricks // per_step,),
        out_shape=(
            jax.ShapeDtypeStruct(features.shape, BF16),
            jax.ShapeDtypeStruct(pack_shape, BF16),
        ),
        in_specs=[block, block] + [whole(array.shape) for array in fixed],
        out_specs=(block, whole(pack_shape)),
        scratch_shapes=[
            pltpu.VMEM((voxels, bricks), BF16),
            pltpu.VMEM((bricks, width), F32),
            pltpu.VMEM((256, 256), BF16),
            pltpu.VMEM((256, 256), BF16),
        ],
        compiler_params=pltpu.CompilerParams(vmem_limit_bytes=57 * MIB),
        cost_estimate=pl.CostEstimate(flops=3 * 10**10, bytes_accessed=6 * MIB, transcendentals=2**21),
        name="fine_block",
    )(features, cotangent, *fixed)


def edge_rows_kernel(own, first, last, sems):
    cells = own.shape[0]
    for copy in start_copies([(own.at[pl.ds(0, 128)], first), (own.at[pl.ds(cells - 128, 128)], last)], sems):
        copy.wait()


def edge_rows(own):
    shape = jax.ShapeDtypeStruct((128, own.shape[1]), BF16)
    return pl.pallas_call(
        edge_rows_kernel,
        out_shape=(shape, shape),
        in_specs=[pl.BlockSpec(memory_space=pl.ANY)],
        out_specs=(VMEM, VMEM),
        scratch_shapes=[pltpu.SemaphoreType.DMA((2,))],
        compiler_params=pltpu.CompilerParams(vmem_limit_bytes=60 * MIB),
        cost_estimate=pl.CostEstimate(flops=0, bytes_accessed=MIB, transcendentals=0),
        name="edge_rows",
    )(own)


def six_rows_kernel(before, own, after, out, sems):
    pairs = [
        (own, out.at[pl.ds(128, 512)]),
        (before, out.at[pl.ds(0, 128)]),
        (after, out.at[pl.ds(640, 128)]),
    ]
    for copy in start_copies(pairs, sems):
        copy.wait()


def six_rows(before, own, after):
    return pl.pallas_call(
        six_rows_kernel,
        out_shape=jax.ShapeDtypeStruct((6 * 128, own.shape[1]), BF16),
        in_specs=[pl.BlockSpec(memory_space=pl.ANY)] * 3,
        out_specs=VMEM,
        scratch_shapes=[pltpu.SemaphoreType.DMA((3,))],
        compiler_params=pltpu.CompilerParams(vmem_limit_bytes=4 * MIB),
        cost_estimate=pl.CostEstimate(flops=0, bytes_accessed=2 * MIB, transcendentals=0),
        name="six_rows",
    )(before, own, after)


def cell_lift(pack, up_weight, first_row):
    spots_t = pack[:, 16:32, :].reshape(256, 128).astype(F32).T
    row = spots_t[0:1, :].astype(jnp.int32) - first_row + 1
    column = spots_t[64:65, :].astype(jnp.int32)
    onehot = jnp.where(
        lax.broadcasted_iota(jnp.int32, (6 * 128, 256), 0) == row * 128 + column, 1.0, 0.0
    ).astype(BF16)
    cell_sums = jnp.dot(onehot, pack[:, 0:16, :].reshape(256, 128), preferred_element_type=F32).astype(BF16)
    return lax.dot_general(cell_sums, up_weight, (((1,), (1,)), ((), ())), preferred_element_type=F32)


def own_lift_kernel(place, packs, up_hbm, lift, up_weight, sems):
    (copy,) = start_copies([(up_hbm, up_weight)], sems)
    copy.wait()
    lift[...] = cell_lift(packs, up_weight[...], place[0])


def own_lift(place, packs, up_weight):
    width = up_weight.shape[0]
    return pl.pallas_call(
        own_lift_kernel,
        out_shape=jax.ShapeDtypeStruct((6 * 128, width), F32),
        in_specs=[SMEM, VMEM, pl.BlockSpec(memory_space=pl.ANY)],
        out_specs=VMEM,
        scratch_shapes=[pltpu.VMEM(up_weight.shape, BF16), pltpu.SemaphoreType.DMA((1,))],
        compiler_params=pltpu.CompilerParams(vmem_limit_bytes=40 * MIB),
        cost_estimate=pl.CostEstimate(flops=10**8, bytes_accessed=2 * MIB, transcendentals=0),
        name="own_lift",
    )(place, packs, up_weight)


def coarse_grad_kernel(
    place, features, own, below, above, mod, lift, packs_below, packs_above, conv_weight, up_weight,
    out, grad, center, total, weights, sems,
):
    cells, width = features.shape
    loads = weight_loads(conv_weight, weights, sems, (1, 2, 0))
    for layer, source in ((1, own), (0, below), (2, above)):
        if layer == 1:
            whole = lift[...] + source[...].astype(F32)
            center[...] = whole[128:640]
        else:
            pack = packs_below if layer == 0 else packs_above
            whole = cell_lift(pack, up_weight[...], place[0]) + source[...].astype(F32)
        grad[layer] = whole.astype(BF16)
    for layer in (1, 0, 2):
        for row_step in range(3):
            loads[3 * (2 - layer) + row_step].wait()
        rows = jnp.concatenate(
            [grad[layer, (2 - row_step) * 128 : (2 - row_step) * 128 + cells] for row_step in range(3)], axis=1
        )
        for column_step in range(3):
            taps = jnp.concatenate(
                [weights[9 * (2 - layer) + 3 * row_step + column_step] for row_step in range(3)], axis=1
            )
            piece = lax.dot_general(rows, taps, (((1,), (1,)), ((), ())), preferred_element_type=F32)
            if layer == 1:
                total[column_step] = piece
            else:
                total[column_step] += piece
    column = lax.broadcasted_iota(jnp.int32, (cells, 1), 0) % 128
    left = jnp.where(column == 127, 0.0, pltpu.roll(total[0], cells - 1, 0))
    right = jnp.where(column == 0, 0.0, pltpu.roll(total[2], 1, 0))
    grad_conv = total[1] + left + right
    scale = 1.0 + mod[0:1, 256:768]
    shift = mod[0:1, 768:1280]
    values = features[...].astype(F32)
    coarse_scale = rms_scale(values)
    normed = values * coarse_scale
    grad_cn = grad_conv * silu_slope(normed * scale + shift) * scale
    inner = jnp.mean(grad_cn * normed, axis=-1, keepdims=True)
    out[...] = (center[...] + coarse_scale * (grad_cn - normed * inner)).astype(BF16)


def coarse_grad(
    place, features, own, below, above, mod, lift, packs_below, packs_above, conv_weight, up_weight
):
    cells, width = features.shape
    return pl.pallas_call(
        coarse_grad_kernel,
        out_shape=jax.ShapeDtypeStruct((cells, width), BF16),
        in_specs=[SMEM] + [VMEM] * 8 + [pl.BlockSpec(memory_space=pl.ANY), VMEM],
        out_specs=VMEM,
        scratch_shapes=[
            pltpu.VMEM((3, 6 * 128, width), BF16),
            pltpu.VMEM((cells, width), F32),
            pltpu.VMEM((3, cells, width), F32),
            pltpu.VMEM(conv_weight.shape, BF16),
            pltpu.SemaphoreType.DMA((9,)),
        ],
        compiler_params=pltpu.CompilerParams(vmem_limit_bytes=48 * MIB),
        cost_estimate=pl.CostEstimate(flops=2 * 512 * 27 * 512 * 512, bytes_accessed=18 * MIB, transcendentals=0),
        name="coarse_grad",
    )(place, features, own, below, above, mod, lift, packs_below, packs_above, conv_weight, up_weight)


def per_device(
    fine_features,
    occupancy,
    parent,
    timestep,
    coarse_features,
    time_weight,
    conv_weight,
    up_weight,
    inner_weight,
    outer_weight,
    coarse_cotangent,
    fine_cotangent,
):
    layer_count, row_count, column_count, width = coarse_features.shape
    fine_width = up_weight.shape[1]
    bricks = parent.shape[0]
    fine_size, coarse_size = lax.axis_size("fine"), lax.axis_size("coarse")
    coarse_index, fine_index = lax.axis_index("coarse"), lax.axis_index("fine")
    cells = layer_count * row_count * column_count
    up, down = shift_pairs(coarse_size)
    row_up, row_down = shift_pairs(fine_size)

    local = parent - coarse_index * (cells * fine_size)
    row, column = local // column_count, local % column_count
    lane = jnp.arange(128)[None, :]
    spots = jnp.where(lane < 64, row[:, None], column[:, None]).astype(BF16)
    place = jnp.stack(
        [fine_index * row_count, (coarse_index > 0).astype(jnp.int32), (coarse_index < coarse_size - 1).astype(jnp.int32)]
    ).astype(jnp.int32)

    features = coarse_features.reshape(cells, width)
    cotangent = coarse_cotangent.reshape(cells, width)
    spots_out = jnp.broadcast_to(spots[None], (fine_size, bricks, 128))
    all_spots = lax.all_to_all(spots_out, "fine", 0, 0, tiled=True).reshape(fine_size * bricks, 128)
    sent_features, _ = lax.optimization_barrier((features, spots_out))
    features_below = lax.ppermute(sent_features, "coarse", up)
    features_above = lax.ppermute(sent_features, "coarse", down)
    edge_cotangent, _ = lax.optimization_barrier((cotangent, all_spots))
    first_rows, last_rows = edge_rows(edge_cotangent)
    row_before = lax.ppermute(last_rows, "fine", row_up)
    row_after = lax.ppermute(first_rows, "fine", row_down)
    mod = modulation(timestep, time_weight)

    partial_rows = parent_conv(
        place, features, features_below, features_above, mod, all_spots, conv_weight, up_weight
    )
    parts = lax.all_to_all(
        partial_rows.reshape(fine_size, bricks, fine_width), "fine", 0, 0, tiled=True
    )
    after_conv, _ = lax.optimization_barrier((cotangent, partial_rows))
    cot_own = six_rows(row_before, after_conv, row_after)
    cot_below = lax.ppermute(cot_own, "coarse", up)
    cot_above = lax.ppermute(cot_own, "coarse", down)

    parts, _ = lax.optimization_barrier((parts, cot_own))
    grad_fine, pack = fine_block(
        fine_features, fine_cotangent, occupancy, parts, spots, mod, inner_weight, outer_weight
    )
    packs = lax.all_to_all(pack, "fine", 0, 0, tiled=True)
    packs_below = lax.ppermute(packs, "coarse", up)
    packs_above = lax.ppermute(packs, "coarse", down)
    lift = own_lift(place, packs, up_weight)
    grad_coarse = coarse_grad(
        place, features, cot_own, cot_below, cot_above, mod,
        lift, packs_below, packs_above, conv_weight, up_weight
    )
    return (grad_coarse.reshape(coarse_features.shape), grad_fine)


def solution(mesh):
    in_specs = (
        P(("coarse", "fine"), None, None),
        P(("coarse", "fine"), None),
        P(("coarse", "fine")),
        P(),
        P("coarse", "fine", None, None),
        P(),
        P(),
        P(),
        P(),
        P(),
        P("coarse", "fine", None, None),
        P(("coarse", "fine"), None, None),
    )
    out_specs = (P("coarse", "fine", None, None), P(("coarse", "fine"), None, None))
    return jax.shard_map(
        per_device, mesh=mesh, in_specs=in_specs, out_specs=out_specs, check_vma=False
    )
```

```python
import math

import jax
import jax.numpy as jnp
from jax import lax
from jax.experimental import pallas as pl
from jax.experimental.pallas import tpu as pltpu
from jax.sharding import PartitionSpec as P

EPSILON = 1e-06
MIB = 1024 * 1024
F32 = jnp.float32
BF16 = jnp.bfloat16
CHUNK = 64
VMEM = pl.BlockSpec(memory_space=pltpu.VMEM)
SMEM = pl.BlockSpec(memory_space=pltpu.SMEM)
HBM = pl.BlockSpec(memory_space=pltpu.HBM)


def start_copies(pairs, sems):
    copies = [pltpu.make_async_copy(src, dst, sems.at[i]) for i, (src, dst) in enumerate(pairs)]
    for copy in copies:
        copy.start()
    return copies


def sigmoid(values):
    return 0.5 * jnp.tanh(0.5 * values) + 0.5


def silu_slope(values):
    gate = sigmoid(values)
    return gate * (1.0 + values * (1.0 - gate))


def rms_scale(values):
    return lax.rsqrt(jnp.mean(values * values, axis=-1, keepdims=True) + EPSILON)


def modulation(timestep, time_weight):
    half_width = time_weight.shape[0] // 2
    frequency = jnp.exp(-math.log(10000.0) * jnp.arange(half_width, dtype=F32) / half_width)
    angles = timestep.astype(F32)[0] * frequency
    embedded = jnp.concatenate([jnp.sin(angles), jnp.cos(angles)]).astype(BF16)
    return jnp.dot(embedded[None, :], time_weight, preferred_element_type=F32)


def shift_pairs(size):
    up = [(i, i + 1) for i in range(size - 1)]
    return up, [(j, i) for i, j in up]


def parent_rows_kernel(parent, out, rows):
    lane = lax.broadcasted_iota(jnp.int32, (1, 128), 1)
    for brick in range(rows.shape[0]):
        local = parent[brick] & 8191
        rows[brick : brick + 1, :] = jnp.where(lane < 64, local >> 7, local & 127).astype(F32)
    values = rows[...].astype(BF16)
    for target in range(out.shape[0]):
        out[target] = values


def parent_rows(parent, targets):
    bricks = parent.shape[0]
    return pl.pallas_call(
        parent_rows_kernel,
        out_shape=jax.ShapeDtypeStruct((targets, bricks, 128), BF16),
        in_specs=[SMEM],
        out_specs=VMEM,
        scratch_shapes=[pltpu.VMEM((bricks, 128), F32)],
        compiler_params=pltpu.CompilerParams(vmem_limit_bytes=4 * MIB),
        cost_estimate=pl.CostEstimate(flops=0, bytes_accessed=65536, transcendentals=0),
        name="parent_rows",
    )(parent)


def near_slots(spots, first_row, valid=True):
    bricks = spots.shape[0]
    spots_t = spots.astype(F32).T
    row_t = spots_t[0:1, :].astype(jnp.int32) - first_row
    near_t = (row_t >= -1) & (row_t <= 4) & valid
    brick_i = lax.broadcasted_iota(jnp.int32, (bricks, bricks), 0)
    brick_j = lax.broadcasted_iota(jnp.int32, (bricks, bricks), 1)
    place_t = jnp.dot(
        jnp.broadcast_to(jnp.where(near_t, 1.0, 0.0), (16, bricks)).astype(BF16),
        jnp.where(brick_i < brick_j, 1.0, 0.0).astype(BF16),
        preferred_element_type=F32,
    )[0:1].astype(jnp.int32)
    count = jnp.sum(jnp.where(near_t, 1.0, 0.0)).astype(jnp.int32)
    return jnp.where(near_t, place_t, -1), count


def tap_cells(pick, spots, first_row, cells):
    found = jnp.dot(pick, spots, preferred_element_type=F32)
    row = found[:, 0:1].astype(jnp.int32) - first_row
    column = found[:, 64:65].astype(jnp.int32)
    lane = lax.broadcasted_iota(jnp.int32, (pick.shape[0], cells), 1)
    onehots = []
    for row_step in (-1, 0, 1):
        for column_step in (-1, 0, 1):
            y, x = row + row_step, column + column_step
            inside = (y >= 0) & (y < 4) & (x >= 0) & (x < 128)
            cell = jnp.where(inside, y * 128 + x, -1)
            onehots.append(jnp.where(lane == cell, 1.0, 0.0).astype(BF16))
    return onehots


def weight_loads(conv_weight, weights, sems, order):
    copies = {}
    for layer in order:
        for part in (3 * layer, 3 * layer + 1, 3 * layer + 2):
            copies[part] = pltpu.make_async_copy(
                conv_weight.at[pl.ds(3 * part, 3)], weights.at[pl.ds(3 * part, 3)], sems.at[part]
            )
            copies[part].start()
    return copies


def hide(values, mod):
    values = values.astype(F32)
    pre = values * rms_scale(values) * (1.0 + mod[0:1, 256:768]) + mod[0:1, 768:1280]
    return pre * sigmoid(pre)


def parent_conv_kernel(
    place, own, below, above, mod, info, weights, up_weight, out, hidden
):
    cells, width = own.shape
    bricks = info.shape[0]
    first_row = place[0]
    spots = info[...]
    slots, near_count = near_slots(spots, first_row)
    hidden[1] = hide(own[...], mod).astype(BF16)
    for layer, source in ((0, below), (2, above)):
        hidden[layer] = jnp.where(place[1 + layer // 2] > 0, hide(source[...], mod), 0.0).astype(BF16)

    def one_chunk(chunk):
        slot = lax.broadcasted_iota(jnp.int32, (CHUNK, bricks), 0) + chunk * CHUNK
        pick = jnp.where(slot == slots, 1.0, 0.0).astype(BF16)
        onehots = tap_cells(pick, spots, first_row, cells)
        onehot = jnp.concatenate(onehots, axis=0)
        total = jnp.dot(onehots[4], own[...], preferred_element_type=F32)
        for layer in (1, 0, 2):
            gathered = jnp.dot(onehot, hidden[layer], preferred_element_type=F32).astype(BF16)
            for corner in range(9):
                total += jnp.dot(
                    gathered[corner * CHUNK : (corner + 1) * CHUNK],
                    weights[9 * layer + corner],
                    preferred_element_type=F32,
                )
        lifted = jnp.dot(total.astype(BF16), up_weight[...], preferred_element_type=F32)
        high = lifted.astype(BF16)
        low = (lifted - high.astype(F32)).astype(BF16)
        across = (((0,), (0,)), ((), ()))
        return lax.dot_general(pick, high, across, preferred_element_type=F32) + lax.dot_general(
            pick, low, across, preferred_element_type=F32
        )

    out[...] = one_chunk(0)

    @pl.loop(1, (near_count + CHUNK - 1) // CHUNK)
    def _(chunk):
        out[...] += one_chunk(chunk)


def parent_conv(place, own, below, above, mod, info, conv_weight, up_weight):
    return pl.pallas_call(
        parent_conv_kernel,
        out_shape=jax.ShapeDtypeStruct((info.shape[0], up_weight.shape[1]), F32),
        in_specs=[SMEM] + [VMEM] * 7,
        out_specs=VMEM,
        scratch_shapes=[
            pltpu.VMEM((3,) + own.shape, BF16),
        ],
        compiler_params=pltpu.CompilerParams(vmem_limit_bytes=20 * MIB),
        cost_estimate=pl.CostEstimate(flops=2 * 128 * 27 * 512 * 512, bytes_accessed=16 * MIB, transcendentals=0),
        name="parent_conv",
    )(place, own, below, above, mod, info, conv_weight, up_weight)


def fine_kernel(
    features, cotangent, occupied, parts, spots, mod, inner_weight, outer_weight,
    grads, pack, spread, sums, inner_pair, outer_pair,
):
    step = pl.program_id(0)
    bricks = occupied.shape[0]

    @pl.when(step == 0)
    def _():
        spread[...] = occupied[...].astype(F32).T.astype(BF16)
        for pair, weight in ((inner_pair, inner_weight), (outer_pair, outer_weight)):
            pair[...] = jnp.zeros((256, 256), BF16)
            pair[0:128, 0:128] = weight[...]
            pair[128:256, 128:256] = weight[...]

    def beside(left, right):
        return jnp.concatenate([left, right], axis=1)

    def mean(values):
        rows = values.shape[0]
        return beside(
            jnp.broadcast_to(jnp.mean(values[:, 0:128], -1, keepdims=True), (rows, 128)),
            jnp.broadcast_to(jnp.mean(values[:, 128:256], -1, keepdims=True), (rows, 128)),
        )

    scale = 1.0 + beside(mod[0:1, 0:128], mod[0:1, 0:128])
    shift = beside(mod[0:1, 128:256], mod[0:1, 128:256])
    transposed = (((1,), (1,)), ((), ()))
    side = lax.broadcasted_iota(jnp.int32, (bricks, 256), 1) // 128
    for item in range(0, features.shape[0], 2):
        brick = step * features.shape[0] + item
        pick = jnp.where(lax.broadcasted_iota(jnp.int32, (bricks, 256), 0) == brick + side, 1.0, 0.0).astype(BF16)
        mask = jnp.dot(spread[...], pick, preferred_element_type=F32)
        lifted = beside(
            jnp.sum(parts[:, pl.ds(brick, 1), :], axis=0), jnp.sum(parts[:, pl.ds(brick + 1, 1), :], axis=0)
        ).astype(BF16).astype(F32)
        fine_in = beside(features[item], features[item + 1]).astype(F32) + lifted
        fine_scale = lax.rsqrt(mean(fine_in * fine_in) + EPSILON)
        normed = fine_in * fine_scale
        pre = normed * scale + shift
        gate = sigmoid(pre)
        act = pre * gate
        slope = gate + act * (1.0 - gate)
        inner_pre = jnp.dot(act.astype(BF16), inner_pair[...], preferred_element_type=F32)
        masked = beside(cotangent[item], cotangent[item + 1]).astype(F32) * mask
        grad_hidden = lax.dot_general(masked.astype(BF16), outer_pair[...], transposed, preferred_element_type=F32)
        grad_inner = (grad_hidden * silu_slope(inner_pre)).astype(BF16)
        grad_act = lax.dot_general(grad_inner, inner_pair[...], transposed, preferred_element_type=F32)
        grad_norm = grad_act * slope * scale
        grad_in = masked + fine_scale * (grad_norm - normed * mean(grad_norm * normed))
        rounded = grad_in.astype(BF16)
        grads[item] = rounded[:, 0:128]
        grads[item + 1] = rounded[:, 128:256]
        total = jnp.sum(grad_in, axis=0, keepdims=True)
        sums[pl.ds(brick, 1), :] = total[:, 0:128]
        sums[pl.ds(brick + 1, 1), :] = total[:, 128:256]

    @pl.when(step == pl.num_programs(0) - 1)
    def _():
        total = sums[...].astype(BF16)
        for target in range(pack.shape[0]):
            pack[target, 0:bricks] = total
            pack[target, bricks : 2 * bricks] = spots[0]


def fine_block(features, cotangent, occupied, parts, spots, mod, inner_weight, outer_weight):
    bricks, voxels, width = features.shape
    per_step = 4
    block = pl.BlockSpec((per_step, voxels, width), lambda i: (i, 0, 0))

    def whole(shape):
        return pl.BlockSpec(shape, lambda i: (0,) * len(shape))

    pack_shape = (parts.shape[0], 2 * bricks, width)
    others = (mod, inner_weight, outer_weight)
    return pl.pallas_call(
        fine_kernel,
        grid=(bricks // per_step,),
        out_shape=(
            jax.ShapeDtypeStruct(features.shape, BF16),
            jax.ShapeDtypeStruct(pack_shape, BF16),
        ),
        in_specs=[block, block, whole(occupied.shape), whole(parts.shape), whole((1, bricks, width))]
        + [whole(array.shape) for array in others],
        out_specs=(block, whole(pack_shape)),
        scratch_shapes=[
            pltpu.VMEM((voxels, bricks), BF16),
            pltpu.VMEM((bricks, width), F32),
            pltpu.VMEM((256, 256), BF16),
            pltpu.VMEM((256, 256), BF16),
        ],
        compiler_params=pltpu.CompilerParams(vmem_limit_bytes=57 * MIB),
        cost_estimate=pl.CostEstimate(flops=3 * 10**10, bytes_accessed=6 * MIB, transcendentals=2**21),
        name="fine_block",
    )(features, cotangent, occupied, parts, spots, *others)


def edge_rows_kernel(own, first, last, sems):
    cells = own.shape[0]
    for copy in start_copies([(own.at[pl.ds(0, 128)], first), (own.at[pl.ds(cells - 128, 128)], last)], sems):
        copy.wait()


def edge_rows(own):
    shape = jax.ShapeDtypeStruct((128, own.shape[1]), BF16)
    return pl.pallas_call(
        edge_rows_kernel,
        out_shape=(shape, shape),
        in_specs=[pl.BlockSpec(memory_space=pl.ANY)],
        out_specs=(VMEM, VMEM),
        scratch_shapes=[pltpu.SemaphoreType.DMA((2,))],
        compiler_params=pltpu.CompilerParams(vmem_limit_bytes=36 * MIB),
        cost_estimate=pl.CostEstimate(flops=10**10, bytes_accessed=MIB, transcendentals=0),
        name="edge_rows",
    )(own)


def six_rows_kernel(before, own, after, out, sems):
    pairs = [
        (own, out.at[pl.ds(128, 512)]),
        (before, out.at[pl.ds(0, 128)]),
        (after, out.at[pl.ds(640, 128)]),
    ]
    for copy in start_copies(pairs, sems):
        copy.wait()


def six_rows(before, own, after):
    return pl.pallas_call(
        six_rows_kernel,
        out_shape=jax.ShapeDtypeStruct((6 * 128, own.shape[1]), BF16),
        in_specs=[pl.BlockSpec(memory_space=pl.ANY)] * 3,
        out_specs=VMEM,
        scratch_shapes=[pltpu.SemaphoreType.DMA((3,))],
        compiler_params=pltpu.CompilerParams(vmem_limit_bytes=4 * MIB),
        cost_estimate=pl.CostEstimate(flops=0, bytes_accessed=2 * MIB, transcendentals=0),
        name="six_rows",
    )(before, own, after)


def cell_lift(pack, up_weight, first_row):
    spots_t = pack[:, 16:32, :].reshape(256, 128).astype(F32).T
    row = spots_t[0:1, :].astype(jnp.int32) - first_row + 1
    column = spots_t[64:65, :].astype(jnp.int32)
    onehot = jnp.where(
        lax.broadcasted_iota(jnp.int32, (6 * 128, 256), 0) == row * 128 + column, 1.0, 0.0
    ).astype(BF16)
    cell_sums = jnp.dot(onehot, pack[:, 0:16, :].reshape(256, 128), preferred_element_type=F32).astype(BF16)
    return lax.dot_general(cell_sums, up_weight, (((1,), (1,)), ((), ())), preferred_element_type=F32)


def own_lift_kernel(place, packs, up_hbm, lift, up_weight, sems):
    (copy,) = start_copies([(up_hbm, up_weight)], sems)
    copy.wait()
    lift[...] = cell_lift(packs, up_weight[...], place[0])


def own_lift(place, packs, up_weight):
    width = up_weight.shape[0]
    return pl.pallas_call(
        own_lift_kernel,
        out_shape=jax.ShapeDtypeStruct((6 * 128, width), F32),
        in_specs=[SMEM, VMEM, pl.BlockSpec(memory_space=pl.ANY)],
        out_specs=VMEM,
        scratch_shapes=[pltpu.VMEM(up_weight.shape, BF16), pltpu.SemaphoreType.DMA((1,))],
        compiler_params=pltpu.CompilerParams(vmem_limit_bytes=40 * MIB),
        cost_estimate=pl.CostEstimate(flops=10**8, bytes_accessed=2 * MIB, transcendentals=0),
        name="own_lift",
    )(place, packs, up_weight)


def coarse_grad_kernel(
    place, features, own, below, above, mod, lift, packs_below, packs_above, conv_weight, up_weight,
    out, grad, center, total, weights, sems,
):
    cells, width = features.shape
    loads = weight_loads(conv_weight, weights, sems, (1, 2, 0))
    for layer, source in ((1, own), (0, below), (2, above)):
        if layer == 1:
            whole = lift[...] + source[...].astype(F32)
            center[...] = whole[128:640]
        else:
            pack = packs_below if layer == 0 else packs_above
            whole = cell_lift(pack, up_weight[...], place[0]) + source[...].astype(F32)
        grad[layer] = whole.astype(BF16)
    for layer in (1, 0, 2):
        for row_step in range(3):
            loads[3 * (2 - layer) + row_step].wait()
        rows = jnp.concatenate(
            [grad[layer, (2 - row_step) * 128 : (2 - row_step) * 128 + cells] for row_step in range(3)], axis=1
        )
        for column_step in range(3):
            taps = jnp.concatenate(
                [weights[9 * (2 - layer) + 3 * row_step + column_step] for row_step in range(3)], axis=1
            )
            piece = lax.dot_general(rows, taps, (((1,), (1,)), ((), ())), preferred_element_type=F32)
            if layer == 1:
                total[column_step] = piece
            else:
                total[column_step] += piece
    column = lax.broadcasted_iota(jnp.int32, (cells, 1), 0) % 128
    left = jnp.where(column == 127, 0.0, pltpu.roll(total[0], cells - 1, 0))
    right = jnp.where(column == 0, 0.0, pltpu.roll(total[2], 1, 0))
    grad_conv = total[1] + left + right
    scale = 1.0 + mod[0:1, 256:768]
    shift = mod[0:1, 768:1280]
    values = features[...].astype(F32)
    coarse_scale = rms_scale(values)
    normed = values * coarse_scale
    grad_cn = grad_conv * silu_slope(normed * scale + shift) * scale
    inner = jnp.mean(grad_cn * normed, axis=-1, keepdims=True)
    out[...] = (center[...] + coarse_scale * (grad_cn - normed * inner)).astype(BF16)


def coarse_grad(
    place, features, own, below, above, mod, lift, packs_below, packs_above, conv_weight, up_weight
):
    cells, width = features.shape
    return pl.pallas_call(
        coarse_grad_kernel,
        out_shape=jax.ShapeDtypeStruct((cells, width), BF16),
        in_specs=[SMEM] + [VMEM] * 8 + [pl.BlockSpec(memory_space=pl.ANY), VMEM],
        out_specs=VMEM,
        scratch_shapes=[
            pltpu.VMEM((3, 6 * 128, width), BF16),
            pltpu.VMEM((cells, width), F32),
            pltpu.VMEM((3, cells, width), F32),
            pltpu.VMEM(conv_weight.shape, BF16),
            pltpu.SemaphoreType.DMA((9,)),
        ],
        compiler_params=pltpu.CompilerParams(vmem_limit_bytes=48 * MIB),
        cost_estimate=pl.CostEstimate(flops=2 * 512 * 27 * 512 * 512, bytes_accessed=18 * MIB, transcendentals=0),
        name="coarse_grad",
    )(place, features, own, below, above, mod, lift, packs_below, packs_above, conv_weight, up_weight)


def per_device(
    fine_features,
    occupancy,
    parent,
    timestep,
    coarse_features,
    time_weight,
    conv_weight,
    up_weight,
    inner_weight,
    outer_weight,
    coarse_cotangent,
    fine_cotangent,
):
    layer_count, row_count, column_count, width = coarse_features.shape
    fine_width = up_weight.shape[1]
    bricks = parent.shape[0]
    fine_size, coarse_size = lax.axis_size("fine"), lax.axis_size("coarse")
    coarse_index, fine_index = lax.axis_index("coarse"), lax.axis_index("fine")
    cells = layer_count * row_count * column_count
    up, down = shift_pairs(coarse_size)
    row_up, row_down = shift_pairs(fine_size)

    spots_out = parent_rows(parent, fine_size)
    place = jnp.stack(
        [fine_index * row_count, (coarse_index > 0).astype(jnp.int32), (coarse_index < coarse_size - 1).astype(jnp.int32)]
    ).astype(jnp.int32)

    features = coarse_features.reshape(cells, width)
    cotangent = coarse_cotangent.reshape(cells, width)
    all_spots = lax.all_to_all(spots_out, "fine", 0, 0, tiled=True).reshape(fine_size * bricks, 128)
    sent_features, _ = lax.optimization_barrier((features, spots_out))
    features_below = lax.ppermute(sent_features, "coarse", up)
    features_above = lax.ppermute(sent_features, "coarse", down)
    edge_cotangent, _ = lax.optimization_barrier((cotangent, all_spots))
    first_rows, last_rows = edge_rows(edge_cotangent)
    row_before = lax.ppermute(last_rows, "fine", row_up)
    row_after = lax.ppermute(first_rows, "fine", row_down)
    mod = modulation(timestep, time_weight)

    partial_rows = parent_conv(
        place, features, features_below, features_above, mod, all_spots, conv_weight, up_weight
    )
    parts = lax.all_to_all(
        partial_rows.reshape(fine_size, bricks, fine_width), "fine", 0, 0, tiled=True
    )
    after_conv, _ = lax.optimization_barrier((cotangent, partial_rows))
    cot_own = six_rows(row_before, after_conv, row_after)
    cot_below = lax.ppermute(cot_own, "coarse", up)
    cot_above = lax.ppermute(cot_own, "coarse", down)

    parts, _ = lax.optimization_barrier((parts, cot_own))
    grad_fine, pack = fine_block(
        fine_features, fine_cotangent, occupancy, parts, spots_out, mod, inner_weight, outer_weight
    )
    packs = lax.all_to_all(pack, "fine", 0, 0, tiled=True)
    packs_below = lax.ppermute(packs, "coarse", up)
    packs_above = lax.ppermute(packs, "coarse", down)
    lift = own_lift(place, packs, up_weight)
    grad_coarse = coarse_grad(
        place, features, cot_own, cot_below, cot_above, mod,
        lift, packs_below, packs_above, conv_weight, up_weight
    )
    return (grad_coarse.reshape(coarse_features.shape), grad_fine)


def solution(mesh):
    in_specs = (
        P(("coarse", "fine"), None, None),
        P(("coarse", "fine"), None),
        P(("coarse", "fine")),
        P(),
        P("coarse", "fine", None, None),
        P(),
        P(),
        P(),
        P(),
        P(),
        P("coarse", "fine", None, None),
        P(("coarse", "fine"), None, None),
    )
    out_specs = (P("coarse", "fine", None, None), P(("coarse", "fine"), None, None))
    return jax.shard_map(
        per_device, mesh=mesh, in_specs=in_specs, out_specs=out_specs, check_vma=False
    )
```

```python
import math

import jax
import jax.numpy as jnp
from jax import lax
from jax.experimental import pallas as pl
from jax.experimental.pallas import tpu as pltpu
from jax.sharding import PartitionSpec as P

EPSILON = 1e-06
MIB = 1024 * 1024
F32 = jnp.float32
BF16 = jnp.bfloat16
CHUNK = 64
VMEM = pl.BlockSpec(memory_space=pltpu.VMEM)
SMEM = pl.BlockSpec(memory_space=pltpu.SMEM)
HBM = pl.BlockSpec(memory_space=pltpu.HBM)


def start_copies(pairs, sems):
    copies = [pltpu.make_async_copy(src, dst, sems.at[i]) for i, (src, dst) in enumerate(pairs)]
    for copy in copies:
        copy.start()
    return copies


def sigmoid(values):
    return 0.5 * jnp.tanh(0.5 * values) + 0.5


def silu_slope(values):
    gate = sigmoid(values)
    return gate * (1.0 + values * (1.0 - gate))


def rms_scale(values):
    return lax.rsqrt(jnp.mean(values * values, axis=-1, keepdims=True) + EPSILON)


def modulation(timestep, time_weight):
    half_width = time_weight.shape[0] // 2
    frequency = jnp.exp(-math.log(10000.0) * jnp.arange(half_width, dtype=F32) / half_width)
    angles = timestep.astype(F32)[0] * frequency
    embedded = jnp.concatenate([jnp.sin(angles), jnp.cos(angles)]).astype(BF16)
    return jnp.dot(embedded[None, :], time_weight, preferred_element_type=F32)


def shift_pairs(size):
    up = [(i, i + 1) for i in range(size - 1)]
    return up, [(j, i) for i, j in up]


def parent_rows_kernel(parent, out, rows):
    lane = lax.broadcasted_iota(jnp.int32, (1, 128), 1)
    for brick in range(rows.shape[0]):
        local = parent[brick] & 8191
        rows[brick : brick + 1, :] = jnp.where(lane < 64, local >> 7, local & 127).astype(F32)
    values = rows[...].astype(BF16)
    for target in range(out.shape[0]):
        out[target] = values


def parent_rows(parent, targets):
    bricks = parent.shape[0]
    return pl.pallas_call(
        parent_rows_kernel,
        out_shape=jax.ShapeDtypeStruct((targets, bricks, 128), BF16),
        in_specs=[SMEM],
        out_specs=VMEM,
        scratch_shapes=[pltpu.VMEM((bricks, 128), F32)],
        compiler_params=pltpu.CompilerParams(vmem_limit_bytes=4 * MIB),
        cost_estimate=pl.CostEstimate(flops=0, bytes_accessed=65536, transcendentals=0),
        name="parent_rows",
    )(parent)


def near_slots(spots, first_row, valid=True):
    bricks = spots.shape[0]
    spots_t = spots.astype(F32).T
    row_t = spots_t[0:1, :].astype(jnp.int32) - first_row
    near_t = (row_t >= -1) & (row_t <= 4) & valid
    brick_i = lax.broadcasted_iota(jnp.int32, (bricks, bricks), 0)
    brick_j = lax.broadcasted_iota(jnp.int32, (bricks, bricks), 1)
    place_t = jnp.dot(
        jnp.broadcast_to(jnp.where(near_t, 1.0, 0.0), (16, bricks)).astype(BF16),
        jnp.where(brick_i < brick_j, 1.0, 0.0).astype(BF16),
        preferred_element_type=F32,
    )[0:1].astype(jnp.int32)
    count = jnp.sum(jnp.where(near_t, 1.0, 0.0)).astype(jnp.int32)
    return jnp.where(near_t, place_t, -1), count


def tap_cells(pick, spots, first_row, cells):
    found = jnp.dot(pick, spots, preferred_element_type=F32)
    row = found[:, 0:1].astype(jnp.int32) - first_row
    column = found[:, 64:65].astype(jnp.int32)
    lane = lax.broadcasted_iota(jnp.int32, (pick.shape[0], cells), 1)
    onehots = []
    for row_step in (-1, 0, 1):
        for column_step in (-1, 0, 1):
            y, x = row + row_step, column + column_step
            inside = (y >= 0) & (y < 4) & (x >= 0) & (x < 128)
            cell = jnp.where(inside, y * 128 + x, -1)
            onehots.append(jnp.where(lane == cell, 1.0, 0.0).astype(BF16))
    return onehots


def hide(values, mod):
    values = values.astype(F32)
    pre = values * rms_scale(values) * (1.0 + mod[0:1, 256:768]) + mod[0:1, 768:1280]
    return pre * sigmoid(pre)


def parent_conv_kernel(
    place, own, below, above, mod, info, weights, up_weight, out, hidden
):
    cells, width = own.shape
    bricks = info.shape[0]
    first_row = place[0]
    spots = info[...]
    slots, near_count = near_slots(spots, first_row)
    hidden[1] = hide(own[...], mod).astype(BF16)
    for layer, source in ((0, below), (2, above)):
        hidden[layer] = jnp.where(place[1 + layer // 2] > 0, hide(source[...], mod), 0.0).astype(BF16)

    def one_chunk(chunk):
        slot = lax.broadcasted_iota(jnp.int32, (CHUNK, bricks), 0) + chunk * CHUNK
        pick = jnp.where(slot == slots, 1.0, 0.0).astype(BF16)
        onehots = tap_cells(pick, spots, first_row, cells)
        onehot = jnp.concatenate(onehots, axis=0)
        total = jnp.dot(onehots[4], own[...], preferred_element_type=F32)
        for layer in (1, 0, 2):
            gathered = jnp.dot(onehot, hidden[layer], preferred_element_type=F32).astype(BF16)
            for corner in range(9):
                total += jnp.dot(
                    gathered[corner * CHUNK : (corner + 1) * CHUNK],
                    weights[9 * layer + corner],
                    preferred_element_type=F32,
                )
        lifted = jnp.dot(total.astype(BF16), up_weight[...], preferred_element_type=F32)
        high = lifted.astype(BF16)
        low = (lifted - high.astype(F32)).astype(BF16)
        across = (((0,), (0,)), ((), ()))
        return lax.dot_general(pick, high, across, preferred_element_type=F32) + lax.dot_general(
            pick, low, across, preferred_element_type=F32
        )

    out[...] = one_chunk(0)

    @pl.loop(1, (near_count + CHUNK - 1) // CHUNK)
    def _(chunk):
        out[...] += one_chunk(chunk)


def parent_conv(place, own, below, above, mod, info, conv_weight, up_weight):
    return pl.pallas_call(
        parent_conv_kernel,
        out_shape=jax.ShapeDtypeStruct((info.shape[0], up_weight.shape[1]), F32),
        in_specs=[SMEM] + [VMEM] * 7,
        out_specs=VMEM,
        scratch_shapes=[
            pltpu.VMEM((3,) + own.shape, BF16),
        ],
        compiler_params=pltpu.CompilerParams(vmem_limit_bytes=20 * MIB),
        cost_estimate=pl.CostEstimate(flops=2 * 128 * 27 * 512 * 512, bytes_accessed=16 * MIB, transcendentals=0),
        name="parent_conv",
    )(place, own, below, above, mod, info, conv_weight, up_weight)


def fine_kernel(
    features, cotangent, occupied, parts, spots, mod, inner_weight, outer_weight,
    grads, pack, spread, sums, inner_pair, outer_pair,
):
    step = pl.program_id(0)
    bricks = occupied.shape[0]

    @pl.when(step == 0)
    def _():
        spread[...] = occupied[...].astype(F32).T.astype(BF16)
        for pair, weight in ((inner_pair, inner_weight), (outer_pair, outer_weight)):
            pair[...] = jnp.zeros((256, 256), BF16)
            pair[0:128, 0:128] = weight[...]
            pair[128:256, 128:256] = weight[...]

    def beside(left, right):
        return jnp.concatenate([left, right], axis=1)

    def mean(values):
        rows = values.shape[0]
        return beside(
            jnp.broadcast_to(jnp.mean(values[:, 0:128], -1, keepdims=True), (rows, 128)),
            jnp.broadcast_to(jnp.mean(values[:, 128:256], -1, keepdims=True), (rows, 128)),
        )

    scale = 1.0 + beside(mod[0:1, 0:128], mod[0:1, 0:128])
    shift = beside(mod[0:1, 128:256], mod[0:1, 128:256])
    transposed = (((1,), (1,)), ((), ()))
    side = lax.broadcasted_iota(jnp.int32, (bricks, 256), 1) // 128
    for item in range(0, features.shape[0], 2):
        brick = step * features.shape[0] + item
        pick = jnp.where(lax.broadcasted_iota(jnp.int32, (bricks, 256), 0) == brick + side, 1.0, 0.0).astype(BF16)
        mask = jnp.dot(spread[...], pick, preferred_element_type=F32)
        lifted = beside(
            jnp.sum(parts[:, pl.ds(brick, 1), :], axis=0), jnp.sum(parts[:, pl.ds(brick + 1, 1), :], axis=0)
        ).astype(BF16).astype(F32)
        fine_in = beside(features[item], features[item + 1]).astype(F32) + lifted
        fine_scale = lax.rsqrt(mean(fine_in * fine_in) + EPSILON)
        normed = fine_in * fine_scale
        pre = normed * scale + shift
        gate = sigmoid(pre)
        act = pre * gate
        slope = gate + act * (1.0 - gate)
        inner_pre = jnp.dot(act.astype(BF16), inner_pair[...], preferred_element_type=F32)
        masked = beside(cotangent[item], cotangent[item + 1]).astype(F32) * mask
        grad_hidden = lax.dot_general(masked.astype(BF16), outer_pair[...], transposed, preferred_element_type=F32)
        grad_inner = (grad_hidden * silu_slope(inner_pre)).astype(BF16)
        grad_act = lax.dot_general(grad_inner, inner_pair[...], transposed, preferred_element_type=F32)
        grad_norm = grad_act * slope * scale
        grad_in = masked + fine_scale * (grad_norm - normed * mean(grad_norm * normed))
        rounded = grad_in.astype(BF16)
        grads[item] = rounded[:, 0:128]
        grads[item + 1] = rounded[:, 128:256]
        total = jnp.sum(grad_in, axis=0, keepdims=True)
        sums[pl.ds(brick, 1), :] = total[:, 0:128]
        sums[pl.ds(brick + 1, 1), :] = total[:, 128:256]

    @pl.when(step == pl.num_programs(0) - 1)
    def _():
        total = sums[...].astype(BF16)
        for target in range(pack.shape[0]):
            pack[target, 0:bricks] = total
            pack[target, bricks : 2 * bricks] = spots[0]


def fine_block(features, cotangent, occupied, parts, spots, mod, inner_weight, outer_weight):
    bricks, voxels, width = features.shape
    per_step = 4
    block = pl.BlockSpec((per_step, voxels, width), lambda i: (i, 0, 0))

    def whole(shape):
        return pl.BlockSpec(shape, lambda i: (0,) * len(shape))

    pack_shape = (parts.shape[0], 2 * bricks, width)
    others = (mod, inner_weight, outer_weight)
    return pl.pallas_call(
        fine_kernel,
        grid=(bricks // per_step,),
        out_shape=(
            jax.ShapeDtypeStruct(features.shape, BF16),
            jax.ShapeDtypeStruct(pack_shape, BF16),
        ),
        in_specs=[block, block, whole(occupied.shape), whole(parts.shape), whole((1, bricks, width))]
        + [whole(array.shape) for array in others],
        out_specs=(block, whole(pack_shape)),
        scratch_shapes=[
            pltpu.VMEM((voxels, bricks), BF16),
            pltpu.VMEM((bricks, width), F32),
            pltpu.VMEM((256, 256), BF16),
            pltpu.VMEM((256, 256), BF16),
        ],
        compiler_params=pltpu.CompilerParams(vmem_limit_bytes=57 * MIB),
        cost_estimate=pl.CostEstimate(flops=3 * 10**10, bytes_accessed=6 * MIB, transcendentals=2**21),
        name="fine_block",
    )(features, cotangent, occupied, parts, spots, *others)


def edge_rows_kernel(own, first, last, sems):
    cells = own.shape[0]
    for copy in start_copies([(own.at[pl.ds(0, 128)], first), (own.at[pl.ds(cells - 128, 128)], last)], sems):
        copy.wait()


def edge_rows(own):
    shape = jax.ShapeDtypeStruct((128, own.shape[1]), BF16)
    return pl.pallas_call(
        edge_rows_kernel,
        out_shape=(shape, shape),
        in_specs=[pl.BlockSpec(memory_space=pl.ANY)],
        out_specs=(VMEM, VMEM),
        scratch_shapes=[pltpu.SemaphoreType.DMA((2,))],
        compiler_params=pltpu.CompilerParams(vmem_limit_bytes=36 * MIB),
        cost_estimate=pl.CostEstimate(flops=10**10, bytes_accessed=MIB, transcendentals=0),
        name="edge_rows",
    )(own)


def six_rows_kernel(before, own, after, out, sems):
    pairs = [
        (own, out.at[pl.ds(128, 512)]),
        (before, out.at[pl.ds(0, 128)]),
        (after, out.at[pl.ds(640, 128)]),
    ]
    for copy in start_copies(pairs, sems):
        copy.wait()


def six_rows(before, own, after):
    return pl.pallas_call(
        six_rows_kernel,
        out_shape=jax.ShapeDtypeStruct((6 * 128, own.shape[1]), BF16),
        in_specs=[pl.BlockSpec(memory_space=pl.ANY)] * 3,
        out_specs=VMEM,
        scratch_shapes=[pltpu.SemaphoreType.DMA((3,))],
        compiler_params=pltpu.CompilerParams(vmem_limit_bytes=4 * MIB),
        cost_estimate=pl.CostEstimate(flops=0, bytes_accessed=2 * MIB, transcendentals=0),
        name="six_rows",
    )(before, own, after)


def cell_lift(pack, up_weight, first_row):
    spots_t = pack[:, 16:32, :].reshape(256, 128).astype(F32).T
    row = spots_t[0:1, :].astype(jnp.int32) - first_row + 1
    column = spots_t[64:65, :].astype(jnp.int32)
    onehot = jnp.where(
        lax.broadcasted_iota(jnp.int32, (6 * 128, 256), 0) == row * 128 + column, 1.0, 0.0
    ).astype(BF16)
    cell_sums = jnp.dot(onehot, pack[:, 0:16, :].reshape(256, 128), preferred_element_type=F32).astype(BF16)
    return lax.dot_general(cell_sums, up_weight, (((1,), (1,)), ((), ())), preferred_element_type=F32)


def own_lift_kernel(place, packs, up_weight, conv_weight, lift, middle, sems):
    copies = start_copies(
        [(conv_weight.at[pl.ds(9 + 3 * part, 3)], middle.at[pl.ds(3 * part, 3)]) for part in range(3)], sems
    )
    lift[...] = cell_lift(packs, up_weight[...], place[0])
    for copy in copies:
        copy.wait()


def own_lift(place, packs, up_weight, conv_weight):
    width = up_weight.shape[0]
    return pl.pallas_call(
        own_lift_kernel,
        out_shape=(
            jax.ShapeDtypeStruct((6 * 128, width), F32),
            jax.ShapeDtypeStruct((9,) + conv_weight.shape[1:], BF16),
        ),
        in_specs=[SMEM, VMEM, VMEM, pl.BlockSpec(memory_space=pl.ANY)],
        out_specs=(VMEM, VMEM),
        scratch_shapes=[pltpu.SemaphoreType.DMA((3,))],
        compiler_params=pltpu.CompilerParams(vmem_limit_bytes=50 * MIB),
        cost_estimate=pl.CostEstimate(flops=10**8, bytes_accessed=6 * MIB, transcendentals=0),
        name="own_lift",
    )(place, packs, up_weight, conv_weight)


def coarse_grad_kernel(
    place, features, own, below, above, mod, lift, middle, packs_below, packs_above, conv_weight, up_weight,
    out, grad, center, total, weights, sems,
):
    cells, width = features.shape
    loads = start_copies(
        [
            (conv_weight.at[pl.ds(tap, 3)], weights.at[pl.ds(3 * part, 3)])
            for part, tap in enumerate((18, 21, 24, 0, 3, 6))
        ],
        sems,
    )
    for layer, source in ((1, own), (0, below), (2, above)):
        if layer == 1:
            whole = lift[...] + source[...].astype(F32)
            center[...] = whole[128:640]
        else:
            pack = packs_below if layer == 0 else packs_above
            whole = cell_lift(pack, up_weight[...], place[0]) + source[...].astype(F32)
        grad[layer] = whole.astype(BF16)
    for layer in (1, 0, 2):
        if layer == 1:
            held, begin = middle, 0
        else:
            held, begin = weights, 9 * (layer // 2)
            for part in range(3):
                loads[3 * (layer // 2) + part].wait()
        rows = jnp.concatenate(
            [grad[layer, (2 - row_step) * 128 : (2 - row_step) * 128 + cells] for row_step in range(3)], axis=1
        )
        for column_step in range(3):
            taps = jnp.concatenate(
                [held[begin + 3 * row_step + column_step] for row_step in range(3)], axis=1
            )
            piece = lax.dot_general(rows, taps, (((1,), (1,)), ((), ())), preferred_element_type=F32)
            if layer == 1:
                total[column_step] = piece
            else:
                total[column_step] += piece
    column = lax.broadcasted_iota(jnp.int32, (cells, 1), 0) % 128
    left = jnp.where(column == 127, 0.0, pltpu.roll(total[0], cells - 1, 0))
    right = jnp.where(column == 0, 0.0, pltpu.roll(total[2], 1, 0))
    grad_conv = total[1] + left + right
    scale = 1.0 + mod[0:1, 256:768]
    shift = mod[0:1, 768:1280]
    values = features[...].astype(F32)
    coarse_scale = rms_scale(values)
    normed = values * coarse_scale
    grad_cn = grad_conv * silu_slope(normed * scale + shift) * scale
    inner = jnp.mean(grad_cn * normed, axis=-1, keepdims=True)
    out[...] = (center[...] + coarse_scale * (grad_cn - normed * inner)).astype(BF16)


def coarse_grad(
    place, features, own, below, above, mod, lift, middle, packs_below, packs_above, conv_weight, up_weight
):
    cells, width = features.shape
    return pl.pallas_call(
        coarse_grad_kernel,
        out_shape=jax.ShapeDtypeStruct((cells, width), BF16),
        in_specs=[SMEM] + [VMEM] * 9 + [pl.BlockSpec(memory_space=pl.ANY), VMEM],
        out_specs=VMEM,
        scratch_shapes=[
            pltpu.VMEM((3, 6 * 128, width), BF16),
            pltpu.VMEM((cells, width), F32),
            pltpu.VMEM((3, cells, width), F32),
            pltpu.VMEM((18,) + conv_weight.shape[1:], BF16),
            pltpu.SemaphoreType.DMA((6,)),
        ],
        compiler_params=pltpu.CompilerParams(vmem_limit_bytes=46 * MIB),
        cost_estimate=pl.CostEstimate(flops=2 * 512 * 27 * 512 * 512, bytes_accessed=18 * MIB, transcendentals=0),
        name="coarse_grad",
    )(place, features, own, below, above, mod, lift, middle, packs_below, packs_above, conv_weight, up_weight)


def per_device(
    fine_features,
    occupancy,
    parent,
    timestep,
    coarse_features,
    time_weight,
    conv_weight,
    up_weight,
    inner_weight,
    outer_weight,
    coarse_cotangent,
    fine_cotangent,
):
    layer_count, row_count, column_count, width = coarse_features.shape
    fine_width = up_weight.shape[1]
    bricks = parent.shape[0]
    fine_size, coarse_size = lax.axis_size("fine"), lax.axis_size("coarse")
    coarse_index, fine_index = lax.axis_index("coarse"), lax.axis_index("fine")
    cells = layer_count * row_count * column_count
    up, down = shift_pairs(coarse_size)
    row_up, row_down = shift_pairs(fine_size)

    spots_out = parent_rows(parent, fine_size)
    place = jnp.stack(
        [fine_index * row_count, (coarse_index > 0).astype(jnp.int32), (coarse_index < coarse_size - 1).astype(jnp.int32)]
    ).astype(jnp.int32)

    features = coarse_features.reshape(cells, width)
    cotangent = coarse_cotangent.reshape(cells, width)
    all_spots = lax.all_to_all(spots_out, "fine", 0, 0, tiled=True).reshape(fine_size * bricks, 128)
    sent_features, _ = lax.optimization_barrier((features, spots_out))
    features_below = lax.ppermute(sent_features, "coarse", up)
    features_above = lax.ppermute(sent_features, "coarse", down)
    edge_cotangent, _ = lax.optimization_barrier((cotangent, all_spots))
    first_rows, last_rows = edge_rows(edge_cotangent)
    row_before = lax.ppermute(last_rows, "fine", row_up)
    row_after = lax.ppermute(first_rows, "fine", row_down)
    mod = modulation(timestep, time_weight)

    partial_rows = parent_conv(
        place, features, features_below, features_above, mod, all_spots, conv_weight, up_weight
    )
    parts = lax.all_to_all(
        partial_rows.reshape(fine_size, bricks, fine_width), "fine", 0, 0, tiled=True
    )
    after_conv, _ = lax.optimization_barrier((cotangent, partial_rows))
    cot_own = six_rows(row_before, after_conv, row_after)
    cot_below = lax.ppermute(cot_own, "coarse", up)
    cot_above = lax.ppermute(cot_own, "coarse", down)

    parts, _ = lax.optimization_barrier((parts, cot_own))
    grad_fine, pack = fine_block(
        fine_features, fine_cotangent, occupancy, parts, spots_out, mod, inner_weight, outer_weight
    )
    packs = lax.all_to_all(pack, "fine", 0, 0, tiled=True)
    packs_below = lax.ppermute(packs, "coarse", up)
    packs_above = lax.ppermute(packs, "coarse", down)
    lift, middle = own_lift(place, packs, up_weight, conv_weight)
    grad_coarse = coarse_grad(
        place, features, cot_own, cot_below, cot_above, mod,
        lift, middle, packs_below, packs_above, conv_weight, up_weight
    )
    return (grad_coarse.reshape(coarse_features.shape), grad_fine)


def solution(mesh):
    in_specs = (
        P(("coarse", "fine"), None, None),
        P(("coarse", "fine"), None),
        P(("coarse", "fine")),
        P(),
        P("coarse", "fine", None, None),
        P(),
        P(),
        P(),
        P(),
        P(),
        P("coarse", "fine", None, None),
        P(("coarse", "fine"), None, None),
    )
    out_specs = (P("coarse", "fine", None, None), P(("coarse", "fine"), None, None))
    return jax.shard_map(
        per_device, mesh=mesh, in_specs=in_specs, out_specs=out_specs, check_vma=False
    )
```

```python
import math

import jax
import jax.numpy as jnp
from jax import lax
from jax.experimental import pallas as pl
from jax.experimental.pallas import tpu as pltpu
from jax.sharding import PartitionSpec as P

EPSILON = 1e-06
MIB = 1024 * 1024
F32 = jnp.float32
BF16 = jnp.bfloat16
CHUNK = 64
VMEM = pl.BlockSpec(memory_space=pltpu.VMEM)
SMEM = pl.BlockSpec(memory_space=pltpu.SMEM)
HBM = pl.BlockSpec(memory_space=pltpu.HBM)


def start_copies(pairs, sems):
    copies = [pltpu.make_async_copy(src, dst, sems.at[i]) for i, (src, dst) in enumerate(pairs)]
    for copy in copies:
        copy.start()
    return copies


def sigmoid(values):
    return 0.5 * jnp.tanh(0.5 * values) + 0.5


def silu_slope(values):
    gate = sigmoid(values)
    return gate * (1.0 + values * (1.0 - gate))


def rms_scale(values):
    return lax.rsqrt(jnp.mean(values * values, axis=-1, keepdims=True) + EPSILON)


def modulation(timestep, time_weight):
    half_width = time_weight.shape[0] // 2
    frequency = jnp.exp(-math.log(10000.0) * jnp.arange(half_width, dtype=F32) / half_width)
    angles = timestep.astype(F32)[0] * frequency
    embedded = jnp.concatenate([jnp.sin(angles), jnp.cos(angles)]).astype(BF16)
    return jnp.dot(embedded[None, :], time_weight, preferred_element_type=F32)


def shift_pairs(size):
    up = [(i, i + 1) for i in range(size - 1)]
    return up, [(j, i) for i, j in up]


def parent_rows_kernel(parent, out, rows):
    lane = lax.broadcasted_iota(jnp.int32, (1, 128), 1)
    for brick in range(rows.shape[0]):
        local = parent[brick] & 8191
        rows[brick : brick + 1, :] = jnp.where(lane < 64, local >> 7, local & 127).astype(F32)
    values = rows[...].astype(BF16)
    for target in range(out.shape[0]):
        out[target] = values


def parent_rows(parent, targets):
    bricks = parent.shape[0]
    return pl.pallas_call(
        parent_rows_kernel,
        out_shape=jax.ShapeDtypeStruct((targets, bricks, 128), BF16),
        in_specs=[SMEM],
        out_specs=VMEM,
        scratch_shapes=[pltpu.VMEM((bricks, 128), F32)],
        compiler_params=pltpu.CompilerParams(vmem_limit_bytes=4 * MIB),
        cost_estimate=pl.CostEstimate(flops=0, bytes_accessed=65536, transcendentals=0),
        name="parent_rows",
    )(parent)


def near_slots(spots, first_row, valid=True):
    bricks = spots.shape[0]
    spots_t = spots.astype(F32).T
    row_t = spots_t[0:1, :].astype(jnp.int32) - first_row
    near_t = (row_t >= -1) & (row_t <= 4) & valid
    brick_i = lax.broadcasted_iota(jnp.int32, (bricks, bricks), 0)
    brick_j = lax.broadcasted_iota(jnp.int32, (bricks, bricks), 1)
    place_t = jnp.dot(
        jnp.broadcast_to(jnp.where(near_t, 1.0, 0.0), (16, bricks)).astype(BF16),
        jnp.where(brick_i < brick_j, 1.0, 0.0).astype(BF16),
        preferred_element_type=F32,
    )[0:1].astype(jnp.int32)
    count = jnp.sum(jnp.where(near_t, 1.0, 0.0)).astype(jnp.int32)
    return jnp.where(near_t, place_t, -1), count


def tap_cells(pick, spots, first_row, cells):
    found = jnp.dot(pick, spots, preferred_element_type=F32)
    row = found[:, 0:1].astype(jnp.int32) - first_row
    column = found[:, 64:65].astype(jnp.int32)
    lane = lax.broadcasted_iota(jnp.int32, (pick.shape[0], cells), 1)
    onehots = []
    for row_step in (-1, 0, 1):
        for column_step in (-1, 0, 1):
            y, x = row + row_step, column + column_step
            inside = (y >= 0) & (y < 4) & (x >= 0) & (x < 128)
            cell = jnp.where(inside, y * 128 + x, -1)
            onehots.append(jnp.where(lane == cell, 1.0, 0.0).astype(BF16))
    return onehots


def weight_loads(conv_weight, weights, sems, order):
    copies = {}
    for layer in order:
        for part in (3 * layer, 3 * layer + 1, 3 * layer + 2):
            copies[part] = pltpu.make_async_copy(
                conv_weight.at[pl.ds(3 * part, 3)], weights.at[pl.ds(3 * part, 3)], sems.at[part]
            )
            copies[part].start()
    return copies


def hide(values, mod):
    values = values.astype(F32)
    pre = values * rms_scale(values) * (1.0 + mod[0:1, 256:768]) + mod[0:1, 768:1280]
    return pre * sigmoid(pre)


def parent_conv_kernel(
    place, own, below, above, mod, info, weights, up_weight, out, hidden
):
    cells, width = own.shape
    bricks = info.shape[0]
    first_row = place[0]
    spots = info[...]
    slots, near_count = near_slots(spots, first_row)
    hidden[1] = hide(own[...], mod).astype(BF16)
    for layer, source in ((0, below), (2, above)):
        hidden[layer] = jnp.where(place[1 + layer // 2] > 0, hide(source[...], mod), 0.0).astype(BF16)

    def one_chunk(chunk):
        slot = lax.broadcasted_iota(jnp.int32, (CHUNK, bricks), 0) + chunk * CHUNK
        pick = jnp.where(slot == slots, 1.0, 0.0).astype(BF16)
        onehots = tap_cells(pick, spots, first_row, cells)
        onehot = jnp.concatenate(onehots, axis=0)
        total = jnp.dot(onehots[4], own[...], preferred_element_type=F32)
        for layer in (1, 0, 2):
            gathered = jnp.dot(onehot, hidden[layer], preferred_element_type=F32).astype(BF16)
            for corner in range(9):
                total += jnp.dot(
                    gathered[corner * CHUNK : (corner + 1) * CHUNK],
                    weights[9 * layer + corner],
                    preferred_element_type=F32,
                )
        lifted = jnp.dot(total.astype(BF16), up_weight[...], preferred_element_type=F32)
        high = lifted.astype(BF16)
        low = (lifted - high.astype(F32)).astype(BF16)
        across = (((0,), (0,)), ((), ()))
        return lax.dot_general(pick, high, across, preferred_element_type=F32) + lax.dot_general(
            pick, low, across, preferred_element_type=F32
        )

    out[...] = one_chunk(0)

    @pl.loop(1, (near_count + CHUNK - 1) // CHUNK)
    def _(chunk):
        out[...] += one_chunk(chunk)


def parent_conv(place, own, below, above, mod, info, conv_weight, up_weight):
    return pl.pallas_call(
        parent_conv_kernel,
        out_shape=jax.ShapeDtypeStruct((info.shape[0], up_weight.shape[1]), F32),
        in_specs=[SMEM] + [VMEM] * 7,
        out_specs=VMEM,
        scratch_shapes=[
            pltpu.VMEM((3,) + own.shape, BF16),
        ],
        compiler_params=pltpu.CompilerParams(vmem_limit_bytes=20 * MIB),
        cost_estimate=pl.CostEstimate(flops=2 * 128 * 27 * 512 * 512, bytes_accessed=16 * MIB, transcendentals=0),
        name="parent_conv",
    )(place, own, below, above, mod, info, conv_weight, up_weight)


def fine_kernel(
    features, cotangent, occupied, parts, spots, mod, inner_weight, outer_weight,
    grads, pack, spread, sums, inner_pair, outer_pair,
):
    step = pl.program_id(0)
    bricks = occupied.shape[0]

    @pl.when(step == 0)
    def _():
        spread[...] = occupied[...].astype(F32).T.astype(BF16)
        for pair, weight in ((inner_pair, inner_weight), (outer_pair, outer_weight)):
            pair[...] = jnp.zeros((256, 256), BF16)
            pair[0:128, 0:128] = weight[...]
            pair[128:256, 128:256] = weight[...]

    def beside(left, right):
        return jnp.concatenate([left, right], axis=1)

    def mean(values):
        rows = values.shape[0]
        return beside(
            jnp.broadcast_to(jnp.mean(values[:, 0:128], -1, keepdims=True), (rows, 128)),
            jnp.broadcast_to(jnp.mean(values[:, 128:256], -1, keepdims=True), (rows, 128)),
        )

    scale = 1.0 + beside(mod[0:1, 0:128], mod[0:1, 0:128])
    shift = beside(mod[0:1, 128:256], mod[0:1, 128:256])
    transposed = (((1,), (1,)), ((), ()))
    side = lax.broadcasted_iota(jnp.int32, (bricks, 256), 1) // 128
    for item in range(0, features.shape[0], 2):
        brick = step * features.shape[0] + item
        pick = jnp.where(lax.broadcasted_iota(jnp.int32, (bricks, 256), 0) == brick + side, 1.0, 0.0).astype(BF16)
        mask = jnp.dot(spread[...], pick, preferred_element_type=F32)
        lifted = beside(
            jnp.sum(parts[:, pl.ds(brick, 1), :], axis=0), jnp.sum(parts[:, pl.ds(brick + 1, 1), :], axis=0)
        ).astype(BF16).astype(F32)
        fine_in = beside(features[item], features[item + 1]).astype(F32) + lifted
        fine_scale = lax.rsqrt(mean(fine_in * fine_in) + EPSILON)
        normed = fine_in * fine_scale
        pre = normed * scale + shift
        gate = sigmoid(pre)
        act = pre * gate
        slope = gate + act * (1.0 - gate)
        inner_pre = jnp.dot(act.astype(BF16), inner_pair[...], preferred_element_type=F32)
        masked = beside(cotangent[item], cotangent[item + 1]).astype(F32) * mask
        grad_hidden = lax.dot_general(masked.astype(BF16), outer_pair[...], transposed, preferred_element_type=F32)
        grad_inner = (grad_hidden * silu_slope(inner_pre)).astype(BF16)
        grad_act = lax.dot_general(grad_inner, inner_pair[...], transposed, preferred_element_type=F32)
        grad_norm = grad_act * slope * scale
        grad_in = masked + fine_scale * (grad_norm - normed * mean(grad_norm * normed))
        rounded = grad_in.astype(BF16)
        grads[item] = rounded[:, 0:128]
        grads[item + 1] = rounded[:, 128:256]
        total = jnp.sum(grad_in, axis=0, keepdims=True)
        sums[pl.ds(brick, 1), :] = total[:, 0:128]
        sums[pl.ds(brick + 1, 1), :] = total[:, 128:256]

    @pl.when(step == pl.num_programs(0) - 1)
    def _():
        total = sums[...].astype(BF16)
        for target in range(pack.shape[0]):
            pack[target, 0:bricks] = total
            pack[target, bricks : 2 * bricks] = spots[0]


def fine_block(features, cotangent, occupied, parts, spots, mod, inner_weight, outer_weight):
    bricks, voxels, width = features.shape
    per_step = 4
    block = pl.BlockSpec((per_step, voxels, width), lambda i: (i, 0, 0))

    def whole(shape):
        return pl.BlockSpec(shape, lambda i: (0,) * len(shape))

    pack_shape = (parts.shape[0], 2 * bricks, width)
    others = (mod, inner_weight, outer_weight)
    return pl.pallas_call(
        fine_kernel,
        grid=(bricks // per_step,),
        out_shape=(
            jax.ShapeDtypeStruct(features.shape, BF16),
            jax.ShapeDtypeStruct(pack_shape, BF16),
        ),
        in_specs=[block, block, whole(occupied.shape), whole(parts.shape), whole((1, bricks, width))]
        + [whole(array.shape) for array in others],
        out_specs=(block, whole(pack_shape)),
        scratch_shapes=[
            pltpu.VMEM((voxels, bricks), BF16),
            pltpu.VMEM((bricks, width), F32),
            pltpu.VMEM((256, 256), BF16),
            pltpu.VMEM((256, 256), BF16),
        ],
        compiler_params=pltpu.CompilerParams(vmem_limit_bytes=56 * MIB),
        cost_estimate=pl.CostEstimate(flops=3 * 10**10, bytes_accessed=6 * MIB, transcendentals=2**21),
        name="fine_block",
    )(features, cotangent, occupied, parts, spots, *others)


def edge_rows_kernel(own, first, last, sems):
    cells = own.shape[0]
    for copy in start_copies([(own.at[pl.ds(0, 128)], first), (own.at[pl.ds(cells - 128, 128)], last)], sems):
        copy.wait()


def edge_rows(own):
    shape = jax.ShapeDtypeStruct((128, own.shape[1]), BF16)
    return pl.pallas_call(
        edge_rows_kernel,
        out_shape=(shape, shape),
        in_specs=[pl.BlockSpec(memory_space=pl.ANY)],
        out_specs=(VMEM, VMEM),
        scratch_shapes=[pltpu.SemaphoreType.DMA((2,))],
        compiler_params=pltpu.CompilerParams(vmem_limit_bytes=36 * MIB),
        cost_estimate=pl.CostEstimate(flops=10**10, bytes_accessed=MIB, transcendentals=0),
        name="edge_rows",
    )(own)


def six_rows_kernel(before, own, after, out, sems):
    pairs = [
        (own, out.at[pl.ds(128, 512)]),
        (before, out.at[pl.ds(0, 128)]),
        (after, out.at[pl.ds(640, 128)]),
    ]
    for copy in start_copies(pairs, sems):
        copy.wait()


def six_rows(before, own, after):
    return pl.pallas_call(
        six_rows_kernel,
        out_shape=jax.ShapeDtypeStruct((6 * 128, own.shape[1]), BF16),
        in_specs=[pl.BlockSpec(memory_space=pl.ANY)] * 3,
        out_specs=VMEM,
        scratch_shapes=[pltpu.SemaphoreType.DMA((3,))],
        compiler_params=pltpu.CompilerParams(vmem_limit_bytes=4 * MIB),
        cost_estimate=pl.CostEstimate(flops=0, bytes_accessed=2 * MIB, transcendentals=0),
        name="six_rows",
    )(before, own, after)


def cell_lift(pack, up_weight, first_row):
    spots_t = pack[:, 16:32, :].reshape(256, 128).astype(F32).T
    row = spots_t[0:1, :].astype(jnp.int32) - first_row + 1
    column = spots_t[64:65, :].astype(jnp.int32)
    onehot = jnp.where(
        lax.broadcasted_iota(jnp.int32, (6 * 128, 256), 0) == row * 128 + column, 1.0, 0.0
    ).astype(BF16)
    cell_sums = jnp.dot(onehot, pack[:, 0:16, :].reshape(256, 128), preferred_element_type=F32).astype(BF16)
    return lax.dot_general(cell_sums, up_weight, (((1,), (1,)), ((), ())), preferred_element_type=F32)


def own_lift_kernel(place, packs, up_hbm, lift, up_weight, sems):
    (copy,) = start_copies([(up_hbm, up_weight)], sems)
    copy.wait()
    lift[...] = cell_lift(packs, up_weight[...], place[0])


def own_lift(place, packs, up_weight):
    width = up_weight.shape[0]
    return pl.pallas_call(
        own_lift_kernel,
        out_shape=jax.ShapeDtypeStruct((6 * 128, width), F32),
        in_specs=[SMEM, VMEM, pl.BlockSpec(memory_space=pl.ANY)],
        out_specs=VMEM,
        scratch_shapes=[pltpu.VMEM(up_weight.shape, BF16), pltpu.SemaphoreType.DMA((1,))],
        compiler_params=pltpu.CompilerParams(vmem_limit_bytes=40 * MIB),
        cost_estimate=pl.CostEstimate(flops=3*10**10, bytes_accessed=2 * MIB, transcendentals=0),
        name="own_lift",
    )(place, packs, up_weight)


def coarse_grad_kernel(
    place, features, own, below, above, mod, lift, packs_below, packs_above, conv_weight, up_weight,
    out, grad, center, total, weights, sems,
):
    cells, width = features.shape
    loads = weight_loads(conv_weight, weights, sems, (1, 2, 0))
    for layer, source in ((1, own), (0, below), (2, above)):
        if layer == 1:
            whole = lift[...] + source[...].astype(F32)
            center[...] = whole[128:640]
        else:
            pack = packs_below if layer == 0 else packs_above
            whole = cell_lift(pack, up_weight[...], place[0]) + source[...].astype(F32)
        grad[layer] = whole.astype(BF16)
    for layer in (1, 0, 2):
        for row_step in range(3):
            loads[3 * (2 - layer) + row_step].wait()
        rows = jnp.concatenate(
            [grad[layer, (2 - row_step) * 128 : (2 - row_step) * 128 + cells] for row_step in range(3)], axis=1
        )
        for column_step in range(3):
            taps = jnp.concatenate(
                [weights[9 * (2 - layer) + 3 * row_step + column_step] for row_step in range(3)], axis=1
            )
            piece = lax.dot_general(rows, taps, (((1,), (1,)), ((), ())), preferred_element_type=F32)
            if layer == 1:
                total[column_step] = piece
            else:
                total[column_step] += piece
    column = lax.broadcasted_iota(jnp.int32, (cells, 1), 0) % 128
    left = jnp.where(column == 127, 0.0, pltpu.roll(total[0], cells - 1, 0))
    right = jnp.where(column == 0, 0.0, pltpu.roll(total[2], 1, 0))
    grad_conv = total[1] + left + right
    scale = 1.0 + mod[0:1, 256:768]
    shift = mod[0:1, 768:1280]
    values = features[...].astype(F32)
    coarse_scale = rms_scale(values)
    normed = values * coarse_scale
    grad_cn = grad_conv * silu_slope(normed * scale + shift) * scale
    inner = jnp.mean(grad_cn * normed, axis=-1, keepdims=True)
    out[...] = (center[...] + coarse_scale * (grad_cn - normed * inner)).astype(BF16)


def coarse_grad(
    place, features, own, below, above, mod, lift, packs_below, packs_above, conv_weight, up_weight
):
    cells, width = features.shape
    return pl.pallas_call(
        coarse_grad_kernel,
        out_shape=jax.ShapeDtypeStruct((cells, width), BF16),
        in_specs=[SMEM] + [VMEM] * 8 + [pl.BlockSpec(memory_space=pl.ANY), VMEM],
        out_specs=VMEM,
        scratch_shapes=[
            pltpu.VMEM((3, 6 * 128, width), BF16),
            pltpu.VMEM((cells, width), F32),
            pltpu.VMEM((3, cells, width), F32),
            pltpu.VMEM(conv_weight.shape, BF16),
            pltpu.SemaphoreType.DMA((9,)),
        ],
        compiler_params=pltpu.CompilerParams(vmem_limit_bytes=48 * MIB),
        cost_estimate=pl.CostEstimate(flops=2 * 512 * 27 * 512 * 512, bytes_accessed=18 * MIB, transcendentals=0),
        name="coarse_grad",
    )(place, features, own, below, above, mod, lift, packs_below, packs_above, conv_weight, up_weight)


def per_device(
    fine_features,
    occupancy,
    parent,
    timestep,
    coarse_features,
    time_weight,
    conv_weight,
    up_weight,
    inner_weight,
    outer_weight,
    coarse_cotangent,
    fine_cotangent,
):
    layer_count, row_count, column_count, width = coarse_features.shape
    fine_width = up_weight.shape[1]
    bricks = parent.shape[0]
    fine_size, coarse_size = lax.axis_size("fine"), lax.axis_size("coarse")
    coarse_index, fine_index = lax.axis_index("coarse"), lax.axis_index("fine")
    cells = layer_count * row_count * column_count
    up, down = shift_pairs(coarse_size)
    row_up, row_down = shift_pairs(fine_size)

    spots_out = parent_rows(parent, fine_size)
    place = jnp.stack(
        [fine_index * row_count, (coarse_index > 0).astype(jnp.int32), (coarse_index < coarse_size - 1).astype(jnp.int32)]
    ).astype(jnp.int32)

    features = coarse_features.reshape(cells, width)
    cotangent = coarse_cotangent.reshape(cells, width)
    all_spots = lax.all_to_all(spots_out, "fine", 0, 0, tiled=True).reshape(fine_size * bricks, 128)
    sent_features, _ = lax.optimization_barrier((features, spots_out))
    features_below = lax.ppermute(sent_features, "coarse", up)
    features_above = lax.ppermute(sent_features, "coarse", down)
    edge_cotangent, _ = lax.optimization_barrier((cotangent, all_spots))
    first_rows, last_rows = edge_rows(edge_cotangent)
    row_before = lax.ppermute(last_rows, "fine", row_up)
    row_after = lax.ppermute(first_rows, "fine", row_down)
    mod = modulation(timestep, time_weight)

    partial_rows = parent_conv(
        place, features, features_below, features_above, mod, all_spots, conv_weight, up_weight
    )
    parts = lax.all_to_all(
        partial_rows.reshape(fine_size, bricks, fine_width), "fine", 0, 0, tiled=True
    )
    after_conv, _ = lax.optimization_barrier((cotangent, partial_rows))
    cot_own = six_rows(row_before, after_conv, row_after)
    cot_below = lax.ppermute(cot_own, "coarse", up)

    parts, _ = lax.optimization_barrier((parts, cot_own))
    grad_fine, pack = fine_block(
        fine_features, fine_cotangent, occupancy, parts, spots_out, mod, inner_weight, outer_weight
    )
    packs = lax.all_to_all(pack, "fine", 0, 0, tiled=True)
    late_own, _ = lax.optimization_barrier((cot_own, pack))
    cot_above = lax.ppermute(late_own, "coarse", down)
    packs_below = lax.ppermute(packs, "coarse", up)
    packs_above = lax.ppermute(packs, "coarse", down)
    late_place, _ = lax.optimization_barrier((place, cot_below))
    lift = own_lift(late_place, packs, up_weight)
    grad_coarse = coarse_grad(
        place, features, cot_own, cot_below, cot_above, mod,
        lift, packs_below, packs_above, conv_weight, up_weight
    )
    return (grad_coarse.reshape(coarse_features.shape), grad_fine)


def solution(mesh):
    in_specs = (
        P(("coarse", "fine"), None, None),
        P(("coarse", "fine"), None),
        P(("coarse", "fine")),
        P(),
        P("coarse", "fine", None, None),
        P(),
        P(),
        P(),
        P(),
        P(),
        P("coarse", "fine", None, None),
        P(("coarse", "fine"), None, None),
    )
    out_specs = (P("coarse", "fine", None, None), P(("coarse", "fine"), None, None))
    return jax.shard_map(
        per_device, mesh=mesh, in_specs=in_specs, out_specs=out_specs, check_vma=False
    )
```

```python
import math

import jax
import jax.numpy as jnp
from jax import lax
from jax.experimental import pallas as pl
from jax.experimental.pallas import tpu as pltpu
from jax.sharding import PartitionSpec as P

EPSILON = 1e-06
MIB = 1024 * 1024
F32 = jnp.float32
BF16 = jnp.bfloat16
CHUNK = 64
VMEM = pl.BlockSpec(memory_space=pltpu.VMEM)
SMEM = pl.BlockSpec(memory_space=pltpu.SMEM)
HBM = pl.BlockSpec(memory_space=pltpu.HBM)


def start_copies(pairs, sems):
    copies = [pltpu.make_async_copy(src, dst, sems.at[i]) for i, (src, dst) in enumerate(pairs)]
    for copy in copies:
        copy.start()
    return copies


def sigmoid(values):
    return 0.5 * jnp.tanh(0.5 * values) + 0.5


def silu_slope(values):
    gate = sigmoid(values)
    return gate * (1.0 + values * (1.0 - gate))


def rms_scale(values):
    return lax.rsqrt(jnp.mean(values * values, axis=-1, keepdims=True) + EPSILON)


def modulation(timestep, time_weight):
    half_width = time_weight.shape[0] // 2
    frequency = jnp.exp(-math.log(10000.0) * jnp.arange(half_width, dtype=F32) / half_width)
    angles = timestep.astype(F32)[0] * frequency
    embedded = jnp.concatenate([jnp.sin(angles), jnp.cos(angles)]).astype(BF16)
    return jnp.dot(embedded[None, :], time_weight, preferred_element_type=F32)


def shift_pairs(size):
    up = [(i, i + 1) for i in range(size - 1)]
    return up, [(j, i) for i, j in up]


def parent_rows_kernel(parent, out, rows):
    lane = lax.broadcasted_iota(jnp.int32, (1, 128), 1)
    for brick in range(rows.shape[0]):
        local = parent[brick] & 8191
        rows[brick : brick + 1, :] = jnp.where(lane < 64, local >> 7, local & 127).astype(F32)
    values = rows[...].astype(BF16)
    for target in range(out.shape[0]):
        out[target] = values


def parent_rows(parent, targets):
    bricks = parent.shape[0]
    return pl.pallas_call(
        parent_rows_kernel,
        out_shape=jax.ShapeDtypeStruct((targets, bricks, 128), BF16),
        in_specs=[SMEM],
        out_specs=VMEM,
        scratch_shapes=[pltpu.VMEM((bricks, 128), F32)],
        compiler_params=pltpu.CompilerParams(vmem_limit_bytes=4 * MIB),
        cost_estimate=pl.CostEstimate(flops=0, bytes_accessed=65536, transcendentals=0),
        name="parent_rows",
    )(parent)


def near_slots(spots, first_row, valid=True):
    bricks = spots.shape[0]
    spots_t = spots.astype(F32).T
    row_t = spots_t[0:1, :].astype(jnp.int32) - first_row
    near_t = (row_t >= -1) & (row_t <= 4) & valid
    brick_i = lax.broadcasted_iota(jnp.int32, (bricks, bricks), 0)
    brick_j = lax.broadcasted_iota(jnp.int32, (bricks, bricks), 1)
    place_t = jnp.dot(
        jnp.broadcast_to(jnp.where(near_t, 1.0, 0.0), (16, bricks)).astype(BF16),
        jnp.where(brick_i < brick_j, 1.0, 0.0).astype(BF16),
        preferred_element_type=F32,
    )[0:1].astype(jnp.int32)
    count = jnp.sum(jnp.where(near_t, 1.0, 0.0)).astype(jnp.int32)
    return jnp.where(near_t, place_t, -1), count


def tap_cells(pick, spots, first_row, cells):
    found = jnp.dot(pick, spots, preferred_element_type=F32)
    row = found[:, 0:1].astype(jnp.int32) - first_row
    column = found[:, 64:65].astype(jnp.int32)
    lane = lax.broadcasted_iota(jnp.int32, (pick.shape[0], cells), 1)
    onehots = []
    for row_step in (-1, 0, 1):
        for column_step in (-1, 0, 1):
            y, x = row + row_step, column + column_step
            inside = (y >= 0) & (y < 4) & (x >= 0) & (x < 128)
            cell = jnp.where(inside, y * 128 + x, -1)
            onehots.append(jnp.where(lane == cell, 1.0, 0.0).astype(BF16))
    return onehots


def weight_loads(conv_weight, weights, sems, order):
    copies = {}
    for layer in order:
        for part in (3 * layer, 3 * layer + 1, 3 * layer + 2):
            copies[part] = pltpu.make_async_copy(
                conv_weight.at[pl.ds(3 * part, 3)], weights.at[pl.ds(3 * part, 3)], sems.at[part]
            )
            copies[part].start()
    return copies


def hide(values, mod):
    values = values.astype(F32)
    pre = values * rms_scale(values) * (1.0 + mod[0:1, 256:768]) + mod[0:1, 768:1280]
    return pre * sigmoid(pre)


def parent_conv_kernel(
    place, own, below, above, mod, info, weights, up_weight, out, hidden
):
    cells, width = own.shape
    bricks = info.shape[0]
    first_row = place[0]
    spots = info[...]
    slots, near_count = near_slots(spots, first_row)
    hidden[1] = hide(own[...], mod).astype(BF16)
    for layer, source in ((0, below), (2, above)):
        hidden[layer] = jnp.where(place[1 + layer // 2] > 0, hide(source[...], mod), 0.0).astype(BF16)

    def one_chunk(chunk):
        slot = lax.broadcasted_iota(jnp.int32, (CHUNK, bricks), 0) + chunk * CHUNK
        pick = jnp.where(slot == slots, 1.0, 0.0).astype(BF16)
        onehots = tap_cells(pick, spots, first_row, cells)
        onehot = jnp.concatenate(onehots, axis=0)
        total = jnp.dot(onehots[4], own[...], preferred_element_type=F32)
        for layer in (1, 0, 2):
            gathered = jnp.dot(onehot, hidden[layer], preferred_element_type=F32).astype(BF16)
            for corner in range(9):
                total += jnp.dot(
                    gathered[corner * CHUNK : (corner + 1) * CHUNK],
                    weights[9 * layer + corner],
                    preferred_element_type=F32,
                )
        lifted = jnp.dot(total.astype(BF16), up_weight[...], preferred_element_type=F32)
        high = lifted.astype(BF16)
        low = (lifted - high.astype(F32)).astype(BF16)
        across = (((0,), (0,)), ((), ()))
        return lax.dot_general(pick, high, across, preferred_element_type=F32) + lax.dot_general(
            pick, low, across, preferred_element_type=F32
        )

    out[...] = one_chunk(0)

    @pl.loop(1, (near_count + CHUNK - 1) // CHUNK)
    def _(chunk):
        out[...] += one_chunk(chunk)


def parent_conv(place, own, below, above, mod, info, conv_weight, up_weight):
    return pl.pallas_call(
        parent_conv_kernel,
        out_shape=jax.ShapeDtypeStruct((info.shape[0], up_weight.shape[1]), F32),
        in_specs=[SMEM] + [VMEM] * 7,
        out_specs=VMEM,
        scratch_shapes=[
            pltpu.VMEM((3,) + own.shape, BF16),
        ],
        compiler_params=pltpu.CompilerParams(vmem_limit_bytes=20 * MIB),
        cost_estimate=pl.CostEstimate(flops=2 * 128 * 27 * 512 * 512, bytes_accessed=16 * MIB, transcendentals=0),
        name="parent_conv",
    )(place, own, below, above, mod, info, conv_weight, up_weight)


def fine_kernel(
    features, cotangent, occupied, parts, spots, mod, inner_weight, outer_weight,
    grads, pack, spread, sums, inner_pair, outer_pair,
):
    step = pl.program_id(0)
    bricks = occupied.shape[0]

    @pl.when(step == 0)
    def _():
        spread[...] = occupied[...].astype(F32).T.astype(BF16)
        for pair, weight in ((inner_pair, inner_weight), (outer_pair, outer_weight)):
            pair[...] = jnp.zeros((256, 256), BF16)
            pair[0:128, 0:128] = weight[...]
            pair[128:256, 128:256] = weight[...]

    def beside(left, right):
        return jnp.concatenate([left, right], axis=1)

    def mean(values):
        rows = values.shape[0]
        return beside(
            jnp.broadcast_to(jnp.mean(values[:, 0:128], -1, keepdims=True), (rows, 128)),
            jnp.broadcast_to(jnp.mean(values[:, 128:256], -1, keepdims=True), (rows, 128)),
        )

    scale = 1.0 + beside(mod[0:1, 0:128], mod[0:1, 0:128])
    shift = beside(mod[0:1, 128:256], mod[0:1, 128:256])
    transposed = (((1,), (1,)), ((), ()))
    side = lax.broadcasted_iota(jnp.int32, (bricks, 256), 1) // 128
    for item in range(0, features.shape[0], 2):
        brick = step * features.shape[0] + item
        pick = jnp.where(lax.broadcasted_iota(jnp.int32, (bricks, 256), 0) == brick + side, 1.0, 0.0).astype(BF16)
        mask = jnp.dot(spread[...], pick, preferred_element_type=F32)
        lifted = beside(
            jnp.sum(parts[:, pl.ds(brick, 1), :], axis=0), jnp.sum(parts[:, pl.ds(brick + 1, 1), :], axis=0)
        ).astype(BF16).astype(F32)
        fine_in = beside(features[item], features[item + 1]).astype(F32) + lifted
        fine_scale = lax.rsqrt(mean(fine_in * fine_in) + EPSILON)
        normed = fine_in * fine_scale
        pre = normed * scale + shift
        gate = sigmoid(pre)
        act = pre * gate
        slope = gate + act * (1.0 - gate)
        inner_pre = jnp.dot(act.astype(BF16), inner_pair[...], preferred_element_type=F32)
        masked = beside(cotangent[item], cotangent[item + 1]).astype(F32) * mask
        grad_hidden = lax.dot_general(masked.astype(BF16), outer_pair[...], transposed, preferred_element_type=F32)
        grad_inner = (grad_hidden * silu_slope(inner_pre)).astype(BF16)
        grad_act = lax.dot_general(grad_inner, inner_pair[...], transposed, preferred_element_type=F32)
        grad_norm = grad_act * slope * scale
        grad_in = masked + fine_scale * (grad_norm - normed * mean(grad_norm * normed))
        rounded = grad_in.astype(BF16)
        grads[item] = rounded[:, 0:128]
        grads[item + 1] = rounded[:, 128:256]
        total = jnp.sum(grad_in, axis=0, keepdims=True)
        sums[pl.ds(brick, 1), :] = total[:, 0:128]
        sums[pl.ds(brick + 1, 1), :] = total[:, 128:256]

    @pl.when(step == pl.num_programs(0) - 1)
    def _():
        total = sums[...].astype(BF16)
        for target in range(pack.shape[0]):
            pack[target, 0:bricks] = total
            pack[target, bricks : 2 * bricks] = spots[0]


def fine_block(features, cotangent, occupied, parts, spots, mod, inner_weight, outer_weight):
    bricks, voxels, width = features.shape
    per_step = 4
    block = pl.BlockSpec((per_step, voxels, width), lambda i: (i, 0, 0))

    def whole(shape):
        return pl.BlockSpec(shape, lambda i: (0,) * len(shape))

    pack_shape = (parts.shape[0], 2 * bricks, width)
    others = (mod, inner_weight, outer_weight)
    return pl.pallas_call(
        fine_kernel,
        grid=(bricks // per_step,),
        out_shape=(
            jax.ShapeDtypeStruct(features.shape, BF16),
            jax.ShapeDtypeStruct(pack_shape, BF16),
        ),
        in_specs=[block, block, whole(occupied.shape), whole(parts.shape), whole((1, bricks, width))]
        + [whole(array.shape) for array in others],
        out_specs=(block, whole(pack_shape)),
        scratch_shapes=[
            pltpu.VMEM((voxels, bricks), BF16),
            pltpu.VMEM((bricks, width), F32),
            pltpu.VMEM((256, 256), BF16),
            pltpu.VMEM((256, 256), BF16),
        ],
        compiler_params=pltpu.CompilerParams(vmem_limit_bytes=56 * MIB),
        cost_estimate=pl.CostEstimate(flops=3 * 10**10, bytes_accessed=6 * MIB, transcendentals=2**21),
        name="fine_block",
    )(features, cotangent, occupied, parts, spots, *others)


def edge_rows_kernel(own, first, last, sems):
    cells = own.shape[0]
    for copy in start_copies([(own.at[pl.ds(0, 128)], first), (own.at[pl.ds(cells - 128, 128)], last)], sems):
        copy.wait()


def edge_rows(own):
    shape = jax.ShapeDtypeStruct((128, own.shape[1]), BF16)
    return pl.pallas_call(
        edge_rows_kernel,
        out_shape=(shape, shape),
        in_specs=[pl.BlockSpec(memory_space=pl.ANY)],
        out_specs=(VMEM, VMEM),
        scratch_shapes=[pltpu.SemaphoreType.DMA((2,))],
        compiler_params=pltpu.CompilerParams(vmem_limit_bytes=36 * MIB),
        cost_estimate=pl.CostEstimate(flops=10**10, bytes_accessed=MIB, transcendentals=0),
        name="edge_rows",
    )(own)


def six_rows_kernel(before, own, after, out, sems):
    pairs = [
        (own, out.at[pl.ds(128, 512)]),
        (before, out.at[pl.ds(0, 128)]),
        (after, out.at[pl.ds(640, 128)]),
    ]
    for copy in start_copies(pairs, sems):
        copy.wait()


def six_rows(before, own, after):
    return pl.pallas_call(
        six_rows_kernel,
        out_shape=jax.ShapeDtypeStruct((6 * 128, own.shape[1]), BF16),
        in_specs=[pl.BlockSpec(memory_space=pl.ANY)] * 3,
        out_specs=VMEM,
        scratch_shapes=[pltpu.SemaphoreType.DMA((3,))],
        compiler_params=pltpu.CompilerParams(vmem_limit_bytes=4 * MIB),
        cost_estimate=pl.CostEstimate(flops=0, bytes_accessed=2 * MIB, transcendentals=0),
        name="six_rows",
    )(before, own, after)


def cell_lift(pack, up_weight, first_row):
    spots_t = pack[:, 16:32, :].reshape(256, 128).astype(F32).T
    row = spots_t[0:1, :].astype(jnp.int32) - first_row + 1
    column = spots_t[64:65, :].astype(jnp.int32)
    onehot = jnp.where(
        lax.broadcasted_iota(jnp.int32, (6 * 128, 256), 0) == row * 128 + column, 1.0, 0.0
    ).astype(BF16)
    cell_sums = jnp.dot(onehot, pack[:, 0:16, :].reshape(256, 128), preferred_element_type=F32).astype(BF16)
    return lax.dot_general(cell_sums, up_weight, (((1,), (1,)), ((), ())), preferred_element_type=F32)


def own_lift_kernel(place, packs, up_hbm, lift, up_weight, sems):
    (copy,) = start_copies([(up_hbm, up_weight)], sems)
    copy.wait()
    lift[...] = cell_lift(packs, up_weight[...], place[0])


def own_lift(place, packs, up_weight):
    width = up_weight.shape[0]
    return pl.pallas_call(
        own_lift_kernel,
        out_shape=jax.ShapeDtypeStruct((6 * 128, width), F32),
        in_specs=[SMEM, VMEM, pl.BlockSpec(memory_space=pl.ANY)],
        out_specs=VMEM,
        scratch_shapes=[pltpu.VMEM(up_weight.shape, BF16), pltpu.SemaphoreType.DMA((1,))],
        compiler_params=pltpu.CompilerParams(vmem_limit_bytes=40 * MIB),
        cost_estimate=pl.CostEstimate(flops=3*10**10, bytes_accessed=2 * MIB, transcendentals=0),
        name="own_lift",
    )(place, packs, up_weight)


def coarse_grad_kernel(
    place, features, own, below, above, mod, lift, packs_below, packs_above, conv_weight, up_weight,
    out, grad, center, total, weights, sems,
):
    cells, width = features.shape
    loads = weight_loads(conv_weight, weights, sems, (1, 2, 0))
    for layer, source in ((1, own), (0, below), (2, above)):
        if layer == 1:
            whole = lift[...] + source[...].astype(F32)
            center[...] = whole[128:640]
        else:
            pack = packs_below if layer == 0 else packs_above
            whole = cell_lift(pack, up_weight[...], place[0]) + source[...].astype(F32)
        grad[layer] = whole.astype(BF16)
    for layer in (1, 0, 2):
        for row_step in range(3):
            loads[3 * (2 - layer) + row_step].wait()
        rows = jnp.concatenate(
            [grad[layer, (2 - row_step) * 128 : (2 - row_step) * 128 + cells] for row_step in range(3)], axis=1
        )
        for column_step in range(3):
            taps = jnp.concatenate(
                [weights[9 * (2 - layer) + 3 * row_step + column_step] for row_step in range(3)], axis=1
            )
            piece = lax.dot_general(rows, taps, (((1,), (1,)), ((), ())), preferred_element_type=F32)
            if layer == 1:
                total[column_step] = piece
            else:
                total[column_step] += piece
    column = lax.broadcasted_iota(jnp.int32, (cells, 1), 0) % 128
    left = jnp.where(column == 127, 0.0, pltpu.roll(total[0], cells - 1, 0))
    right = jnp.where(column == 0, 0.0, pltpu.roll(total[2], 1, 0))
    grad_conv = total[1] + left + right
    scale = 1.0 + mod[0:1, 256:768]
    shift = mod[0:1, 768:1280]
    values = features[...].astype(F32)
    coarse_scale = rms_scale(values)
    normed = values * coarse_scale
    grad_cn = grad_conv * silu_slope(normed * scale + shift) * scale
    inner = jnp.mean(grad_cn * normed, axis=-1, keepdims=True)
    out[...] = (center[...] + coarse_scale * (grad_cn - normed * inner)).astype(BF16)


def coarse_grad(
    place, features, own, below, above, mod, lift, packs_below, packs_above, conv_weight, up_weight
):
    cells, width = features.shape
    return pl.pallas_call(
        coarse_grad_kernel,
        out_shape=jax.ShapeDtypeStruct((cells, width), BF16),
        in_specs=[SMEM] + [VMEM] * 8 + [pl.BlockSpec(memory_space=pl.ANY), VMEM],
        out_specs=VMEM,
        scratch_shapes=[
            pltpu.VMEM((3, 6 * 128, width), BF16),
            pltpu.VMEM((cells, width), F32),
            pltpu.VMEM((3, cells, width), F32),
            pltpu.VMEM(conv_weight.shape, BF16),
            pltpu.SemaphoreType.DMA((9,)),
        ],
        compiler_params=pltpu.CompilerParams(vmem_limit_bytes=48 * MIB),
        cost_estimate=pl.CostEstimate(flops=2 * 512 * 27 * 512 * 512, bytes_accessed=18 * MIB, transcendentals=0),
        name="coarse_grad",
    )(place, features, own, below, above, mod, lift, packs_below, packs_above, conv_weight, up_weight)


def per_device(
    fine_features,
    occupancy,
    parent,
    timestep,
    coarse_features,
    time_weight,
    conv_weight,
    up_weight,
    inner_weight,
    outer_weight,
    coarse_cotangent,
    fine_cotangent,
):
    layer_count, row_count, column_count, width = coarse_features.shape
    fine_width = up_weight.shape[1]
    bricks = parent.shape[0]
    fine_size, coarse_size = lax.axis_size("fine"), lax.axis_size("coarse")
    coarse_index, fine_index = lax.axis_index("coarse"), lax.axis_index("fine")
    cells = layer_count * row_count * column_count
    up, down = shift_pairs(coarse_size)
    row_up, row_down = shift_pairs(fine_size)

    spots_out = parent_rows(parent, fine_size)
    place = jnp.stack(
        [fine_index * row_count, (coarse_index > 0).astype(jnp.int32), (coarse_index < coarse_size - 1).astype(jnp.int32)]
    ).astype(jnp.int32)

    features = coarse_features.reshape(cells, width)
    cotangent = coarse_cotangent.reshape(cells, width)
    all_spots = lax.all_to_all(spots_out, "fine", 0, 0, tiled=True).reshape(fine_size * bricks, 128)
    sent_features, _ = lax.optimization_barrier((features, spots_out))
    features_below = lax.ppermute(sent_features, "coarse", up)
    features_above = lax.ppermute(sent_features, "coarse", down)
    edge_cotangent, _ = lax.optimization_barrier((cotangent, all_spots))
    first_rows, last_rows = edge_rows(edge_cotangent)
    row_before = lax.ppermute(last_rows, "fine", row_up)
    mod = modulation(timestep, time_weight)

    partial_rows = parent_conv(
        place, features, features_below, features_above, mod, all_spots, conv_weight, up_weight
    )
    parts = lax.all_to_all(
        partial_rows.reshape(fine_size, bricks, fine_width), "fine", 0, 0, tiled=True
    )
    after_conv, late_rows, _ = lax.optimization_barrier((cotangent, first_rows, partial_rows))
    row_after = lax.ppermute(late_rows, "fine", row_down)
    cot_own = six_rows(row_before, after_conv, row_after)
    cot_below = lax.ppermute(cot_own, "coarse", up)

    parts, _ = lax.optimization_barrier((parts, cot_own))
    grad_fine, pack = fine_block(
        fine_features, fine_cotangent, occupancy, parts, spots_out, mod, inner_weight, outer_weight
    )
    packs = lax.all_to_all(pack, "fine", 0, 0, tiled=True)
    late_own, _ = lax.optimization_barrier((cot_own, pack))
    cot_above = lax.ppermute(late_own, "coarse", down)
    packs_below = lax.ppermute(packs, "coarse", up)
    packs_above = lax.ppermute(packs, "coarse", down)
    late_place, _ = lax.optimization_barrier((place, cot_below))
    lift = own_lift(late_place, packs, up_weight)
    grad_coarse = coarse_grad(
        place, features, cot_own, cot_below, cot_above, mod,
        lift, packs_below, packs_above, conv_weight, up_weight
    )
    return (grad_coarse.reshape(coarse_features.shape), grad_fine)


def solution(mesh):
    in_specs = (
        P(("coarse", "fine"), None, None),
        P(("coarse", "fine"), None),
        P(("coarse", "fine")),
        P(),
        P("coarse", "fine", None, None),
        P(),
        P(),
        P(),
        P(),
        P(),
        P("coarse", "fine", None, None),
        P(("coarse", "fine"), None, None),
    )
    out_specs = (P("coarse", "fine", None, None), P(("coarse", "fine"), None, None))
    return jax.shard_map(
        per_device, mesh=mesh, in_specs=in_specs, out_specs=out_specs, check_vma=False
    )
```
